256 devices in a mesh: section: 2 (over y_lo), ctx: 64 (over z, x, y_hi), mp: 2 (over core).
Axes of the slice: x: 4, y: 4 (y_hi: 2, y_lo: 2; y = y_hi * 2 + y_lo), z: 8, core: 2. Of those that a mesh axis runs over, the one named last changes fastest.
Arguments:
- depth_logits: float32 [2, 32768, 41], P('section', ('ctx', 'mp')), may hold values from -20 to 320
- features: bfloat16 [2, 32768, 64], P('section', ('ctx', 'mp')), may hold values from -6 to 6
- cell_index: int32 [2, 32768, 41], P('section', ('ctx', 'mp')), may hold values from 0 to 511
- embed: bfloat16 [32768, 8192], P('ctx', ('section', 'mp')), may hold values from -6 to 6
- w_visual: bfloat16 [64, 8192], P(None, ('section', 'mp')), may hold values from -0.75 to 0.75
- w_gate: bfloat16 [64, 8192], P(None, ('section', 'mp')), may hold values from -0.75 to 0.75
- input_map: bfloat16 [32768, 128], P('ctx'), may hold values from -0.5 to 0.5
- output_map: bfloat16 [32768, 128], P('ctx'), may hold values from -0.5 to 0.5
- forget: float32 [32768, 64], P('ctx', ('section', 'mp')), may hold values from 0 to 1
- skip: float32 [64], P(('section', 'mp')), may hold values from 0.5 to 6
- frame_ids: int32 [32768], P('ctx'), may hold values from 0 to 681, never falling along the last dimension, each value on 1 to 96 neighbouring positions
- norm_gain: float32 [8192], P(('section', 'mp')), may hold values from 0.1 to 1.9
Outputs:
- layer_out: bfloat16 [32768, 8192], P('ctx', ('section', 'mp'))
The draws below stay inside these ranges and needn't reach their ends.
Inputs may be any that keep to these rules, and one draw needn't show every extreme that they name: `frame_ids`: frame numbers never fall along the sequence; a frame holds at most 96 tokens.
All inputs are finite; a program needn't handle non-finite values.
Results may differ from the reference program's by a relative error of at most 0.0033.
The reference program's roundings to bfloat16 on the way (of `stream`, `weights` and `keys_scaled`) count: a program that leaves them out, or rounds other values in their place, can miss the bound.
Values sent between devices are 32-bit elements; how exact they have to be, the bound alone decides.
No kernel may reach another device: no remote copies, remote signals or barrier semaphores. Data moves between devices by JAX's collectives and lax.ppermute only.
A program may use at most 192 MiB of HBM per device.

```python
import math
import jax
import jax.numpy as jnp
import numpy as np
from jax import lax

H = 64
P_SIZE = 128
N = 128
BLK = 256
CF = 64
DB = 41
TOK_DEV = 512
DI = 8192
TOKEN_TOTAL = 32768
PIX_BLOCK = 512
PIX_ALL = 32768
GROUPS = 2
N_CTX = 64


def draw_depth_logits(key, part):
    key = jax.random.fold_in(key, 11)
    random_keys = jax.random.split(key, 1)
    full_shape = (GROUPS, PIX_ALL, DB)
    return jnp.clip(3.0 * jax.random.normal(random_keys[0], full_shape, jnp.float32), -18.0, 18.0)


def draw_forget(key, part):
    key = jax.random.fold_in(key, 23)
    random_keys = jax.random.split(key, 11)
    slow_share = 0.5
    middle_share = 0.25
    shard_count = TOKEN_TOTAL // TOK_DEV
    head_pick = jax.random.uniform(random_keys[0], (1, H))
    is_slow = head_pick < slow_share
    is_middle = (head_pick >= slow_share) & (head_pick < slow_share + middle_share)
    slow_rate = jnp.exp(jax.random.uniform(random_keys[1], (1, H), jnp.float32, jnp.log(0.1), jnp.log(0.25))) / TOKEN_TOTAL
    middle_rate = jnp.exp(jax.random.uniform(random_keys[7], (1, H), jnp.float32, jnp.log(0.035), jnp.log(0.05))) / BLK
    fast_rate = jnp.exp(jax.random.uniform(random_keys[2], (1, H), jnp.float32, jnp.log(1.0 / 50.0), jnp.log(1.0 / 30.0)))
    base_rate = jnp.where(is_slow, slow_rate, jnp.where(is_middle, middle_rate, fast_rate))
    wide_factor = jnp.exp(jax.random.uniform(random_keys[3], (shard_count, 1, H), jnp.float32, jnp.log(0.5), jnp.log(2.0)))
    narrow_factor = jnp.exp(jax.random.uniform(random_keys[8], (shard_count, 1, H), jnp.float32, jnp.log(0.7), jnp.log(1.4)))
    drawn_factor = jnp.exp(jax.random.uniform(random_keys[9], (shard_count, 1, H), jnp.float32, jnp.log(0.004), jnp.log(0.02)))
    is_drawn = jax.random.uniform(random_keys[10], (shard_count, 1, H)) < 0.25
    fast_factor = jnp.where(is_drawn, drawn_factor, wide_factor)
    shard_factor = jnp.where(is_slow[None], wide_factor, jnp.where(is_middle[None], narrow_factor, fast_factor))
    token_factor = jnp.exp(jax.random.uniform(random_keys[4], (TOKEN_TOTAL, H), jnp.float32, jnp.log(0.6), jnp.log(1.7)))
    decay_rates = ((base_rate * token_factor).reshape(shard_count, TOK_DEV, H) * shard_factor).reshape(TOKEN_TOTAL, H)
    spike_start = jax.random.randint(random_keys[5], (3,), 0, TOKEN_TOTAL)
    spike_length = jax.random.uniform(random_keys[6], (3,), jnp.float32, 0.22, 0.5)
    token_position = lax.broadcasted_iota(jnp.int32, (TOKEN_TOTAL, 3), 0)
    spike_run = jnp.sum(jnp.where(token_position == spike_start[None, :], spike_length[None, :], 0.0), axis=1)
    return decay_rates + spike_run[:, None]


def draw_skip(key, part):
    key = jax.random.fold_in(key, 37)
    token_position = lax.broadcasted_iota(jnp.float32, (H,), 0) / (H - 1)
    spread = jax.random.uniform(key, (H,), jnp.float32, 0.8, 1.25)
    rising = 0.8 * jnp.power(3.0, token_position)
    return rising * spread


def plant(result, stream_key, smallest, largest):
    extent = result.shape
    index_at = [jax.random.randint(jax.random.fold_in(stream_key, axis), (), 0, extent[axis]) for axis in range(len(extent))]
    result = result.at[tuple(index_at)].set(smallest)
    longest = extent.index(max(extent))
    index_at[longest] = (index_at[longest] + 1) % extent[longest]
    return result.at[tuple(index_at)].set(largest)


def shard_levels(key, extent, cuts, smallest, top_value):
    def one(position, parts):
        steps = jax.random.uniform(jax.random.fold_in(jax.random.fold_in(key, 6), position), (parts,), jnp.float32, smallest / len(cuts), top_value / len(cuts))
        return jnp.repeat(jnp.exp(steps), extent[position] // parts).reshape((-1,) + (1,) * (len(extent) - position - 1))

    loudness = one(*cuts[0])
    for cut in cuts[1:]:
        loudness = loudness * one(*cut)
    return loudness


def split_up(count, total, most, lean):
    weights = [(1 << 20) // math.isqrt(grade ** lean) + 1 for grade in range(2, count + 1)]
    surplus, given = total - most - (count - 1), [1] * (count - 1)
    while surplus > 0:
        free = [i for i in range(count - 1) if given[i] < most]
        whole, budget = sum([weights[i] for i in free]), surplus
        for i in free:
            extra = min(most - given[i], max(1, budget * weights[i] // whole), surplus)
            given[i] = given[i] + extra
            surplus = surplus - extra
    return np.array([most] + given)


def uneven_parts(key, amount, total, most, lean):
    if amount == 2:
        one = jax.random.randint(key, (), max(1, total - most), min(most, total - 1) + 1)
        return jnp.stack([one, total - one])
    lengths = jnp.asarray(split_up(amount, total, most, lean), jnp.int32)
    couples = (amount - 1) // 2
    giver, receiver = lengths[1:1 + 2 * couples:2], lengths[2:2 + 2 * couples:2]
    slack = jnp.minimum(giver - 1, most - receiver)
    passed = jax.random.randint(jax.random.fold_in(key, 1), (couples,), 0, 1 << 20) % (slack + 1)
    lengths = lengths.at[1:1 + 2 * couples:2].set(giver - passed).at[2:2 + 2 * couples:2].set(receiver + passed)
    return lengths[jax.random.permutation(jax.random.fold_in(key, 2), amount)]


def scatter_about(stream_key, extent, scale, most, pieces=(), held_as=jnp.bfloat16):
    loudness = shard_levels(stream_key, extent, pieces, -0.22, 0.18) if pieces else 1.0
    array = jax.random.normal(stream_key, extent, jnp.float32) * scale * loudness
    return jnp.minimum(jnp.maximum(array, -most), most).astype(held_as)


def setup_inputs(seed: int = 0) -> dict:
    key_list = jax.random.split(jax.random.key(seed), 13)
    depth_logits = draw_depth_logits(jax.random.fold_in(key_list[12], 71), 0)
    features = scatter_about(key_list[1], (GROUPS, PIX_ALL, CF), 1.0, 6.0, ((0, 2), (1, 128)))
    cell_index = plant(jax.random.randint(key_list[2], (GROUPS, PIX_ALL, DB), 0, TOK_DEV), jax.random.fold_in(key_list[2], 1), 0, TOK_DEV - 1).astype(jnp.int32)
    embed = scatter_about(key_list[3], (TOKEN_TOTAL, DI), 1.0, 6.0, ((0, 64), (1, 4)))
    w_visual = scatter_about(key_list[4], (CF, DI), CF ** -0.5, 0.75, ((1, 4),))
    w_gate = scatter_about(key_list[5], (CF, DI), CF ** -0.5, 0.75, ((1, 4),))
    input_map = scatter_about(key_list[6], (TOKEN_TOTAL, N), 0.08, 0.5, ((0, 64),))
    output_map = scatter_about(key_list[7], (TOKEN_TOTAL, N), 0.08, 0.5, ((0, 64),))
    forget = draw_forget(jax.random.fold_in(key_list[12], 71), 0)
    skip = draw_skip(jax.random.fold_in(key_list[12], 71), 0)
    frame_ids = jnp.searchsorted(jnp.cumsum(uneven_parts(key_list[10], TOKEN_TOTAL // 48, TOKEN_TOTAL, 96, 0)), jnp.arange(TOKEN_TOTAL), side="right").astype(jnp.int32)
    norm_gain = jnp.clip(1.0 + 0.18 * jax.random.normal(key_list[11], (DI,), jnp.float32), 0.1, 1.9)
    return dict(depth_logits=depth_logits, features=features, cell_index=cell_index, embed=embed, w_visual=w_visual, w_gate=w_gate, input_map=input_map, output_map=output_map, forget=forget, skip=skip, frame_ids=frame_ids, norm_gain=norm_gain)


EPSILON = 1e-05

def pool_block(items):
    depth_rows, feature_rows, cell_rows = items
    probability = jax.nn.softmax(depth_rows, axis=-1)
    lifted = probability[..., None] * feature_rows[:, :, None, :].astype(jnp.float32)
    return jax.ops.segment_sum(lifted.reshape(-1, CF), cell_rows.reshape(-1), num_segments=TOK_DEV)

def reference(depth_logits, features, cell_index, embed, w_visual, w_gate, input_map, output_map, forget, skip, frame_ids, norm_gain):
    highest = lax.Precision.HIGHEST
    depth_blocks = depth_logits.reshape(GROUPS, N_CTX, PIX_BLOCK, DB).transpose(1, 0, 2, 3)
    feature_blocks = features.reshape(GROUPS, N_CTX, PIX_BLOCK, CF).transpose(1, 0, 2, 3)
    cell_blocks = cell_index.reshape(GROUPS, N_CTX, PIX_BLOCK, DB).transpose(1, 0, 2, 3)
    pooled = lax.map(pool_block, (depth_blocks, feature_blocks, cell_blocks)).reshape(TOKEN_TOTAL, CF)
    visual_part = jnp.dot(pooled, w_visual.astype(jnp.float32), precision=highest)
    stream = (embed.astype(jnp.float32) + visual_part).astype(jnp.bfloat16)
    gate_act = jnp.dot(pooled, w_gate.astype(jnp.float32), precision=highest)
    block_count = TOKEN_TOTAL // BLK
    streams = stream.reshape(block_count, BLK, H, P_SIZE)
    cumulative = jnp.cumsum(forget.reshape(block_count, BLK, H), axis=1)
    writes = input_map.reshape(block_count, BLK, N)
    read_all = output_map.reshape(block_count, BLK, N)
    frames = frame_ids.reshape(block_count, BLK)
    row_order = lax.broadcasted_iota(jnp.int32, (BLK, BLK), 0)
    col_order = lax.broadcasted_iota(jnp.int32, (BLK, BLK), 1)

    def advance(carry_state, items):
        block_stream, block_cum, write_rows, read_rows, frame_rows = items
        stream_wide = block_stream.astype(jnp.float32)
        scores = jnp.dot(read_rows, write_rows.T, preferred_element_type=jnp.float32)
        visible = (col_order <= row_order) | (frame_rows[:, None] == frame_rows[None, :])
        distance = jnp.abs(block_cum[:, None, :] - block_cum[None, :, :])
        weights = jnp.where(visible[..., None], scores[..., None] * jnp.exp(-distance), 0.0).astype(jnp.bfloat16)
        within = jnp.einsum('tsh,shp->thp', weights.astype(jnp.float32), stream_wide, precision=highest)
        block_end = block_cum[-1]
        keys_scaled = (jnp.exp(block_cum - block_end[None, :])[..., None] * write_rows.astype(jnp.float32)[:, None, :]).astype(jnp.bfloat16)
        block_state = jnp.einsum('shn,shp->hnp', keys_scaled.astype(jnp.float32), stream_wide, precision=highest)
        reads_scaled = read_rows.astype(jnp.float32)[:, None, :] * jnp.exp(-block_cum)[..., None]
        carried = jnp.einsum('thn,hnp->thp', reads_scaled, carry_state, precision=highest)
        mixed = within + carried + skip[None, :, None] * stream_wide
        return (jnp.exp(-block_end)[:, None, None] * carry_state + block_state, mixed)
    initial = jnp.zeros((H, N, P_SIZE), jnp.float32)
    unused, mixed = lax.scan(advance, initial, (streams, cumulative, writes, read_all, frames))
    gated = mixed.reshape(TOKEN_TOTAL, DI) * jax.nn.silu(gate_act)
    energy = lax.optimization_barrier(jnp.sum(gated * gated, axis=1))
    return (gated * lax.rsqrt(energy / DI + EPSILON)[:, None] * norm_gain[None, :]).astype(jnp.bfloat16)
```

```python
import functools
import math

import jax
import jax.numpy as jnp
from jax import lax
from jax.experimental import pallas as pl
from jax.experimental.pallas import tpu as pltpu
from jax.sharding import PartitionSpec as P

P_SIZE = 128
N = 128
BLK = 256
CF = 64
DI = 8192
EPSILON = 1e-05
LOG2E = math.log2(math.e)
CHUNK = 64
EXTRA = 8

f32 = jnp.float32
bf16 = jnp.bfloat16

VMEM = pl.BlockSpec(memory_space=pltpu.VMEM)
SMEM = pl.BlockSpec(memory_space=pltpu.SMEM)
PARAMS = pltpu.CompilerParams(vmem_limit_bytes=48 * 1024 * 1024)


def terms(x, count):
    parts = []
    for _ in range(count - 1):
        part = x.astype(bf16)
        parts.append(part)
        x = x - part.astype(f32)
    parts.append(x.astype(bf16))
    return parts


def dot(a, b):
    return jnp.dot(a, b, preferred_element_type=f32)


def pool_kernel(logits_ref, cells_ref, feats_ref, out_ref, wide, prob, cell, hits):
    rows, bins = logits_ref.shape
    wide[:, :bins] = logits_ref[...]
    logits = wide[...].T[:bins]
    raised = jnp.exp(logits - jnp.max(logits, axis=0, keepdims=True))
    prob[...] = raised / jnp.sum(raised, axis=0, keepdims=True)
    wide[:, :bins] = cells_ref[...].astype(f32)
    cell[...] = wide[...].T[:bins]

    def chunk(k, carry):
        first = pl.multiple_of(k * CHUNK, CHUNK)
        ids = (lax.broadcasted_iota(jnp.int32, (CHUNK, rows), 0) + first).astype(f32)
        acc = jnp.zeros((CHUNK, rows), f32)
        for d in range(bins):
            acc = acc + jnp.where(cell[d : d + 1, :] == ids, prob[d : d + 1, :], 0.0)
        high, low = terms(acc, 2)
        hits[pl.ds(first, CHUNK), :rows] = high
        hits[pl.ds(first, CHUNK), rows:] = low
        return carry

    lax.fori_loop(0, hits.shape[0] // CHUNK, chunk, 0)
    feats = feats_ref[...]
    pooled = dot(hits[...], jnp.concatenate([feats, feats], axis=0))
    half = pooled.shape[0] // 2
    out_ref[...] = jnp.concatenate([pooled[:half], pooled[half:]], axis=1)


def mask_kernel(
    forget_ref, in_ref, read_ref, frames_ref, weights_ref, keys_ref, ends_ref, decay_ref, wide, cum_t
):
    heads = forget_ref.shape[1]
    blocks = weights_ref.shape[0]
    row_order = lax.broadcasted_iota(jnp.int32, (BLK, BLK), 0)
    col_order = lax.broadcasted_iota(jnp.int32, (BLK, BLK), 1)
    causal = col_order <= row_order
    lower = jnp.where(causal, 1.0, 0.0).astype(bf16)
    before = jnp.zeros((1, heads), f32)
    for b in range(blocks):
        rows = slice(b * BLK, (b + 1) * BLK)
        cum = sum(dot(lower, part) for part in terms(forget_ref[rows, :], 3))
        wide[rows, :heads] = cum
        decay = terms(jnp.exp(-(cum + before)), 3)
        own = terms(jnp.exp(-cum), 3)
        decay_ref[0, rows, :] = jnp.concatenate(decay, axis=1)
        decay_ref[1, rows, :] = jnp.concatenate(own, axis=1)
        before = before + cum[BLK - 1 :, :]
    turned = wide[...].T
    cum_t[...] = turned[:heads]

    def block(b, carry):
        rows = pl.ds(pl.multiple_of(b * BLK, BLK), BLK)
        scores = lax.dot_general(
            read_ref[rows, :], in_ref[rows, :], (((1,), (1,)), ((), ())), preferred_element_type=f32
        )
        frame_row = frames_ref[:, rows].astype(f32)
        frame_col = jnp.broadcast_to(frame_row, (128, BLK)).T
        same = jnp.concatenate([frame_col, frame_col], axis=1) == frame_row
        scored = jnp.where(causal | same, scores, 0.0)
        write_t = in_ref[rows, :].astype(f32).T
        cum_b = cum_t[:, rows]
        end = cum_b[:, BLK - 1 :]
        rise = jnp.exp(cum_b - end)
        ends_ref[b] = jnp.broadcast_to(end, (heads, 128))
        scaled_rows = cum_b * LOG2E
        scaled_cols = wide[rows, :] * LOG2E
        for h in range(heads):
            distance = jnp.abs(scaled_cols[:, h : h + 1] - scaled_rows[h : h + 1, :])
            weights_ref[b, h] = (scored * jnp.exp2(-distance)).astype(bf16)
            keys_ref[b, h] = (write_t * rise[h : h + 1, :]).astype(bf16)
        return carry

    lax.fori_loop(0, blocks, block, 0)


def stream_kernel(
    mine_ref, other_ref, w_ref, embed_ref, keys_ref, ends_ref, stream_ref, pay_ref, first_ref, pooled_ref
):
    packed = mine_ref[...] + other_ref[...]
    pooled = jnp.concatenate([packed[:, :CF], packed[:, CF:]], axis=0)
    pooled_ref[...] = jnp.concatenate(terms(pooled, 3), axis=1)
    heads = first_ref.shape[0]

    def pair(q, carry):
        lanes = pl.ds(pl.multiple_of(q * 256, 256), 256)
        w = w_ref[:, lanes]
        visual = dot(pooled_ref[...], jnp.concatenate([w, w, w], axis=0))
        stream = (embed_ref[:, lanes].astype(f32) + visual).astype(bf16)
        stream_ref[:, lanes] = stream
        for j in range(2):
            h = 2 * q + j
            part = stream[:, j * P_SIZE : (j + 1) * P_SIZE]
            early = dot(keys_ref[0, h], part[:BLK])
            late = dot(keys_ref[1, h], part[BLK:])
            end_early = ends_ref[0, pl.ds(h, 1), :]
            end_late = ends_ref[1, pl.ds(h, 1), :]
            first_ref[h] = early
            pay_ref[h, :N, :] = jnp.exp(-end_late) * early + late
            pay_ref[h, N:, :] = jnp.broadcast_to(end_early + end_late, (EXTRA, P_SIZE))
        return carry

    lax.fori_loop(0, heads // 2, pair, 0)


def pick(heads, h):
    row = lax.broadcasted_iota(jnp.int32, (3 * heads, P_SIZE), 0)
    hit = (row == h) | (row == h + heads) | (row == h + 2 * heads)
    return jnp.where(hit, 1.0, 0.0).astype(bf16)


def within_kernel(
    weights_ref, stream_ref, pooled_ref, w_ref, skip_ref, first_ref, read_ref, decay_ref, base_ref, gain_ref
):
    heads = first_ref.shape[0]
    read = read_ref[BLK:, :]
    read_twice = jnp.concatenate([read, read], axis=1)

    def head(h, carry):
        lanes = pl.ds(pl.multiple_of(h * P_SIZE, P_SIZE), P_SIZE)
        w = w_ref[:, lanes]
        gate = dot(pooled_ref[...], jnp.concatenate([w, w, w], axis=0))
        silu = gate / (1.0 + jnp.exp(-gate))
        chosen = pick(heads, h)
        gain_ref[:, lanes] = silu * dot(decay_ref[0], chosen)
        stream = stream_ref[:, lanes]
        direct = skip_ref[0, h] * stream.astype(f32)
        early = dot(weights_ref[0, h], stream[:BLK])
        late = dot(weights_ref[1, h], stream[BLK:])
        state = jnp.concatenate(terms(first_ref[h], 2), axis=0)
        late = late + dot(decay_ref[1, BLK:, :], chosen) * dot(read_twice, state)
        base_ref[:BLK, lanes] = (early + direct[:BLK]) * silu[:BLK]
        base_ref[BLK:, lanes] = (late + direct[BLK:]) * silu[BLK:]
        return carry

    lax.fori_loop(0, heads, head, 0)


def total_kernel(got_ref, total_ref):
    state = got_ref[0, :N, :]
    log = got_ref[0, N:, :]
    for i in range(1, got_ref.shape[0]):
        gone = got_ref[i, N:, :]
        state = jnp.exp(-gone[:1]) * state + got_ref[i, :N, :]
        log = log + gone
    total_ref[:N, :] = state
    total_ref[N:, :] = log


def join_kernel(total_ref, near_ref, out_ref):
    out_ref[...] = total_ref[:N, :] + jnp.exp(-total_ref[N : N + 1, :]) * near_ref[:N, :]


def spread_kernel(got_ref, near_ref, far_ref, out_ref):
    state = near_ref[:N, :] + jnp.exp(-near_ref[N : N + 1, :]) * far_ref[...]
    for i in range(got_ref.shape[0]):
        out_ref[i] = state
        state = jnp.exp(-got_ref[i, N : N + 1, :]) * state + got_ref[i, :N, :]


def carry_kernel(state_ref, read_ref, base_ref, gain_ref, gated_ref, energy_ref, acc):
    heads = state_ref.shape[0]
    read = read_ref[...]
    read_twice = jnp.concatenate([read, read], axis=1)
    acc[...] = jnp.zeros_like(acc)

    def head(h, carry):
        lanes = pl.ds(pl.multiple_of(h * P_SIZE, P_SIZE), P_SIZE)
        state = jnp.concatenate(terms(state_ref[h], 2), axis=0)
        gated = base_ref[:, lanes] + gain_ref[:, lanes] * dot(read_twice, state)
        gated_ref[:, lanes] = gated
        acc[...] += gated * gated
        return carry

    lax.fori_loop(0, heads, head, 0)
    energy_ref[...] = jnp.sum(acc[...].T, axis=0, keepdims=True)


def norm_kernel(gated_ref, mine_ref, other_ref, gain_ref, out_ref):
    inverse = lax.rsqrt((mine_ref[...] + other_ref[...]) / DI + EPSILON)
    column = jnp.broadcast_to(inverse, (P_SIZE, inverse.shape[1])).T

    def head(h, carry):
        lanes = pl.ds(pl.multiple_of(h * P_SIZE, P_SIZE), P_SIZE)
        out_ref[:, lanes] = (gated_ref[:, lanes] * column * gain_ref[:, lanes]).astype(bf16)
        return carry

    lax.fori_loop(0, gated_ref.shape[1] // P_SIZE, head, 0)


def call(kernel, ins, outs, scratch=(), specs=None):
    return pl.pallas_call(
        kernel,
        out_shape=[jax.ShapeDtypeStruct(shape, dtype) for shape, dtype in outs],
        in_specs=specs or [VMEM] * len(ins),
        out_specs=[VMEM] * len(outs),
        scratch_shapes=list(scratch),
        compiler_params=PARAMS,
    )(*ins)


def swap(value, axis):
    return lax.ppermute(value, axis, [(0, 1), (1, 0)])


def body(
    depth_logits,
    features,
    cell_index,
    embed,
    w_visual,
    w_gate,
    input_map,
    output_map,
    forget,
    skip,
    frame_ids,
    norm_gain,
):
    tokens, width = embed.shape
    heads = forget.shape[1]
    blocks = tokens // BLK
    pixels, bins = depth_logits.shape[1:]
    shards = lax.axis_size("ctx")
    groups = [list(range(g, g + heads)) for g in range(0, shards, heads)]

    (partial_sum,) = call(
        pool_kernel,
        (depth_logits[0], cell_index[0], features[0]),
        [((tokens // 2, 2 * CF), f32)],
        [
            pltpu.VMEM((pixels, 128), f32),
            pltpu.VMEM((bins, pixels), f32),
            pltpu.VMEM((bins, pixels), f32),
            pltpu.VMEM((tokens, 2 * pixels), bf16),
        ],
    )
    chip_sum = partial_sum + swap(partial_sum, "mp")
    other_sum = swap(chip_sum, "section")

    weights, keys, ends, decay = call(
        mask_kernel,
        (forget, input_map, output_map, frame_ids.reshape(1, tokens)),
        [
            ((blocks, heads, BLK, BLK), bf16),
            ((blocks, heads, N, BLK), bf16),
            ((blocks, heads, 128), f32),
            ((2, tokens, 3 * heads), bf16),
        ],
        [pltpu.VMEM((tokens, 128), f32), pltpu.VMEM((heads, tokens), f32)],
    )

    stream, pay, first, pooled = call(
        stream_kernel,
        (chip_sum, other_sum, w_visual, embed, keys, ends),
        [
            ((tokens, width), bf16),
            ((heads, N + EXTRA, P_SIZE), f32),
            ((heads, N, P_SIZE), f32),
            ((tokens, 3 * CF), bf16),
        ],
    )
    got = lax.all_to_all(pay, "ctx", 0, 0, axis_index_groups=groups, tiled=True)

    base, gain = call(
        within_kernel,
        (weights, stream, pooled, w_gate, skip.reshape(1, heads), first, output_map, decay),
        [((tokens, width), f32), ((tokens, width), f32)],
        specs=[VMEM] * 4 + [SMEM] + [VMEM] * 3,
    )

    (total,) = call(total_kernel, (got,), [((N + EXTRA, P_SIZE), f32)])
    near = lax.ppermute(total, "ctx", [(i, i + heads) for i in range(shards - heads)])
    (joined,) = call(join_kernel, (total, near), [((N, P_SIZE), f32)])
    far = lax.ppermute(joined, "ctx", [(i, i + 2 * heads) for i in range(shards - 2 * heads)])
    (sent,) = call(spread_kernel, (got, near, far), [((heads, N, P_SIZE), f32)])
    incoming = lax.all_to_all(sent, "ctx", 0, 0, axis_index_groups=groups, tiled=True)

    gated, energy = call(
        carry_kernel,
        (incoming, output_map, base, gain),
        [((tokens, width), f32), ((1, tokens), f32)],
        [pltpu.VMEM((tokens, P_SIZE), f32)],
    )
    chip_energy = energy + swap(energy, "mp")
    other_energy = swap(chip_energy, "section")
    (out,) = call(
        norm_kernel,
        (gated, chip_energy, other_energy, norm_gain.reshape(1, width)),
        [((tokens, width), bf16)],
    )
    return out


def solution(mesh):
    return jax.shard_map(
        body,
        mesh=mesh,
        in_specs=(
            P("section", ("ctx", "mp"), None),
            P("section", ("ctx", "mp"), None),
            P("section", ("ctx", "mp"), None),
            P("ctx", ("section", "mp")),
            P(None, ("section", "mp")),
            P(None, ("section", "mp")),
            P("ctx", None),
            P("ctx", None),
            P("ctx", ("section", "mp")),
            P(("section", "mp")),
            P("ctx"),
            P(("section", "mp")),
        ),
        out_specs=P("ctx", ("section", "mp")),
        check_vma=False,
    )
```

```python
import math

import jax
import jax.numpy as jnp
from jax import lax
from jax.experimental import pallas as pl
from jax.experimental.pallas import tpu as pltpu
from jax.sharding import PartitionSpec as P

P_SIZE = 128
N = 128
BLK = 256
CF = 64
DI = 8192
EPSILON = 1e-05
LOG2E = math.log2(math.e)
CHUNK = 64
EXTRA = 8

f32 = jnp.float32
bf16 = jnp.bfloat16

VMEM = pl.BlockSpec(memory_space=pltpu.VMEM)
SMEM = pl.BlockSpec(memory_space=pltpu.SMEM)
HBM = pl.BlockSpec(memory_space=pltpu.HBM)
PARAMS = pltpu.CompilerParams(vmem_limit_bytes=24 * 1024 * 1024)


def terms(x, count):
    parts = []
    for _ in range(count - 1):
        part = x.astype(bf16)
        parts.append(part)
        x = x - part.astype(f32)
    parts.append(x.astype(bf16))
    return parts


def dot(a, b):
    return jnp.dot(a, b, preferred_element_type=f32)


def pool_kernel(*refs):
    count = (len(refs) - 4) // 2
    far, out_ref, near = refs[:count], refs[count], refs[count + 1 : 2 * count - 2]
    logits_ref, cells_ref, feats_ref, prob, hits, sems = refs[2 * count - 2 :]
    near = (logits_ref, cells_ref, feats_ref) + tuple(near)
    copies = [pltpu.make_async_copy(far[i], near[i], sems.at[i]) for i in range(count)]
    for copy in copies:
        copy.start()
    for copy in copies[:3]:
        copy.wait()
    bins, _, rows = logits_ref.shape
    logits = logits_ref[...]
    raised = jnp.exp(logits - jnp.max(logits, axis=0, keepdims=True))
    prob[...] = raised / jnp.sum(raised, axis=0, keepdims=True)

    def chunk(k, carry):
        first = pl.multiple_of(k * CHUNK, CHUNK)
        ids = lax.broadcasted_iota(jnp.int32, (CHUNK, rows), 0) + first
        acc = jnp.zeros((CHUNK, rows), f32)
        for d in range(bins):
            acc = acc + jnp.where(cells_ref[d] == ids, prob[d], 0.0)
        high, low = terms(acc, 2)
        hits[pl.ds(first, CHUNK), :rows] = high
        hits[pl.ds(first, CHUNK), rows:] = low
        return carry

    lax.fori_loop(0, hits.shape[0] // CHUNK, chunk, 0)
    feats = feats_ref[...]
    pooled = lax.dot_general(
        hits[...],
        jnp.concatenate([feats, feats], axis=1),
        (((1,), (1,)), ((), ())),
        preferred_element_type=f32,
    )
    half = pooled.shape[0] // 2
    out_ref[...] = jnp.concatenate([pooled[:half], pooled[half:]], axis=1)
    for copy in copies[3:]:
        copy.wait()


def mask_kernel(
    forget_ref, in_ref, read_ref, frames_ref, weights_ref, keys_ref, ends_ref, decay_ref, wide, turned, cum_t
):
    heads = forget_ref.shape[0]
    blocks = weights_ref.shape[0]
    row_order = lax.broadcasted_iota(jnp.int32, (BLK, BLK), 0)
    col_order = lax.broadcasted_iota(jnp.int32, (BLK, BLK), 1)
    causal = col_order <= row_order
    upper = jnp.where(row_order <= col_order, 1.0, 0.0).astype(bf16)
    for b in range(blocks):
        lanes = slice(b * BLK, (b + 1) * BLK)
        cum_t[:, lanes] = sum(dot(part, upper) for part in terms(forget_ref[:, lanes], 3))
    turned[:heads, :] = cum_t[...]
    wide[...] = turned[...].T
    before = jnp.zeros((1, heads), f32)
    for b in range(blocks):
        rows = slice(b * BLK, (b + 1) * BLK)
        cum = wide[rows, :heads]
        decay_ref[0, rows, :] = jnp.concatenate(terms(jnp.exp(-(cum + before)), 3), axis=1)
        decay_ref[1, rows, :] = jnp.concatenate(terms(jnp.exp(-cum), 3), axis=1)
        before = before + cum[BLK - 1 :, :]

    def block(b, carry):
        rows = pl.ds(pl.multiple_of(b * BLK, BLK), BLK)
        scores = lax.dot_general(
            read_ref[rows, :], in_ref[rows, :], (((1,), (1,)), ((), ())), preferred_element_type=f32
        )
        frame_row = frames_ref[:, rows].astype(f32)
        frame_col = jnp.broadcast_to(frame_row, (128, BLK)).T
        same = jnp.concatenate([frame_col, frame_col], axis=1) == frame_row
        scored = jnp.where(causal | same, scores, 0.0)
        write_t = in_ref[rows, :].astype(f32).T
        cum_b = cum_t[:, rows]
        end = cum_b[:, BLK - 1 :]
        rise = jnp.exp(cum_b - end)
        ends_ref[b] = jnp.broadcast_to(end, (heads, 128))
        scaled_rows = cum_b * LOG2E
        scaled_cols = wide[rows, :] * LOG2E
        for h in range(heads):
            distance = jnp.abs(scaled_cols[:, h : h + 1] - scaled_rows[h : h + 1, :])
            weights_ref[b, h] = (scored * jnp.exp2(-distance)).astype(bf16)
            keys_ref[b, h] = (write_t * rise[h : h + 1, :]).astype(bf16)
        return carry

    lax.fori_loop(0, blocks, block, 0)


def stream_kernel(
    mine_ref, other_ref, w_ref, embed_ref, keys_ref, ends_ref, stream_ref, pay_ref, first_ref, pooled_ref
):
    packed = mine_ref[...] + other_ref[...]
    pooled = jnp.concatenate([packed[:, :CF], packed[:, CF:]], axis=0)
    pooled_ref[...] = jnp.concatenate(terms(pooled, 3), axis=1)
    heads = first_ref.shape[0]

    def pair(q, carry):
        lanes = pl.ds(pl.multiple_of(q * 256, 256), 256)
        w = w_ref[:, lanes]
        visual = dot(pooled_ref[...], jnp.concatenate([w, w, w], axis=0))
        stream = (embed_ref[:, lanes].astype(f32) + visual).astype(bf16)
        stream_ref[:, lanes] = stream
        for j in range(2):
            h = 2 * q + j
            part = stream[:, j * P_SIZE : (j + 1) * P_SIZE]
            early = dot(keys_ref[0, h], part[:BLK])
            late = dot(keys_ref[1, h], part[BLK:])
            end_early = ends_ref[0, pl.ds(h, 1), :]
            end_late = ends_ref[1, pl.ds(h, 1), :]
            first_ref[h] = early
            pay_ref[h, :N, :] = jnp.exp(-end_late) * early + late
            pay_ref[h, N:, :] = jnp.broadcast_to(end_early + end_late, (EXTRA, P_SIZE))
        return carry

    lax.fori_loop(0, heads // 2, pair, 0, unroll=2)


def pick(heads, q):
    row = lax.broadcasted_iota(jnp.int32, (3 * heads, 2 * P_SIZE), 0)
    lane = lax.broadcasted_iota(jnp.int32, (3 * heads, 2 * P_SIZE), 1)
    h = 2 * q + jnp.where(lane < P_SIZE, 0, 1)
    hit = (row == h) | (row == h + heads) | (row == h + 2 * heads)
    return jnp.where(hit, 1.0, 0.0).astype(bf16)


def side_by_side(ref, q):
    parts = [jnp.concatenate(terms(ref[2 * q + j], 2), axis=0) for j in range(2)]
    return jnp.concatenate(parts, axis=1)


def within_kernel(
    weights_ref, stream_ref, pooled_ref, w_ref, skip_ref, first_ref, read_ref, decay_ref, base_ref, gain_ref
):
    heads = first_ref.shape[0]
    read = read_ref[BLK:, :]
    read_twice = jnp.concatenate([read, read], axis=1)

    def pair(q, carry):
        lanes = pl.ds(pl.multiple_of(q * 2 * P_SIZE, 2 * P_SIZE), 2 * P_SIZE)
        w = w_ref[:, lanes]
        gate = dot(pooled_ref[...], jnp.concatenate([w, w, w], axis=0))
        silu = gate / (1.0 + jnp.exp(-gate))
        chosen = pick(heads, q)
        gain_ref[:, lanes] = silu * dot(decay_ref[0], chosen)
        stream = stream_ref[:, lanes]
        early, late = [], []
        for j in range(2):
            h = 2 * q + j
            part = stream[:, j * P_SIZE : (j + 1) * P_SIZE]
            direct = skip_ref[0, h] * part.astype(f32)
            early.append(dot(weights_ref[0, h], part[:BLK]) + direct[:BLK])
            late.append(dot(weights_ref[1, h], part[BLK:]) + direct[BLK:])
        carried = dot(decay_ref[1, BLK:, :], chosen) * dot(read_twice, side_by_side(first_ref, q))
        base_ref[:BLK, lanes] = jnp.concatenate(early, axis=1) * silu[:BLK]
        base_ref[BLK:, lanes] = (jnp.concatenate(late, axis=1) + carried) * silu[BLK:]
        return carry

    lax.fori_loop(0, heads // 2, pair, 0)


def total_kernel(got_ref, total_ref):
    state = got_ref[0, :N, :]
    log = got_ref[0, N:, :]
    for i in range(1, got_ref.shape[0]):
        gone = got_ref[i, N:, :]
        state = jnp.exp(-gone[:1]) * state + got_ref[i, :N, :]
        log = log + gone
    for k in range(total_ref.shape[0]):
        total_ref[k, :N, :] = state
        total_ref[k, N:, :] = log


def spread_kernel(got_ref, totals_ref, place_ref, out_ref):
    place = place_ref[0]
    state = jnp.zeros(out_ref.shape[1:], f32)
    for k in range(totals_ref.shape[0] - 1):
        later = jnp.exp(-totals_ref[k, N : N + 1, :]) * state + totals_ref[k, :N, :]
        state = jnp.where(k < place, later, state)
    for i in range(got_ref.shape[0]):
        out_ref[i] = state
        state = jnp.exp(-got_ref[i, N : N + 1, :]) * state + got_ref[i, :N, :]


def carry_kernel(state_ref, read_ref, base_ref, gain_ref, gated_ref, energy_ref, acc):
    heads = state_ref.shape[0]
    read = read_ref[...]
    read_twice = jnp.concatenate([read, read], axis=1)
    acc[...] = jnp.zeros_like(acc)

    def pair(q, carry):
        lanes = pl.ds(pl.multiple_of(q * 2 * P_SIZE, 2 * P_SIZE), 2 * P_SIZE)
        gated = base_ref[:, lanes] + gain_ref[:, lanes] * dot(read_twice, side_by_side(state_ref, q))
        gated_ref[:, lanes] = gated
        squares = gated * gated
        acc[...] += squares[:, :P_SIZE] + squares[:, P_SIZE:]
        return carry

    lax.fori_loop(0, heads // 2, pair, 0, unroll=2)
    energy_ref[...] = jnp.sum(acc[...].T, axis=0, keepdims=True)


def norm_kernel(gated_ref, mine_ref, other_ref, gain_ref, out_ref, held, sems):
    inverse = lax.rsqrt((mine_ref[...] + other_ref[...]) / DI + EPSILON)
    copies = []
    for k in range(held.shape[0] // P_SIZE):
        rows = slice(k * P_SIZE, (k + 1) * P_SIZE)
        column = jnp.broadcast_to(inverse[:, rows], (P_SIZE, P_SIZE)).T

        def head(h, carry):
            lanes = pl.ds(pl.multiple_of(h * P_SIZE, P_SIZE), P_SIZE)
            held[rows, lanes] = (gated_ref[rows, lanes] * column * gain_ref[:, lanes]).astype(bf16)
            return carry

        lax.fori_loop(0, held.shape[1] // P_SIZE, head, 0, unroll=4)
        copies.append(pltpu.make_async_copy(held.at[rows], out_ref.at[rows], sems.at[k]))
        copies[-1].start()
    for copy in copies:
        copy.wait()


def call(kernel, ins, outs, scratch=(), specs=None, out_specs=None):
    return pl.pallas_call(
        kernel,
        out_shape=[jax.ShapeDtypeStruct(shape, dtype) for shape, dtype in outs],
        in_specs=specs or [VMEM] * len(ins),
        out_specs=out_specs or [VMEM] * len(outs),
        scratch_shapes=list(scratch),
        compiler_params=PARAMS,
    )(*ins)


def swap(value, axis):
    return lax.ppermute(value, axis, [(0, 1), (1, 0)])


def body(
    depth_logits,
    features,
    cell_index,
    embed,
    w_visual,
    w_gate,
    input_map,
    output_map,
    forget,
    skip,
    frame_ids,
    norm_gain,
):
    tokens, width = embed.shape
    heads = forget.shape[1]
    blocks = tokens // BLK
    pixels, bins = depth_logits.shape[1:]
    shards = lax.axis_size("ctx")
    groups = [list(range(g, g + heads)) for g in range(0, shards, heads)]
    peers = [list(range(g, shards, heads)) for g in range(heads)]
    place = (lax.axis_index("ctx") // heads).astype(jnp.int32).reshape(1)

    near = (depth_logits.transpose(2, 0, 1), cell_index.transpose(2, 0, 1), features[0].T)
    far = (forget.T, input_map, output_map, frame_ids.reshape(1, tokens))
    far += (w_visual, embed, w_gate, norm_gain.reshape(1, width))
    partial_sum, forget, input_map, output_map, frames, w_visual, embed, w_gate, norm_gain = call(
        pool_kernel,
        tuple(pltpu.with_memory_space_constraint(array, pltpu.HBM) for array in near + far),
        [((tokens // 2, 2 * CF), f32)] + [(array.shape, array.dtype) for array in far],
        [
            pltpu.VMEM((bins, 1, pixels), f32),
            pltpu.VMEM((bins, 1, pixels), jnp.int32),
            pltpu.VMEM((CF, pixels), bf16),
            pltpu.VMEM((bins, 1, pixels), f32),
            pltpu.VMEM((tokens, 2 * pixels), bf16),
            pltpu.SemaphoreType.DMA((3 + len(far),)),
        ],
        specs=[HBM] * (3 + len(far)),
    )
    chip_sum = partial_sum + swap(partial_sum, "mp")
    other_sum = swap(chip_sum, "section")

    weights, keys, ends, decay = call(
        mask_kernel,
        (forget, input_map, output_map, frames),
        [
            ((blocks, heads, BLK, BLK), bf16),
            ((blocks, heads, N, BLK), bf16),
            ((blocks, heads, 128), f32),
            ((2, tokens, 3 * heads), bf16),
        ],
        [
            pltpu.VMEM((tokens, 128), f32),
            pltpu.VMEM((128, tokens), f32),
            pltpu.VMEM((heads, tokens), f32),
        ],
    )

    stream, pay, first, pooled = call(
        stream_kernel,
        (chip_sum, other_sum, w_visual, embed, keys, ends),
        [
            ((tokens, width), bf16),
            ((heads, N + EXTRA, P_SIZE), f32),
            ((heads, N, P_SIZE), f32),
            ((tokens, 3 * CF), bf16),
        ],
    )
    got = lax.all_to_all(pay, "ctx", 0, 0, axis_index_groups=groups, tiled=True)

    base, gain = call(
        within_kernel,
        (weights, stream, pooled, w_gate, skip.reshape(1, heads), first, output_map, decay),
        [((tokens, width), f32), ((tokens, width), f32)],
        specs=[VMEM] * 4 + [SMEM] + [VMEM] * 3,
    )

    (total,) = call(total_kernel, (got,), [((shards // heads, N + EXTRA, P_SIZE), f32)])
    totals = lax.all_to_all(total, "ctx", 0, 0, axis_index_groups=peers, tiled=True)
    (sent,) = call(
        spread_kernel, (got, totals, place), [((heads, N, P_SIZE), f32)], specs=[VMEM, VMEM, SMEM]
    )
    incoming = lax.all_to_all(sent, "ctx", 0, 0, axis_index_groups=groups, tiled=True)

    gated, energy = call(
        carry_kernel,
        (incoming, output_map, base, gain),
        [((tokens, width), f32), ((1, tokens), f32)],
        [pltpu.VMEM((tokens, P_SIZE), f32)],
    )
    chip_energy = energy + swap(energy, "mp")
    other_energy = swap(chip_energy, "section")
    (out,) = call(
        norm_kernel,
        (gated, chip_energy, other_energy, norm_gain),
        [((tokens, width), bf16)],
        [pltpu.VMEM((tokens, width), bf16), pltpu.SemaphoreType.DMA((tokens // P_SIZE,))],
        out_specs=[HBM],
    )
    return out


def solution(mesh):
    return jax.shard_map(
        body,
        mesh=mesh,
        in_specs=(
            P("section", ("ctx", "mp"), None),
            P("section", ("ctx", "mp"), None),
            P("section", ("ctx", "mp"), None),
            P("ctx", ("section", "mp")),
            P(None, ("section", "mp")),
            P(None, ("section", "mp")),
            P("ctx", None),
            P("ctx", None),
            P("ctx", ("section", "mp")),
            P(("section", "mp")),
            P("ctx"),
            P(("section", "mp")),
        ),
        out_specs=P("ctx", ("section", "mp")),
        check_vma=False,
    )
```

```python
import math

import jax
import jax.numpy as jnp
from jax import lax
from jax.experimental import pallas as pl
from jax.experimental.pallas import tpu as pltpu
from jax.sharding import PartitionSpec as P

P_SIZE = 128
N = 128
BLK = 256
CF = 64
DI = 8192
EPSILON = 1e-05
LOG2E = math.log2(math.e)
CHUNK = 64
EXTRA = 8

f32 = jnp.float32
bf16 = jnp.bfloat16

VMEM = pl.BlockSpec(memory_space=pltpu.VMEM)
SMEM = pl.BlockSpec(memory_space=pltpu.SMEM)
HBM = pl.BlockSpec(memory_space=pltpu.HBM)
PARAMS = pltpu.CompilerParams(vmem_limit_bytes=24 * 1024 * 1024)


def terms(x, count):
    parts = []
    for _ in range(count - 1):
        part = x.astype(bf16)
        parts.append(part)
        x = x - part.astype(f32)
    parts.append(x.astype(bf16))
    return parts


def dot(a, b):
    return jnp.dot(a, b, preferred_element_type=f32)


def fetch(far, near, sems):
    copies = [pltpu.make_async_copy(f, n, sems.at[i]) for i, (f, n) in enumerate(zip(far, near))]
    for copy in copies:
        copy.start()
    return copies


def pool_kernel(*refs):
    count = (len(refs) - 4) // 2
    far, out_ref, near = refs[:count], refs[count], refs[count + 1 : 2 * count - 2]
    logits_ref, cells_ref, feats_ref, prob, hits, sems = refs[2 * count - 2 :]
    near = (logits_ref, cells_ref, feats_ref) + tuple(near)
    copies = [pltpu.make_async_copy(far[i], near[i], sems.at[i]) for i in range(count)]
    for copy in copies:
        copy.start()
    for copy in copies[:3]:
        copy.wait()
    bins, _, rows = logits_ref.shape
    logits = logits_ref[...]
    raised = jnp.exp(logits - jnp.max(logits, axis=0, keepdims=True))
    prob[...] = raised / jnp.sum(raised, axis=0, keepdims=True)

    def chunk(k, carry):
        first = pl.multiple_of(k * CHUNK, CHUNK)
        ids = lax.broadcasted_iota(jnp.int32, (CHUNK, rows), 0) + first
        acc = jnp.zeros((CHUNK, rows), f32)
        for d in range(bins):
            acc = acc + jnp.where(cells_ref[d] == ids, prob[d], 0.0)
        high, low = terms(acc, 2)
        hits[pl.ds(first, CHUNK), :rows] = high
        hits[pl.ds(first, CHUNK), rows:] = low
        return carry

    lax.fori_loop(0, hits.shape[0] // CHUNK, chunk, 0)
    feats = feats_ref[...]
    pooled = lax.dot_general(
        hits[...],
        jnp.concatenate([feats, feats], axis=1),
        (((1,), (1,)), ((), ())),
        preferred_element_type=f32,
    )
    half = pooled.shape[0] // 2
    out_ref[...] = jnp.concatenate([pooled[:half], pooled[half:]], axis=1)
    for copy in copies[3:]:
        copy.wait()


def decay_kernel(
    forget_ref, in_ref, keys_ref, ends_ref, columns_out, rows_out, columns_ref, rows_ref, wide, turned, sems
):
    heads = forget_ref.shape[0]
    blocks = keys_ref.shape[0]
    row_order = lax.broadcasted_iota(jnp.int32, (BLK, BLK), 0)
    col_order = lax.broadcasted_iota(jnp.int32, (BLK, BLK), 1)
    upper = jnp.where(row_order <= col_order, 1.0, 0.0).astype(bf16)
    for b in range(blocks):
        span = slice(b * BLK, (b + 1) * BLK)
        cum = sum(dot(part, upper) for part in terms(forget_ref[:, span], 3))
        turned[:heads, span] = cum
        end = cum[:, BLK - 1 :]
        rise = jnp.exp(cum - end)
        ends_ref[b] = jnp.broadcast_to(end, (heads, 128))
        write_t = in_ref[span, :].astype(f32).T
        for h in range(heads):
            keys_ref[b, h] = (write_t * rise[h : h + 1, :]).astype(bf16)
    rows_ref[...] = turned[:heads, :] * LOG2E
    wide[...] = turned[...].T
    before = jnp.zeros((1, heads), f32)
    for b in range(blocks):
        span = slice(b * BLK, (b + 1) * BLK)
        cum = wide[span, :heads]
        parts = terms(jnp.exp(-(cum + before)), 3) + terms(jnp.exp(-cum), 3) + terms(cum * LOG2E, 3)
        columns_ref[span, :] = jnp.concatenate(parts, axis=1)
        before = before + cum[BLK - 1 :, :]
    for copy in fetch((columns_ref, rows_ref), (columns_out, rows_out), sems):
        copy.wait()


def stream_kernel(
    mine_ref, other_ref, w_ref, embed_ref, keys_ref, ends_ref, pay_ref, *refs
):
    stream_out, first_out, pooled_out, stream_ref, first_ref, pooled_ref, sems = refs
    packed = mine_ref[...] + other_ref[...]
    pooled = jnp.concatenate([packed[:, :CF], packed[:, CF:]], axis=0)
    pooled_ref[...] = jnp.concatenate(terms(pooled, 3), axis=1)
    heads = first_ref.shape[0]
    saved = pltpu.make_async_copy(pooled_ref, pooled_out, sems.at[0, heads // 2])
    saved.start()

    def results(q):
        lanes = pl.ds(pl.multiple_of(q * 256, 256), 256)
        both = pl.ds(2 * q, 2)
        return (
            pltpu.make_async_copy(stream_ref.at[:, lanes], stream_out.at[:, lanes], sems.at[0, q]),
            pltpu.make_async_copy(first_ref.at[both], first_out.at[both], sems.at[1, q]),
        )

    def pair(q, carry):
        lanes = pl.ds(pl.multiple_of(q * 256, 256), 256)
        w = w_ref[:, lanes]
        visual = dot(pooled_ref[...], jnp.concatenate([w, w, w], axis=0))
        stream = (embed_ref[:, lanes].astype(f32) + visual).astype(bf16)
        stream_ref[:, lanes] = stream
        for j in range(2):
            h = 2 * q + j
            part = stream[:, j * P_SIZE : (j + 1) * P_SIZE]
            early = dot(keys_ref[0, h], part[:BLK])
            late = dot(keys_ref[1, h], part[BLK:])
            end_early = ends_ref[0, pl.ds(h, 1), :]
            end_late = ends_ref[1, pl.ds(h, 1), :]
            first_ref[h] = early
            pay_ref[h, :N, :] = jnp.exp(-end_late) * early + late
            pay_ref[h, N:, :] = jnp.broadcast_to(end_early + end_late, (EXTRA, P_SIZE))
        for copy in results(q):
            copy.start()
        return carry

    def finish(q, carry):
        for copy in results(q):
            copy.wait()
        return carry

    lax.fori_loop(0, heads // 2, pair, 0, unroll=2)
    lax.fori_loop(0, heads // 2, finish, 0)
    saved.wait()


def pick(heads, q):
    row = lax.broadcasted_iota(jnp.int32, (3 * heads, 2 * P_SIZE), 0)
    lane = lax.broadcasted_iota(jnp.int32, (3 * heads, 2 * P_SIZE), 1)
    h = 2 * q + jnp.where(lane < P_SIZE, 0, 1)
    hit = (row == h) | (row == h + heads) | (row == h + 2 * heads)
    return jnp.where(hit, 1.0, 0.0).astype(bf16)


def side_by_side(ref, q):
    parts = [jnp.concatenate(terms(ref[2 * q + j], 2), axis=0) for j in range(2)]
    return jnp.concatenate(parts, axis=1)


def within_kernel(skip_ref, *refs):
    far, (base_out, gain_out), near = refs[:9], refs[9:11], refs[11:20]
    base_ref, gain_ref, scored, in_sems, out_sems = refs[20:]
    copies = fetch(far, near, in_sems)
    in_ref, read_ref, frames_ref, rows_ref, columns_ref, w_ref, pooled_ref, first_ref, stream_ref = near
    heads = first_ref.shape[0]
    row_order = lax.broadcasted_iota(jnp.int32, (BLK, BLK), 0)
    col_order = lax.broadcasted_iota(jnp.int32, (BLK, BLK), 1)
    causal = col_order <= row_order
    for copy in copies[:3]:
        copy.wait()
    for b in range(scored.shape[0]):
        span = slice(b * BLK, (b + 1) * BLK)
        scores = lax.dot_general(
            read_ref[span, :], in_ref[span, :], (((1,), (1,)), ((), ())), preferred_element_type=f32
        )
        frame_row = frames_ref[:, span].astype(f32)
        frame_col = jnp.broadcast_to(frame_row, (128, BLK)).T
        same = jnp.concatenate([frame_col, frame_col], axis=1) == frame_row
        scored[b] = jnp.where(causal | same, scores, 0.0)
    for copy in copies[3:]:
        copy.wait()
    read = read_ref[BLK:, :]
    read_twice = jnp.concatenate([read, read], axis=1)
    late_rows = slice(BLK, 2 * BLK)

    def results(q):
        lanes = pl.ds(pl.multiple_of(q * 2 * P_SIZE, 2 * P_SIZE), 2 * P_SIZE)
        return (
            pltpu.make_async_copy(base_ref.at[:, lanes], base_out.at[:, lanes], out_sems.at[0, q]),
            pltpu.make_async_copy(gain_ref.at[:, lanes], gain_out.at[:, lanes], out_sems.at[1, q]),
        )

    def pair(q, carry):
        lanes = pl.ds(pl.multiple_of(q * 2 * P_SIZE, 2 * P_SIZE), 2 * P_SIZE)
        w = w_ref[:, lanes]
        gate = dot(pooled_ref[...], jnp.concatenate([w, w, w], axis=0))
        silu = gate / (1.0 + jnp.exp(-gate))
        chosen = pick(heads, q)
        gain_ref[:, lanes] = silu * dot(columns_ref[:, : 3 * heads], chosen)
        cum_col = dot(columns_ref[:, 6 * heads :], chosen)
        stream = stream_ref[:, lanes]
        mixed = [[], []]
        for j in range(2):
            h = 2 * q + j
            cum_row = rows_ref[pl.ds(h, 1), :]
            side = slice(j * P_SIZE, (j + 1) * P_SIZE)
            for b in range(2):
                span = slice(b * BLK, (b + 1) * BLK)
                column = cum_col[span, side]
                distance = jnp.abs(jnp.concatenate([column, column], axis=1) - cum_row[:, span])
                weights = (scored[b] * jnp.exp2(-distance)).astype(bf16)
                part = stream[span, side]
                mixed[b].append(dot(weights, part) + skip_ref[0, h] * part.astype(f32))
        own = dot(columns_ref[late_rows, 3 * heads : 6 * heads], chosen)
        carried = own * dot(read_twice, side_by_side(first_ref, q))
        base_ref[:BLK, lanes] = jnp.concatenate(mixed[0], axis=1) * silu[:BLK]
        base_ref[BLK:, lanes] = (jnp.concatenate(mixed[1], axis=1) + carried) * silu[BLK:]
        for copy in results(q):
            copy.start()
        return carry

    def finish(q, carry):
        for copy in results(q):
            copy.wait()
        return carry

    lax.fori_loop(0, heads // 2, pair, 0)
    lax.fori_loop(0, heads // 2, finish, 0)


def total_kernel(got_ref, total_ref):
    state = got_ref[0, :N, :]
    log = got_ref[0, N:, :]
    for i in range(1, got_ref.shape[0]):
        gone = got_ref[i, N:, :]
        state = jnp.exp(-gone[:1]) * state + got_ref[i, :N, :]
        log = log + gone
    for k in range(total_ref.shape[0]):
        total_ref[k, :N, :] = state
        total_ref[k, N:, :] = log


def spread_kernel(got_ref, totals_ref, place_ref, out_ref):
    place = place_ref[...]
    state = jnp.zeros(out_ref.shape[1:], f32)
    for k in range(totals_ref.shape[0] - 1):
        later = jnp.exp(-totals_ref[k, N : N + 1, :]) * state + totals_ref[k, :N, :]
        state = jnp.where(jnp.broadcast_to(place, state.shape) > k, later, state)
    for i in range(got_ref.shape[0]):
        out_ref[i] = state
        state = jnp.exp(-got_ref[i, N : N + 1, :]) * state + got_ref[i, :N, :]


def carry_kernel(state_ref, read_far, base_far, gain_far, gated_ref, energy_ref, read_ref, base_ref, gain_ref, acc, sems):
    heads = state_ref.shape[0]

    def operands(q):
        lanes = pl.ds(pl.multiple_of(q * 2 * P_SIZE, 2 * P_SIZE), 2 * P_SIZE)
        return (
            pltpu.make_async_copy(base_far.at[:, lanes], base_ref.at[:, lanes], sems.at[0, q]),
            pltpu.make_async_copy(gain_far.at[:, lanes], gain_ref.at[:, lanes], sems.at[1, q]),
        )

    first = pltpu.make_async_copy(read_far, read_ref, sems.at[0, heads // 2])
    first.start()
    for q in range(heads // 2):
        for copy in operands(q):
            copy.start()
    acc[...] = jnp.zeros_like(acc)
    first.wait()
    read = read_ref[...]
    read_twice = jnp.concatenate([read, read], axis=1)

    def pair(q, carry):
        lanes = pl.ds(pl.multiple_of(q * 2 * P_SIZE, 2 * P_SIZE), 2 * P_SIZE)
        carried = dot(read_twice, side_by_side(state_ref, q))
        for copy in operands(q):
            copy.wait()
        gated = base_ref[:, lanes] + gain_ref[:, lanes] * carried
        gated_ref[:, lanes] = gated
        squares = gated * gated
        acc[...] += squares[:, :P_SIZE] + squares[:, P_SIZE:]
        return carry

    lax.fori_loop(0, heads // 2, pair, 0)
    energy_ref[...] = jnp.sum(acc[...].T, axis=0, keepdims=True)


def norm_kernel(gated_ref, mine_ref, other_ref, gain_ref, out_ref, held, sems):
    inverse = lax.rsqrt((mine_ref[...] + other_ref[...]) / DI + EPSILON)
    copies = []
    for k in range(held.shape[0] // P_SIZE):
        rows = slice(k * P_SIZE, (k + 1) * P_SIZE)
        column = jnp.broadcast_to(inverse[:, rows], (P_SIZE, P_SIZE)).T

        def head(h, carry):
            lanes = pl.ds(pl.multiple_of(h * P_SIZE, P_SIZE), P_SIZE)
            held[rows, lanes] = (gated_ref[rows, lanes] * column * gain_ref[:, lanes]).astype(bf16)
            return carry

        lax.fori_loop(0, held.shape[1] // P_SIZE, head, 0, unroll=4)
        copies.append(pltpu.make_async_copy(held.at[rows], out_ref.at[rows], sems.at[k]))
        copies[-1].start()
    for copy in copies:
        copy.wait()


def outside(arrays):
    return tuple(pltpu.with_memory_space_constraint(array, pltpu.HBM) for array in arrays)


def call(kernel, ins, outs, scratch=(), specs=None):
    return pl.pallas_call(
        kernel,
        out_shape=[
            pltpu.HBM(*out[:2]) if out[2:] else jax.ShapeDtypeStruct(*out) for out in outs
        ],
        in_specs=specs or [VMEM] * len(ins),
        out_specs=[HBM if out[2:] else VMEM for out in outs],
        scratch_shapes=list(scratch),
        compiler_params=PARAMS,
    )(*ins)


def swap(value, axis):
    return lax.ppermute(value, axis, [(0, 1), (1, 0)])


def body(
    depth_logits,
    features,
    cell_index,
    embed,
    w_visual,
    w_gate,
    input_map,
    output_map,
    forget,
    skip,
    frame_ids,
    norm_gain,
):
    tokens, width = embed.shape
    heads = forget.shape[1]
    blocks = tokens // BLK
    pixels, bins = depth_logits.shape[1:]
    shards = lax.axis_size("ctx")
    groups = [list(range(g, g + heads)) for g in range(0, shards, heads)]
    peers = [list(range(g, shards, heads)) for g in range(heads)]
    place = jnp.full((1, P_SIZE), lax.axis_index("ctx") // heads, jnp.int32)

    near = (depth_logits.transpose(2, 0, 1), cell_index.transpose(2, 0, 1), features[0].T)
    far = (forget.T, input_map, w_visual, embed, norm_gain.reshape(1, width))
    partial_sum, forget_t, writes, w_visual, embed, norm_gain = call(
        pool_kernel,
        outside(near + far),
        [((tokens // 2, 2 * CF), f32)] + [(array.shape, array.dtype) for array in far],
        [
            pltpu.VMEM((bins, 1, pixels), f32),
            pltpu.VMEM((bins, 1, pixels), jnp.int32),
            pltpu.VMEM((CF, pixels), bf16),
            pltpu.VMEM((bins, 1, pixels), f32),
            pltpu.VMEM((tokens, 2 * pixels), bf16),
            pltpu.SemaphoreType.DMA((len(near + far),)),
        ],
        specs=[HBM] * len(near + far),
    )
    chip_sum = partial_sum + swap(partial_sum, "mp")
    other_sum = swap(chip_sum, "section")

    keys, ends, columns, row_sums = call(
        decay_kernel,
        (forget_t, writes),
        [
            ((blocks, heads, N, BLK), bf16),
            ((blocks, heads, 128), f32),
            ((tokens, 9 * heads), bf16, True),
            ((heads, tokens), f32, True),
        ],
        [
            pltpu.VMEM((tokens, 9 * heads), bf16),
            pltpu.VMEM((heads, tokens), f32),
            pltpu.VMEM((tokens, 128), f32),
            pltpu.VMEM((128, tokens), f32),
            pltpu.SemaphoreType.DMA((2,)),
        ],
    )

    pay, stream, first, pooled = call(
        stream_kernel,
        (chip_sum, other_sum, w_visual, embed, keys, ends),
        [
            ((heads, N + EXTRA, P_SIZE), f32),
            ((tokens, width), bf16, True),
            ((heads, N, P_SIZE), f32, True),
            ((tokens, 3 * CF), bf16, True),
        ],
        [
            pltpu.VMEM((tokens, width), bf16),
            pltpu.VMEM((heads, N, P_SIZE), f32),
            pltpu.VMEM((tokens, 3 * CF), bf16),
            pltpu.SemaphoreType.DMA((2, heads // 2 + 1)),
        ],
    )
    got = lax.all_to_all(pay, "ctx", 0, 0, axis_index_groups=groups, tiled=True)

    held = (input_map, output_map, frame_ids.reshape(1, tokens), row_sums, columns)
    held += (w_gate, pooled, first, stream)
    base, gain = call(
        within_kernel,
        (skip.reshape(1, heads),) + outside(held),
        [((tokens, width), f32, True), ((tokens, width), f32, True)],
        [pltpu.VMEM(array.shape, array.dtype) for array in held]
        + [
            pltpu.VMEM((tokens, width), f32),
            pltpu.VMEM((tokens, width), f32),
            pltpu.VMEM((blocks, BLK, BLK), f32),
            pltpu.SemaphoreType.DMA((len(held),)),
            pltpu.SemaphoreType.DMA((2, heads // 2)),
        ],
        specs=[SMEM] + [HBM] * len(held),
    )

    (total,) = call(total_kernel, (got,), [((shards // heads, N + EXTRA, P_SIZE), f32)])
    totals = lax.all_to_all(total, "ctx", 0, 0, axis_index_groups=peers, tiled=True)
    (sent,) = call(spread_kernel, (got, totals, place), [((heads, N, P_SIZE), f32)])
    incoming = lax.all_to_all(sent, "ctx", 0, 0, axis_index_groups=groups, tiled=True)

    gated, energy = call(
        carry_kernel,
        (incoming,) + outside((output_map, base, gain)),
        [((tokens, width), f32), ((1, tokens), f32)],
        [
            pltpu.VMEM((tokens, N), bf16),
            pltpu.VMEM((tokens, width), f32),
            pltpu.VMEM((tokens, width), f32),
            pltpu.VMEM((tokens, P_SIZE), f32),
            pltpu.SemaphoreType.DMA((2, heads // 2 + 1)),
        ],
        specs=[VMEM, HBM, HBM, HBM],
    )
    chip_energy = energy + swap(energy, "mp")
    other_energy = swap(chip_energy, "section")
    (out,) = call(
        norm_kernel,
        (gated, chip_energy, other_energy, norm_gain),
        [((tokens, width), bf16, True)],
        [pltpu.VMEM((tokens, width), bf16), pltpu.SemaphoreType.DMA((tokens // P_SIZE,))],
    )
    return out


def solution(mesh):
    return jax.shard_map(
        body,
        mesh=mesh,
        in_specs=(
            P("section", ("ctx", "mp"), None),
            P("section", ("ctx", "mp"), None),
            P("section", ("ctx", "mp"), None),
            P("ctx", ("section", "mp")),
            P(None, ("section", "mp")),
            P(None, ("section", "mp")),
            P("ctx", None),
            P("ctx", None),
            P("ctx", ("section", "mp")),
            P(("section", "mp")),
            P("ctx"),
            P(("section", "mp")),
        ),
        out_specs=P("ctx", ("section", "mp")),
        check_vma=False,
    )
```

```python
import math

import jax
import jax.numpy as jnp
from jax import lax
from jax.experimental import pallas as pl
from jax.experimental.pallas import tpu as pltpu
from jax.sharding import PartitionSpec as P

P_SIZE = 128
N = 128
BLK = 256
CF = 64
DI = 8192
EPSILON = 1e-05
LOG2E = math.log2(math.e)
CHUNK = 64
EXTRA = 8

f32 = jnp.float32
bf16 = jnp.bfloat16

VMEM = pl.BlockSpec(memory_space=pltpu.VMEM)
SMEM = pl.BlockSpec(memory_space=pltpu.SMEM)
HBM = pl.BlockSpec(memory_space=pltpu.HBM)
PARAMS = pltpu.CompilerParams(vmem_limit_bytes=24 * 1024 * 1024)


def terms(x, count):
    parts = []
    for _ in range(count - 1):
        part = x.astype(bf16)
        parts.append(part)
        x = x - part.astype(f32)
    parts.append(x.astype(bf16))
    return parts


def dot(a, b):
    return jnp.dot(a, b, preferred_element_type=f32)


def fetch(far, near, sems):
    copies = [pltpu.make_async_copy(f, n, sems.at[i]) for i, (f, n) in enumerate(zip(far, near))]
    for copy in copies:
        copy.start()
    return copies


def pool_kernel(*refs):
    count = (len(refs) - 4) // 2
    far, out_ref, near = refs[:count], refs[count], refs[count + 1 : 2 * count - 2]
    logits_ref, cells_ref, feats_ref, prob, hits, sems = refs[2 * count - 2 :]
    near = (logits_ref, cells_ref, feats_ref) + tuple(near)
    copies = [pltpu.make_async_copy(far[i], near[i], sems.at[i]) for i in range(count)]
    for copy in copies:
        copy.start()
    for copy in copies[:3]:
        copy.wait()
    bins, _, rows = logits_ref.shape
    logits = logits_ref[...]
    raised = jnp.exp(logits - jnp.max(logits, axis=0, keepdims=True))
    prob[...] = raised / jnp.sum(raised, axis=0, keepdims=True)

    def chunk(k, carry):
        first = pl.multiple_of(k * CHUNK, CHUNK)
        ids = lax.broadcasted_iota(jnp.int32, (CHUNK, rows), 0) + first
        acc = jnp.zeros((CHUNK, rows), f32)
        for d in range(bins):
            acc = acc + jnp.where(cells_ref[d] == ids, prob[d], 0.0)
        high, low = terms(acc, 2)
        hits[pl.ds(first, CHUNK), :rows] = high
        hits[pl.ds(first, CHUNK), rows:] = low
        return carry

    lax.fori_loop(0, hits.shape[0] // CHUNK, chunk, 0)
    feats = feats_ref[...]
    pooled = lax.dot_general(
        hits[...],
        jnp.concatenate([feats, feats], axis=1),
        (((1,), (1,)), ((), ())),
        preferred_element_type=f32,
    )
    half = pooled.shape[0] // 2
    out_ref[...] = jnp.concatenate([pooled[:half], pooled[half:]], axis=1)
    for copy in copies[3:]:
        copy.wait()


def decay_kernel(
    forget_ref, in_ref, keys_ref, ends_ref, columns_out, rows_out, columns_ref, rows_ref, wide, turned, sems
):
    heads = forget_ref.shape[0]
    blocks = keys_ref.shape[0]
    row_order = lax.broadcasted_iota(jnp.int32, (BLK, BLK), 0)
    col_order = lax.broadcasted_iota(jnp.int32, (BLK, BLK), 1)
    upper = jnp.where(row_order <= col_order, 1.0, 0.0).astype(bf16)
    for b in range(blocks):
        span = slice(b * BLK, (b + 1) * BLK)
        cum = sum(dot(part, upper) for part in terms(forget_ref[:, span], 3))
        turned[:heads, span] = cum
        end = cum[:, BLK - 1 :]
        rise = jnp.exp(cum - end)
        ends_ref[b] = jnp.broadcast_to(end, (heads, 128))
        write_t = in_ref[span, :].astype(f32).T
        for h in range(heads):
            keys_ref[b, h] = (write_t * rise[h : h + 1, :]).astype(bf16)
    rows_ref[...] = turned[:heads, :] * LOG2E
    wide[...] = turned[...].T
    before = jnp.zeros((1, heads), f32)
    for b in range(blocks):
        span = slice(b * BLK, (b + 1) * BLK)
        cum = wide[span, :heads]
        parts = terms(jnp.exp(-(cum + before)), 3) + terms(jnp.exp(-cum), 3) + terms(cum * LOG2E, 3)
        columns_ref[span, :] = jnp.concatenate(parts, axis=1)
        before = before + cum[BLK - 1 :, :]
    for copy in fetch((columns_ref, rows_ref), (columns_out, rows_out), sems):
        copy.wait()


def stream_kernel(
    mine_ref, other_ref, w_ref, embed_ref, keys_ref, ends_ref, pay_ref, *refs
):
    stream_out, first_out, pooled_out, stream_ref, first_ref, pooled_ref, sems = refs
    packed = mine_ref[...] + other_ref[...]
    pooled = jnp.concatenate([packed[:, :CF], packed[:, CF:]], axis=0)
    pooled_ref[...] = jnp.concatenate(terms(pooled, 3), axis=1)
    heads = first_ref.shape[0]
    saved = pltpu.make_async_copy(pooled_ref, pooled_out, sems.at[0, heads // 2])
    saved.start()

    def results(q):
        lanes = pl.ds(pl.multiple_of(q * 256, 256), 256)
        both = pl.ds(2 * q, 2)
        return (
            pltpu.make_async_copy(stream_ref.at[:, lanes], stream_out.at[:, lanes], sems.at[0, q]),
            pltpu.make_async_copy(first_ref.at[both], first_out.at[both], sems.at[1, q]),
        )

    def pair(q, carry):
        lanes = pl.ds(pl.multiple_of(q * 256, 256), 256)
        w = w_ref[:, lanes]
        visual = dot(pooled_ref[...], jnp.concatenate([w, w, w], axis=0))
        stream = (embed_ref[:, lanes].astype(f32) + visual).astype(bf16)
        stream_ref[:, lanes] = stream
        for j in range(2):
            h = 2 * q + j
            part = stream[:, j * P_SIZE : (j + 1) * P_SIZE]
            early = dot(keys_ref[0, h], part[:BLK])
            late = dot(keys_ref[1, h], part[BLK:])
            end_early = ends_ref[0, pl.ds(h, 1), :]
            end_late = ends_ref[1, pl.ds(h, 1), :]
            first_ref[h] = early
            pay_ref[h, :N, :] = jnp.exp(-end_late) * early + late
            pay_ref[h, N:, :] = jnp.broadcast_to(end_early + end_late, (EXTRA, P_SIZE))
        for copy in results(q):
            copy.start()
        return carry

    def finish(q, carry):
        for copy in results(q):
            copy.wait()
        return carry

    lax.fori_loop(0, heads // 2, pair, 0, unroll=2)
    lax.fori_loop(0, heads // 2, finish, 0)
    saved.wait()


def pick(heads, q):
    row = lax.broadcasted_iota(jnp.int32, (3 * heads, 2 * P_SIZE), 0)
    lane = lax.broadcasted_iota(jnp.int32, (3 * heads, 2 * P_SIZE), 1)
    h = 2 * q + jnp.where(lane < P_SIZE, 0, 1)
    hit = (row == h) | (row == h + heads) | (row == h + 2 * heads)
    return jnp.where(hit, 1.0, 0.0).astype(bf16)


def side_by_side(ref, q):
    parts = [jnp.concatenate(terms(ref[2 * q + j], 2), axis=0) for j in range(2)]
    return jnp.concatenate(parts, axis=1)


def within_kernel(skip_ref, *refs):
    far, (base_out, gain_out), near = refs[:9], refs[9:11], refs[11:20]
    base_ref, gain_ref, scored, in_sems, out_sems = refs[20:]
    copies = fetch(far, near, in_sems)
    in_ref, read_ref, frames_ref, rows_ref, columns_ref, w_ref, pooled_ref, first_ref, stream_ref = near
    heads = first_ref.shape[0]
    row_order = lax.broadcasted_iota(jnp.int32, (BLK, BLK), 0)
    col_order = lax.broadcasted_iota(jnp.int32, (BLK, BLK), 1)
    causal = col_order <= row_order
    for copy in copies[:3]:
        copy.wait()
    for b in range(scored.shape[0]):
        span = slice(b * BLK, (b + 1) * BLK)
        scores = lax.dot_general(
            read_ref[span, :], in_ref[span, :], (((1,), (1,)), ((), ())), preferred_element_type=f32
        )
        frame_row = frames_ref[:, span].astype(f32)
        frame_col = jnp.broadcast_to(frame_row, (128, BLK)).T
        same = jnp.concatenate([frame_col, frame_col], axis=1) == frame_row
        scored[b] = jnp.where(causal | same, scores, 0.0)
    for copy in copies[3:]:
        copy.wait()
    read = read_ref[BLK:, :]
    read_twice = jnp.concatenate([read, read], axis=1)
    late_rows = slice(BLK, 2 * BLK)

    def results(q):
        lanes = pl.ds(pl.multiple_of(q * 2 * P_SIZE, 2 * P_SIZE), 2 * P_SIZE)
        return (
            pltpu.make_async_copy(base_ref.at[:, lanes], base_out.at[:, lanes], out_sems.at[0, q]),
            pltpu.make_async_copy(gain_ref.at[:, lanes], gain_out.at[:, lanes], out_sems.at[1, q]),
        )

    def pair(q, carry):
        lanes = pl.ds(pl.multiple_of(q * 2 * P_SIZE, 2 * P_SIZE), 2 * P_SIZE)
        w = w_ref[:, lanes]
        gate = dot(pooled_ref[...], jnp.concatenate([w, w, w], axis=0))
        silu = gate / (1.0 + jnp.exp(-gate))
        chosen = pick(heads, q)
        gain_ref[:, lanes] = silu * dot(columns_ref[:, : 3 * heads], chosen)
        cum_col = dot(columns_ref[:, 6 * heads :], chosen)
        stream = stream_ref[:, lanes]
        mixed = [[], []]
        for j in range(2):
            h = 2 * q + j
            cum_row = rows_ref[pl.ds(h, 1), :]
            side = slice(j * P_SIZE, (j + 1) * P_SIZE)
            for b in range(2):
                span = slice(b * BLK, (b + 1) * BLK)
                column = cum_col[span, side]
                distance = jnp.abs(jnp.concatenate([column, column], axis=1) - cum_row[:, span])
                weights = (scored[b] * jnp.exp2(-distance)).astype(bf16)
                part = stream[span, side]
                mixed[b].append(dot(weights, part) + skip_ref[0, h] * part.astype(f32))
        own = dot(columns_ref[late_rows, 3 * heads : 6 * heads], chosen)
        carried = own * dot(read_twice, side_by_side(first_ref, q))
        base_ref[:BLK, lanes] = jnp.concatenate(mixed[0], axis=1) * silu[:BLK]
        base_ref[BLK:, lanes] = (jnp.concatenate(mixed[1], axis=1) + carried) * silu[BLK:]
        for copy in results(q):
            copy.start()
        return carry

    def finish(q, carry):
        for copy in results(q):
            copy.wait()
        return carry

    lax.fori_loop(0, heads // 2, pair, 0)
    lax.fori_loop(0, heads // 2, finish, 0)


def total_kernel(got_ref, total_ref):
    state = got_ref[0, :N, :]
    log = got_ref[0, N:, :]
    for i in range(1, got_ref.shape[0]):
        gone = got_ref[i, N:, :]
        state = jnp.exp(-gone[:1]) * state + got_ref[i, :N, :]
        log = log + gone
    for k in range(total_ref.shape[0]):
        total_ref[k, :N, :] = state
        total_ref[k, N:, :] = log


def spread_kernel(got_ref, totals_ref, place_ref, out_ref):
    place = place_ref[...]
    state = jnp.zeros(out_ref.shape[1:], f32)
    for k in range(totals_ref.shape[0] - 1):
        later = jnp.exp(-totals_ref[k, N : N + 1, :]) * state + totals_ref[k, :N, :]
        state = jnp.where(jnp.broadcast_to(place, state.shape) > k, later, state)
    for i in range(got_ref.shape[0]):
        out_ref[i] = state
        state = jnp.exp(-got_ref[i, N : N + 1, :]) * state + got_ref[i, :N, :]


def carry_kernel(state_ref, read_ref, base_ref, gain_far, gated_ref, energy_ref, gain_ref, acc, sems):
    heads = state_ref.shape[0]

    def gains(q):
        lanes = pl.ds(pl.multiple_of(q * 2 * P_SIZE, 2 * P_SIZE), 2 * P_SIZE)
        return pltpu.make_async_copy(gain_far.at[:, lanes], gain_ref.at[:, lanes], sems.at[q])

    for q in range(heads // 2):
        gains(q).start()
    read = read_ref[...]
    read_twice = jnp.concatenate([read, read], axis=1)
    acc[...] = jnp.zeros_like(acc)

    def pair(q, carry):
        lanes = pl.ds(pl.multiple_of(q * 2 * P_SIZE, 2 * P_SIZE), 2 * P_SIZE)
        carried = dot(read_twice, side_by_side(state_ref, q))
        gains(q).wait()
        gated = base_ref[:, lanes] + gain_ref[:, lanes] * carried
        gated_ref[:, lanes] = gated
        squares = gated * gated
        acc[...] += squares[:, :P_SIZE] + squares[:, P_SIZE:]
        return carry

    lax.fori_loop(0, heads // 2, pair, 0)
    energy_ref[...] = jnp.sum(acc[...].T, axis=0, keepdims=True)


def norm_kernel(gated_ref, mine_ref, other_ref, gain_ref, out_ref, held, sems):
    inverse = lax.rsqrt((mine_ref[...] + other_ref[...]) / DI + EPSILON)
    copies = []
    for k in range(held.shape[0] // P_SIZE):
        rows = slice(k * P_SIZE, (k + 1) * P_SIZE)
        column = jnp.broadcast_to(inverse[:, rows], (P_SIZE, P_SIZE)).T

        def head(h, carry):
            lanes = pl.ds(pl.multiple_of(h * P_SIZE, P_SIZE), P_SIZE)
            held[rows, lanes] = (gated_ref[rows, lanes] * column * gain_ref[:, lanes]).astype(bf16)
            return carry

        lax.fori_loop(0, held.shape[1] // P_SIZE, head, 0, unroll=4)
        copies.append(pltpu.make_async_copy(held.at[rows], out_ref.at[rows], sems.at[k]))
        copies[-1].start()
    for copy in copies:
        copy.wait()


def outside(arrays):
    return tuple(pltpu.with_memory_space_constraint(array, pltpu.HBM) for array in arrays)


def call(kernel, ins, outs, scratch=(), specs=None):
    return pl.pallas_call(
        kernel,
        out_shape=[
            pltpu.HBM(*out[:2]) if out[2:] else jax.ShapeDtypeStruct(*out) for out in outs
        ],
        in_specs=specs or [VMEM] * len(ins),
        out_specs=[HBM if out[2:] else VMEM for out in outs],
        scratch_shapes=list(scratch),
        compiler_params=PARAMS,
    )(*ins)


def swap(value, axis):
    return lax.ppermute(value, axis, [(0, 1), (1, 0)])


def body(
    depth_logits,
    features,
    cell_index,
    embed,
    w_visual,
    w_gate,
    input_map,
    output_map,
    forget,
    skip,
    frame_ids,
    norm_gain,
):
    tokens, width = embed.shape
    heads = forget.shape[1]
    blocks = tokens // BLK
    pixels, bins = depth_logits.shape[1:]
    shards = lax.axis_size("ctx")
    groups = [list(range(g, g + heads)) for g in range(0, shards, heads)]
    peers = [list(range(g, shards, heads)) for g in range(heads)]
    place = jnp.full((1, P_SIZE), lax.axis_index("ctx") // heads, jnp.int32)

    near = (depth_logits.transpose(2, 0, 1), cell_index.transpose(2, 0, 1), features[0].T)
    far = (forget.T, input_map, w_visual, embed, norm_gain.reshape(1, width))
    partial_sum, forget_t, writes, w_visual, embed, norm_gain = call(
        pool_kernel,
        outside(near + far),
        [((tokens // 2, 2 * CF), f32)] + [(array.shape, array.dtype) for array in far],
        [
            pltpu.VMEM((bins, 1, pixels), f32),
            pltpu.VMEM((bins, 1, pixels), jnp.int32),
            pltpu.VMEM((CF, pixels), bf16),
            pltpu.VMEM((bins, 1, pixels), f32),
            pltpu.VMEM((tokens, 2 * pixels), bf16),
            pltpu.SemaphoreType.DMA((len(near + far),)),
        ],
        specs=[HBM] * len(near + far),
    )
    chip_sum = partial_sum + swap(partial_sum, "mp")
    other_sum = swap(chip_sum, "section")

    keys, ends, columns, row_sums = call(
        decay_kernel,
        (forget_t, writes),
        [
            ((blocks, heads, N, BLK), bf16),
            ((blocks, heads, 128), f32),
            ((tokens, 9 * heads), bf16, True),
            ((heads, tokens), f32, True),
        ],
        [
            pltpu.VMEM((tokens, 9 * heads), bf16),
            pltpu.VMEM((heads, tokens), f32),
            pltpu.VMEM((tokens, 128), f32),
            pltpu.VMEM((128, tokens), f32),
            pltpu.SemaphoreType.DMA((2,)),
        ],
    )

    pay, stream, first, pooled = call(
        stream_kernel,
        (chip_sum, other_sum, w_visual, embed, keys, ends),
        [
            ((heads, N + EXTRA, P_SIZE), f32),
            ((tokens, width), bf16, True),
            ((heads, N, P_SIZE), f32, True),
            ((tokens, 3 * CF), bf16, True),
        ],
        [
            pltpu.VMEM((tokens, width), bf16),
            pltpu.VMEM((heads, N, P_SIZE), f32),
            pltpu.VMEM((tokens, 3 * CF), bf16),
            pltpu.SemaphoreType.DMA((2, heads // 2 + 1)),
        ],
    )
    got = lax.all_to_all(pay, "ctx", 0, 0, axis_index_groups=groups, tiled=True)

    held = (input_map, output_map, frame_ids.reshape(1, tokens), row_sums, columns)
    held += (w_gate, pooled, first, stream)
    base, gain = call(
        within_kernel,
        (skip.reshape(1, heads),) + outside(held),
        [((tokens, width), f32, True), ((tokens, width), f32, True)],
        [pltpu.VMEM(array.shape, array.dtype) for array in held]
        + [
            pltpu.VMEM((tokens, width), f32),
            pltpu.VMEM((tokens, width), f32),
            pltpu.VMEM((blocks, BLK, BLK), f32),
            pltpu.SemaphoreType.DMA((len(held),)),
            pltpu.SemaphoreType.DMA((2, heads // 2)),
        ],
        specs=[SMEM] + [HBM] * len(held),
    )

    got, base, gain = lax.optimization_barrier((got, base, gain))
    (total,) = call(total_kernel, (got,), [((shards // heads, N + EXTRA, P_SIZE), f32)])
    totals = lax.all_to_all(total, "ctx", 0, 0, axis_index_groups=peers, tiled=True)
    (sent,) = call(spread_kernel, (got, totals, place), [((heads, N, P_SIZE), f32)])
    incoming = lax.all_to_all(sent, "ctx", 0, 0, axis_index_groups=groups, tiled=True)

    gated, energy = call(
        carry_kernel,
        (incoming, output_map, base) + outside((gain,)),
        [((tokens, width), f32), ((1, tokens), f32)],
        [
            pltpu.VMEM((tokens, width), f32),
            pltpu.VMEM((tokens, P_SIZE), f32),
            pltpu.SemaphoreType.DMA((heads // 2,)),
        ],
        specs=[VMEM] * 3 + [HBM],
    )
    chip_energy = energy + swap(energy, "mp")
    other_energy = swap(chip_energy, "section")
    (out,) = call(
        norm_kernel,
        (gated, chip_energy, other_energy, norm_gain),
        [((tokens, width), bf16, True)],
        [pltpu.VMEM((tokens, width), bf16), pltpu.SemaphoreType.DMA((tokens // P_SIZE,))],
    )
    return out


def solution(mesh):
    return jax.shard_map(
        body,
        mesh=mesh,
        in_specs=(
            P("section", ("ctx", "mp"), None),
            P("section", ("ctx", "mp"), None),
            P("section", ("ctx", "mp"), None),
            P("ctx", ("section", "mp")),
            P(None, ("section", "mp")),
            P(None, ("section", "mp")),
            P("ctx", None),
            P("ctx", None),
            P("ctx", ("section", "mp")),
            P(("section", "mp")),
            P("ctx"),
            P(("section", "mp")),
        ),
        out_specs=P("ctx", ("section", "mp")),
        check_vma=False,
    )
```

```python
import math

import jax
import jax.numpy as jnp
from jax import lax
from jax.experimental import pallas as pl
from jax.experimental.pallas import tpu as pltpu
from jax.sharding import PartitionSpec as P

P_SIZE = 128
N = 128
BLK = 256
CF = 64
DI = 8192
EPSILON = 1e-05
LOG2E = math.log2(math.e)
CHUNK = 64
EXTRA = 8

f32 = jnp.float32
bf16 = jnp.bfloat16

VMEM = pl.BlockSpec(memory_space=pltpu.VMEM)
SMEM = pl.BlockSpec(memory_space=pltpu.SMEM)
HBM = pl.BlockSpec(memory_space=pltpu.HBM)
PARAMS = pltpu.CompilerParams(vmem_limit_bytes=24 * 1024 * 1024)


def terms(x, count):
    parts = []
    for _ in range(count - 1):
        part = x.astype(bf16)
        parts.append(part)
        x = x - part.astype(f32)
    parts.append(x.astype(bf16))
    return parts


def dot(a, b):
    return jnp.dot(a, b, preferred_element_type=f32)


def fetch(far, near, sems):
    copies = [pltpu.make_async_copy(f, n, sems.at[i]) for i, (f, n) in enumerate(zip(far, near))]
    for copy in copies:
        copy.start()
    return copies


def pool_kernel(*refs):
    count = (len(refs) - 4) // 2
    far, out_ref, near = refs[:count], refs[count], refs[count + 1 : 2 * count - 2]
    logits_ref, cells_ref, feats_ref, prob, hits, sems = refs[2 * count - 2 :]
    near = (logits_ref, cells_ref, feats_ref) + tuple(near)
    copies = [pltpu.make_async_copy(far[i], near[i], sems.at[i]) for i in range(count)]
    for copy in copies:
        copy.start()
    for copy in copies[:3]:
        copy.wait()
    bins, _, rows = logits_ref.shape
    logits = logits_ref[...]
    raised = jnp.exp(logits - jnp.max(logits, axis=0, keepdims=True))
    prob[...] = raised / jnp.sum(raised, axis=0, keepdims=True)

    def chunk(k, carry):
        first = pl.multiple_of(k * CHUNK, CHUNK)
        ids = lax.broadcasted_iota(jnp.int32, (CHUNK, rows), 0) + first
        acc = jnp.zeros((CHUNK, rows), f32)
        for d in range(bins):
            acc = acc + jnp.where(cells_ref[d] == ids, prob[d], 0.0)
        high, low = terms(acc, 2)
        hits[pl.ds(first, CHUNK), :rows] = high
        hits[pl.ds(first, CHUNK), rows:] = low
        return carry

    lax.fori_loop(0, hits.shape[0] // CHUNK, chunk, 0)
    feats = feats_ref[...]
    pooled = lax.dot_general(
        hits[...],
        jnp.concatenate([feats, feats], axis=1),
        (((1,), (1,)), ((), ())),
        preferred_element_type=f32,
    )
    half = pooled.shape[0] // 2
    out_ref[...] = jnp.concatenate([pooled[:half], pooled[half:]], axis=1)
    for copy in copies[3:]:
        copy.wait()


def decay_kernel(
    forget_ref, in_ref, keys_ref, ends_ref, columns_out, rows_out, early_out, columns_ref, rows_ref, wide, turned, sems
):
    heads = forget_ref.shape[0]
    blocks = keys_ref.shape[0]
    row_order = lax.broadcasted_iota(jnp.int32, (BLK, BLK), 0)
    col_order = lax.broadcasted_iota(jnp.int32, (BLK, BLK), 1)
    upper = jnp.where(row_order <= col_order, 1.0, 0.0).astype(bf16)
    for b in range(blocks):
        span = slice(b * BLK, (b + 1) * BLK)
        cum = sum(dot(part, upper) for part in terms(forget_ref[:, span], 3))
        turned[:heads, span] = cum
        end = cum[:, BLK - 1 :]
        rise = jnp.exp(cum - end)
        ends_ref[b] = jnp.broadcast_to(end, (heads, 128))
        write_t = in_ref[span, :].astype(f32).T
        for h in range(heads):
            keys_ref[b, h] = (write_t * rise[h : h + 1, :]).astype(bf16)
        if b == 0:
            early = pltpu.make_async_copy(keys_ref.at[0], early_out, sems.at[2])
            early.start()
    rows_ref[...] = turned[:heads, :] * LOG2E
    wide[...] = turned[...].T
    before = jnp.zeros((1, heads), f32)
    for b in range(blocks):
        span = slice(b * BLK, (b + 1) * BLK)
        cum = wide[span, :heads]
        parts = terms(jnp.exp(-(cum + before)), 3) + terms(jnp.exp(-cum), 3) + terms(cum * LOG2E, 3)
        columns_ref[span, :] = jnp.concatenate(parts, axis=1)
        before = before + cum[BLK - 1 :, :]
    for copy in fetch((columns_ref, rows_ref), (columns_out, rows_out), sems):
        copy.wait()
    early.wait()


def stream_kernel(
    mine_ref, other_ref, w_ref, embed_ref, keys_ref, ends_ref, pay_ref, stream_out, pooled_out, stream_ref, pooled_ref, sems
):
    packed = mine_ref[...] + other_ref[...]
    pooled = jnp.concatenate([packed[:, :CF], packed[:, CF:]], axis=0)
    pooled_ref[...] = jnp.concatenate(terms(pooled, 3), axis=1)
    heads = pay_ref.shape[0]
    saved = pltpu.make_async_copy(pooled_ref, pooled_out, sems.at[heads // 2])
    saved.start()

    def result(q):
        lanes = pl.ds(pl.multiple_of(q * 256, 256), 256)
        return pltpu.make_async_copy(stream_ref.at[:, lanes], stream_out.at[:, lanes], sems.at[q])

    def pair(q, carry):
        lanes = pl.ds(pl.multiple_of(q * 256, 256), 256)
        w = w_ref[:, lanes]
        visual = dot(pooled_ref[...], jnp.concatenate([w, w, w], axis=0))
        stream_ref[:, lanes] = (embed_ref[:, lanes].astype(f32) + visual).astype(bf16)
        result(q).start()
        return carry

    def states(q, carry):
        stream = stream_ref[:, pl.ds(pl.multiple_of(q * 256, 256), 256)]
        for j in range(2):
            h = 2 * q + j
            part = stream[:, j * P_SIZE : (j + 1) * P_SIZE]
            early = dot(keys_ref[0, h], part[:BLK])
            late = dot(keys_ref[1, h], part[BLK:])
            end_early = ends_ref[0, pl.ds(h, 1), :]
            end_late = ends_ref[1, pl.ds(h, 1), :]
            pay_ref[h, :N, :] = jnp.exp(-end_late) * early + late
            pay_ref[h, N:, :] = jnp.broadcast_to(end_early + end_late, (EXTRA, P_SIZE))
        return carry

    def finish(q, carry):
        result(q).wait()
        return carry

    lax.fori_loop(0, heads // 2, pair, 0, unroll=2)
    lax.fori_loop(0, heads // 2, states, 0, unroll=2)
    lax.fori_loop(0, heads // 2, finish, 0)
    saved.wait()


def pick(heads, q):
    row = lax.broadcasted_iota(jnp.int32, (3 * heads, 2 * P_SIZE), 0)
    lane = lax.broadcasted_iota(jnp.int32, (3 * heads, 2 * P_SIZE), 1)
    h = 2 * q + jnp.where(lane < P_SIZE, 0, 1)
    hit = (row == h) | (row == h + heads) | (row == h + 2 * heads)
    return jnp.where(hit, 1.0, 0.0).astype(bf16)


def side_by_side(states):
    return jnp.concatenate([jnp.concatenate(terms(state, 2), axis=0) for state in states], axis=1)


def within_kernel(skip_ref, *refs):
    far, (base_out, gain_out), near = refs[:9], refs[9:11], refs[11:20]
    base_ref, gain_ref, scored, in_sems, out_sems = refs[20:]
    copies = fetch(far, near, in_sems)
    in_ref, read_ref, frames_ref, rows_ref, columns_ref, w_ref, pooled_ref, keys_ref, stream_ref = near
    heads = keys_ref.shape[0]
    row_order = lax.broadcasted_iota(jnp.int32, (BLK, BLK), 0)
    col_order = lax.broadcasted_iota(jnp.int32, (BLK, BLK), 1)
    causal = col_order <= row_order
    for copy in copies[:3]:
        copy.wait()
    for b in range(scored.shape[0]):
        span = slice(b * BLK, (b + 1) * BLK)
        scores = lax.dot_general(
            read_ref[span, :], in_ref[span, :], (((1,), (1,)), ((), ())), preferred_element_type=f32
        )
        frame_row = frames_ref[:, span].astype(f32)
        frame_col = jnp.broadcast_to(frame_row, (128, BLK)).T
        same = jnp.concatenate([frame_col, frame_col], axis=1) == frame_row
        scored[b] = jnp.where(causal | same, scores, 0.0)
    for copy in copies[3:]:
        copy.wait()
    read = read_ref[BLK:, :]
    read_twice = jnp.concatenate([read, read], axis=1)
    late_rows = slice(BLK, 2 * BLK)

    def results(q):
        lanes = pl.ds(pl.multiple_of(q * 2 * P_SIZE, 2 * P_SIZE), 2 * P_SIZE)
        return (
            pltpu.make_async_copy(base_ref.at[:, lanes], base_out.at[:, lanes], out_sems.at[0, q]),
            pltpu.make_async_copy(gain_ref.at[:, lanes], gain_out.at[:, lanes], out_sems.at[1, q]),
        )

    def pair(q, carry):
        lanes = pl.ds(pl.multiple_of(q * 2 * P_SIZE, 2 * P_SIZE), 2 * P_SIZE)
        w = w_ref[:, lanes]
        gate = dot(pooled_ref[...], jnp.concatenate([w, w, w], axis=0))
        silu = gate / (1.0 + jnp.exp(-gate))
        chosen = pick(heads, q)
        gain_ref[:, lanes] = silu * dot(columns_ref[:, : 3 * heads], chosen)
        cum_col = dot(columns_ref[:, 6 * heads :], chosen)
        stream = stream_ref[:, lanes]
        mixed = [[], []]
        for j in range(2):
            h = 2 * q + j
            cum_row = rows_ref[pl.ds(h, 1), :]
            side = slice(j * P_SIZE, (j + 1) * P_SIZE)
            for b in range(2):
                span = slice(b * BLK, (b + 1) * BLK)
                column = cum_col[span, side]
                distance = jnp.abs(jnp.concatenate([column, column], axis=1) - cum_row[:, span])
                weights = (scored[b] * jnp.exp2(-distance)).astype(bf16)
                part = stream[span, side]
                mixed[b].append(dot(weights, part) + skip_ref[0, h] * part.astype(f32))
        own = dot(columns_ref[late_rows, 3 * heads : 6 * heads], chosen)
        first = [
            dot(keys_ref[2 * q + j], stream[:BLK, j * P_SIZE : (j + 1) * P_SIZE]) for j in range(2)
        ]
        carried = own * dot(read_twice, side_by_side(first))
        base_ref[:BLK, lanes] = jnp.concatenate(mixed[0], axis=1) * silu[:BLK]
        base_ref[BLK:, lanes] = (jnp.concatenate(mixed[1], axis=1) + carried) * silu[BLK:]
        for copy in results(q):
            copy.start()
        return carry

    def finish(q, carry):
        for copy in results(q):
            copy.wait()
        return carry

    lax.fori_loop(0, heads // 2, pair, 0)
    lax.fori_loop(0, heads // 2, finish, 0)


def total_kernel(got_ref, total_ref):
    state = got_ref[0, :N, :]
    log = got_ref[0, N:, :]
    for i in range(1, got_ref.shape[0]):
        gone = got_ref[i, N:, :]
        state = jnp.exp(-gone[:1]) * state + got_ref[i, :N, :]
        log = log + gone
    for k in range(total_ref.shape[0]):
        total_ref[k, :N, :] = state
        total_ref[k, N:, :] = log


def spread_kernel(got_ref, totals_ref, place_ref, out_ref):
    place = place_ref[...]
    state = jnp.zeros(out_ref.shape[1:], f32)
    for k in range(totals_ref.shape[0] - 1):
        later = jnp.exp(-totals_ref[k, N : N + 1, :]) * state + totals_ref[k, :N, :]
        state = jnp.where(jnp.broadcast_to(place, state.shape) > k, later, state)
    for i in range(got_ref.shape[0]):
        out_ref[i] = state
        state = jnp.exp(-got_ref[i, N : N + 1, :]) * state + got_ref[i, :N, :]


def carry_kernel(state_ref, read_far, base_far, gain_far, gated_ref, energy_ref, read_ref, base_ref, gain_ref, acc, sems):
    heads = state_ref.shape[0]

    def operands(q):
        lanes = pl.ds(pl.multiple_of(q * 2 * P_SIZE, 2 * P_SIZE), 2 * P_SIZE)
        return (
            pltpu.make_async_copy(base_far.at[:, lanes], base_ref.at[:, lanes], sems.at[0, q]),
            pltpu.make_async_copy(gain_far.at[:, lanes], gain_ref.at[:, lanes], sems.at[1, q]),
        )

    first = pltpu.make_async_copy(read_far, read_ref, sems.at[0, heads // 2])
    first.start()
    for q in range(heads // 2):
        for copy in operands(q):
            copy.start()
    acc[...] = jnp.zeros_like(acc)
    first.wait()
    read = read_ref[...]
    read_twice = jnp.concatenate([read, read], axis=1)

    def pair(q, carry):
        lanes = pl.ds(pl.multiple_of(q * 2 * P_SIZE, 2 * P_SIZE), 2 * P_SIZE)
        carried = dot(read_twice, side_by_side([state_ref[2 * q], state_ref[2 * q + 1]]))
        for copy in operands(q):
            copy.wait()
        gated = base_ref[:, lanes] + gain_ref[:, lanes] * carried
        gated_ref[:, lanes] = gated
        squares = gated * gated
        acc[...] += squares[:, :P_SIZE] + squares[:, P_SIZE:]
        return carry

    lax.fori_loop(0, heads // 2, pair, 0)
    energy_ref[...] = jnp.sum(acc[...].T, axis=0, keepdims=True)


def norm_kernel(gated_ref, mine_ref, other_ref, gain_ref, out_ref, held, sems):
    inverse = lax.rsqrt((mine_ref[...] + other_ref[...]) / DI + EPSILON)
    copies = []
    for k in range(held.shape[0] // P_SIZE):
        rows = slice(k * P_SIZE, (k + 1) * P_SIZE)
        column = jnp.broadcast_to(inverse[:, rows], (P_SIZE, P_SIZE)).T

        def head(h, carry):
            lanes = pl.ds(pl.multiple_of(h * P_SIZE, P_SIZE), P_SIZE)
            held[rows, lanes] = (gated_ref[rows, lanes] * column * gain_ref[:, lanes]).astype(bf16)
            return carry

        lax.fori_loop(0, held.shape[1] // P_SIZE, head, 0, unroll=4)
        copies.append(pltpu.make_async_copy(held.at[rows], out_ref.at[rows], sems.at[k]))
        copies[-1].start()
    for copy in copies:
        copy.wait()


def outside(arrays):
    return tuple(pltpu.with_memory_space_constraint(array, pltpu.HBM) for array in arrays)


def call(kernel, ins, outs, scratch=(), specs=None):
    return pl.pallas_call(
        kernel,
        out_shape=[
            pltpu.HBM(*out[:2]) if out[2:] else jax.ShapeDtypeStruct(*out) for out in outs
        ],
        in_specs=specs or [VMEM] * len(ins),
        out_specs=[HBM if out[2:] else VMEM for out in outs],
        scratch_shapes=list(scratch),
        compiler_params=PARAMS,
    )(*ins)


def swap(value, axis):
    return lax.ppermute(value, axis, [(0, 1), (1, 0)])


def body(
    depth_logits,
    features,
    cell_index,
    embed,
    w_visual,
    w_gate,
    input_map,
    output_map,
    forget,
    skip,
    frame_ids,
    norm_gain,
):
    tokens, width = embed.shape
    heads = forget.shape[1]
    blocks = tokens // BLK
    pixels, bins = depth_logits.shape[1:]
    shards = lax.axis_size("ctx")
    groups = [list(range(g, g + heads)) for g in range(0, shards, heads)]
    peers = [list(range(g, shards, heads)) for g in range(heads)]
    place = jnp.full((1, P_SIZE), lax.axis_index("ctx") // heads, jnp.int32)

    near = (depth_logits.transpose(2, 0, 1), cell_index.transpose(2, 0, 1), features[0].T)
    far = (forget.T, input_map, w_visual, embed, norm_gain.reshape(1, width))
    partial_sum, forget_t, writes, w_visual, embed, norm_gain = call(
        pool_kernel,
        outside(near + far),
        [((tokens // 2, 2 * CF), f32)] + [(array.shape, array.dtype) for array in far],
        [
            pltpu.VMEM((bins, 1, pixels), f32),
            pltpu.VMEM((bins, 1, pixels), jnp.int32),
            pltpu.VMEM((CF, pixels), bf16),
            pltpu.VMEM((bins, 1, pixels), f32),
            pltpu.VMEM((tokens, 2 * pixels), bf16),
            pltpu.SemaphoreType.DMA((len(near + far),)),
        ],
        specs=[HBM] * len(near + far),
    )
    partial_sum, place = lax.optimization_barrier((partial_sum, place))
    chip_sum = partial_sum + swap(partial_sum, "mp")
    other_sum = swap(chip_sum, "section")

    keys, ends, columns, row_sums, early_keys = call(
        decay_kernel,
        (forget_t, writes),
        [
            ((blocks, heads, N, BLK), bf16),
            ((blocks, heads, 128), f32),
            ((tokens, 9 * heads), bf16, True),
            ((heads, tokens), f32, True),
            ((heads, N, BLK), bf16, True),
        ],
        [
            pltpu.VMEM((tokens, 9 * heads), bf16),
            pltpu.VMEM((heads, tokens), f32),
            pltpu.VMEM((tokens, 128), f32),
            pltpu.VMEM((128, tokens), f32),
            pltpu.SemaphoreType.DMA((3,)),
        ],
    )

    pay, stream, pooled = call(
        stream_kernel,
        (chip_sum, other_sum, w_visual, embed, keys, ends),
        [
            ((heads, N + EXTRA, P_SIZE), f32),
            ((tokens, width), bf16, True),
            ((tokens, 3 * CF), bf16, True),
        ],
        [
            pltpu.VMEM((tokens, width), bf16),
            pltpu.VMEM((tokens, 3 * CF), bf16),
            pltpu.SemaphoreType.DMA((heads // 2 + 1,)),
        ],
    )
    got = lax.all_to_all(pay, "ctx", 0, 0, axis_index_groups=groups, tiled=True)

    held = (input_map, output_map, frame_ids.reshape(1, tokens), row_sums, columns)
    held += (w_gate, pooled, early_keys, stream)
    base, gain = call(
        within_kernel,
        (skip.reshape(1, heads),) + outside(held),
        [((tokens, width), f32, True), ((tokens, width), f32, True)],
        [pltpu.VMEM(array.shape, array.dtype) for array in held]
        + [
            pltpu.VMEM((tokens, width), f32),
            pltpu.VMEM((tokens, width), f32),
            pltpu.VMEM((blocks, BLK, BLK), f32),
            pltpu.SemaphoreType.DMA((len(held),)),
            pltpu.SemaphoreType.DMA((2, heads // 2)),
        ],
        specs=[SMEM] + [HBM] * len(held),
    )

    (total,) = call(total_kernel, (got,), [((shards // heads, N + EXTRA, P_SIZE), f32)])
    totals = lax.all_to_all(total, "ctx", 0, 0, axis_index_groups=peers, tiled=True)
    (sent,) = call(spread_kernel, (got, totals, place), [((heads, N, P_SIZE), f32)])
    incoming = lax.all_to_all(sent, "ctx", 0, 0, axis_index_groups=groups, tiled=True)

    gated, energy = call(
        carry_kernel,
        (incoming,) + outside((output_map, base, gain)),
        [((tokens, width), f32), ((1, tokens), f32)],
        [
            pltpu.VMEM((tokens, N), bf16),
            pltpu.VMEM((tokens, width), f32),
            pltpu.VMEM((tokens, width), f32),
            pltpu.VMEM((tokens, P_SIZE), f32),
            pltpu.SemaphoreType.DMA((2, heads // 2 + 1)),
        ],
        specs=[VMEM, HBM, HBM, HBM],
    )
    chip_energy = energy + swap(energy, "mp")
    other_energy = swap(chip_energy, "section")
    (out,) = call(
        norm_kernel,
        (gated, chip_energy, other_energy, norm_gain),
        [((tokens, width), bf16, True)],
        [pltpu.VMEM((tokens, width), bf16), pltpu.SemaphoreType.DMA((tokens // P_SIZE,))],
    )
    return out


def solution(mesh):
    return jax.shard_map(
        body,
        mesh=mesh,
        in_specs=(
            P("section", ("ctx", "mp"), None),
            P("section", ("ctx", "mp"), None),
            P("section", ("ctx", "mp"), None),
            P("ctx", ("section", "mp")),
            P(None, ("section", "mp")),
            P(None, ("section", "mp")),
            P("ctx", None),
            P("ctx", None),
            P("ctx", ("section", "mp")),
            P(("section", "mp")),
            P("ctx"),
            P(("section", "mp")),
        ),
        out_specs=P("ctx", ("section", "mp")),
        check_vma=False,
    )
```

```python
import math

import jax
import jax.numpy as jnp
from jax import lax
from jax.experimental import pallas as pl
from jax.experimental.pallas import tpu as pltpu
from jax.sharding import PartitionSpec as P

P_SIZE = 128
N = 128
BLK = 256
CF = 64
DI = 8192
EPSILON = 1e-05
LOG2E = math.log2(math.e)
CHUNK = 64
EXTRA = 8

f32 = jnp.float32
bf16 = jnp.bfloat16

VMEM = pl.BlockSpec(memory_space=pltpu.VMEM)
SMEM = pl.BlockSpec(memory_space=pltpu.SMEM)
HBM = pl.BlockSpec(memory_space=pltpu.HBM)
PARAMS = pltpu.CompilerParams(vmem_limit_bytes=24 * 1024 * 1024)


def terms(x, count):
    parts = []
    for _ in range(count - 1):
        part = x.astype(bf16)
        parts.append(part)
        x = x - part.astype(f32)
    parts.append(x.astype(bf16))
    return parts


def dot(a, b):
    return jnp.dot(a, b, preferred_element_type=f32)


def fetch(far, near, sems):
    copies = [pltpu.make_async_copy(f, n, sems.at[i]) for i, (f, n) in enumerate(zip(far, near))]
    for copy in copies:
        copy.start()
    return copies


def pool_kernel(*refs):
    count = (len(refs) - 4) // 2
    far, out_ref, near = refs[:count], refs[count], refs[count + 1 : 2 * count - 2]
    logits_ref, cells_ref, feats_ref, prob, hits, sems = refs[2 * count - 2 :]
    near = (logits_ref, cells_ref, feats_ref) + tuple(near)
    copies = [pltpu.make_async_copy(far[i], near[i], sems.at[i]) for i in range(count)]
    for copy in copies:
        copy.start()
    for copy in copies[:3]:
        copy.wait()
    bins, _, rows = logits_ref.shape
    logits = logits_ref[...]
    raised = jnp.exp(logits - jnp.max(logits, axis=0, keepdims=True))
    prob[...] = raised / jnp.sum(raised, axis=0, keepdims=True)

    def chunk(k, carry):
        first = pl.multiple_of(k * CHUNK, CHUNK)
        ids = lax.broadcasted_iota(jnp.int32, (CHUNK, rows), 0) + first
        acc = jnp.zeros((CHUNK, rows), f32)
        for d in range(bins):
            acc = acc + jnp.where(cells_ref[d] == ids, prob[d], 0.0)
        high, low = terms(acc, 2)
        hits[pl.ds(first, CHUNK), :rows] = high
        hits[pl.ds(first, CHUNK), rows:] = low
        return carry

    lax.fori_loop(0, hits.shape[0] // CHUNK, chunk, 0)
    feats = feats_ref[...]
    pooled = lax.dot_general(
        hits[...],
        jnp.concatenate([feats, feats], axis=1),
        (((1,), (1,)), ((), ())),
        preferred_element_type=f32,
    )
    half = pooled.shape[0] // 2
    out_ref[...] = jnp.concatenate([pooled[:half], pooled[half:]], axis=1)
    for copy in copies[3:]:
        copy.wait()


def decay_kernel(
    forget_ref, in_ref, keys_ref, ends_ref, columns_out, rows_out, early_out, columns_ref, rows_ref, wide, turned, sems
):
    heads = forget_ref.shape[0]
    blocks = keys_ref.shape[0]
    row_order = lax.broadcasted_iota(jnp.int32, (BLK, BLK), 0)
    col_order = lax.broadcasted_iota(jnp.int32, (BLK, BLK), 1)
    upper = jnp.where(row_order <= col_order, 1.0, 0.0).astype(bf16)
    for b in range(blocks):
        span = slice(b * BLK, (b + 1) * BLK)
        cum = sum(dot(part, upper) for part in terms(forget_ref[:, span], 3))
        turned[:heads, span] = cum
        end = cum[:, BLK - 1 :]
        rise = jnp.exp(cum - end)
        ends_ref[b] = jnp.broadcast_to(end, (heads, 128))
        write_t = in_ref[span, :].astype(f32).T
        for h in range(heads):
            keys_ref[b, h] = (write_t * rise[h : h + 1, :]).astype(bf16)
        if b == 0:
            early = pltpu.make_async_copy(keys_ref.at[0], early_out, sems.at[2])
            early.start()
    rows_ref[...] = turned[:heads, :] * LOG2E
    wide[...] = turned[...].T
    before = jnp.zeros((1, heads), f32)
    for b in range(blocks):
        span = slice(b * BLK, (b + 1) * BLK)
        cum = wide[span, :heads]
        parts = terms(jnp.exp(-(cum + before)), 3) + terms(jnp.exp(-cum), 3) + terms(cum * LOG2E, 3)
        columns_ref[span, :] = jnp.concatenate(parts, axis=1)
        before = before + cum[BLK - 1 :, :]
    for copy in fetch((columns_ref, rows_ref), (columns_out, rows_out), sems):
        copy.wait()
    early.wait()


def stream_kernel(
    mine_ref, other_ref, w_ref, embed_ref, keys_ref, ends_ref, pay_ref, stream_out, pooled_out, stream_ref, pooled_ref, sems
):
    packed = mine_ref[...] + other_ref[...]
    pooled = jnp.concatenate([packed[:, :CF], packed[:, CF:]], axis=0)
    pooled_ref[...] = jnp.concatenate(terms(pooled, 3), axis=1)
    heads = pay_ref.shape[0]
    saved = pltpu.make_async_copy(pooled_ref, pooled_out, sems.at[heads // 2])
    saved.start()

    def result(q):
        lanes = pl.ds(pl.multiple_of(q * 256, 256), 256)
        return pltpu.make_async_copy(stream_ref.at[:, lanes], stream_out.at[:, lanes], sems.at[q])

    def pair(q, carry):
        lanes = pl.ds(pl.multiple_of(q * 256, 256), 256)
        w = w_ref[:, lanes]
        visual = dot(pooled_ref[...], jnp.concatenate([w, w, w], axis=0))
        stream_ref[:, lanes] = (embed_ref[:, lanes].astype(f32) + visual).astype(bf16)
        result(q).start()
        return carry

    def states(q, carry):
        stream = stream_ref[:, pl.ds(pl.multiple_of(q * 256, 256), 256)]
        for j in range(2):
            h = 2 * q + j
            part = stream[:, j * P_SIZE : (j + 1) * P_SIZE]
            early = dot(keys_ref[0, h], part[:BLK])
            late = dot(keys_ref[1, h], part[BLK:])
            end_early = ends_ref[0, pl.ds(h, 1), :]
            end_late = ends_ref[1, pl.ds(h, 1), :]
            pay_ref[h, :N, :] = jnp.exp(-end_late) * early + late
            pay_ref[h, N:, :] = jnp.broadcast_to(end_early + end_late, (EXTRA, P_SIZE))
        return carry

    def finish(q, carry):
        result(q).wait()
        return carry

    lax.fori_loop(0, heads // 2, pair, 0, unroll=2)
    lax.fori_loop(0, heads // 2, states, 0, unroll=2)
    lax.fori_loop(0, heads // 2, finish, 0)
    saved.wait()


def pick(heads, q):
    row = lax.broadcasted_iota(jnp.int32, (3 * heads, 2 * P_SIZE), 0)
    lane = lax.broadcasted_iota(jnp.int32, (3 * heads, 2 * P_SIZE), 1)
    h = 2 * q + jnp.where(lane < P_SIZE, 0, 1)
    hit = (row == h) | (row == h + heads) | (row == h + 2 * heads)
    return jnp.where(hit, 1.0, 0.0).astype(bf16)


def side_by_side(states):
    return jnp.concatenate([jnp.concatenate(terms(state, 2), axis=0) for state in states], axis=1)


def within_kernel(skip_ref, *refs):
    far, base_out, near = refs[:7], refs[7], refs[8:15]
    base_ref, scored, in_sems, out_sems = refs[15:]
    copies = fetch(far, near, in_sems)
    in_ref, read_ref, frames_ref, rows_ref, columns_ref, keys_ref, stream_ref = near
    heads = keys_ref.shape[0]
    row_order = lax.broadcasted_iota(jnp.int32, (BLK, BLK), 0)
    col_order = lax.broadcasted_iota(jnp.int32, (BLK, BLK), 1)
    causal = col_order <= row_order
    for copy in copies[:3]:
        copy.wait()
    for b in range(scored.shape[0]):
        span = slice(b * BLK, (b + 1) * BLK)
        scores = lax.dot_general(
            read_ref[span, :], in_ref[span, :], (((1,), (1,)), ((), ())), preferred_element_type=f32
        )
        frame_row = frames_ref[:, span].astype(f32)
        frame_col = jnp.broadcast_to(frame_row, (128, BLK)).T
        same = jnp.concatenate([frame_col, frame_col], axis=1) == frame_row
        scored[b] = jnp.where(causal | same, scores, 0.0)
    for copy in copies[3:]:
        copy.wait()
    read = read_ref[BLK:, :]
    read_twice = jnp.concatenate([read, read], axis=1)

    def result(q):
        lanes = pl.ds(pl.multiple_of(q * 2 * P_SIZE, 2 * P_SIZE), 2 * P_SIZE)
        return pltpu.make_async_copy(base_ref.at[:, lanes], base_out.at[:, lanes], out_sems.at[q])

    def pair(q, carry):
        lanes = pl.ds(pl.multiple_of(q * 2 * P_SIZE, 2 * P_SIZE), 2 * P_SIZE)
        chosen = pick(heads, q)
        cum_col = dot(columns_ref[:, 6 * heads :], chosen)
        stream = stream_ref[:, lanes]
        mixed = [[], []]
        for j in range(2):
            h = 2 * q + j
            cum_row = rows_ref[pl.ds(h, 1), :]
            side = slice(j * P_SIZE, (j + 1) * P_SIZE)
            for b in range(2):
                span = slice(b * BLK, (b + 1) * BLK)
                column = cum_col[span, side]
                distance = jnp.abs(jnp.concatenate([column, column], axis=1) - cum_row[:, span])
                weights = (scored[b] * jnp.exp2(-distance)).astype(bf16)
                part = stream[span, side]
                mixed[b].append(dot(weights, part) + skip_ref[0, h] * part.astype(f32))
        own = dot(columns_ref[BLK:, 3 * heads : 6 * heads], chosen)
        first = [
            dot(keys_ref[2 * q + j], stream[:BLK, j * P_SIZE : (j + 1) * P_SIZE]) for j in range(2)
        ]
        carried = own * dot(read_twice, side_by_side(first))
        base_ref[:BLK, lanes] = jnp.concatenate(mixed[0], axis=1)
        base_ref[BLK:, lanes] = jnp.concatenate(mixed[1], axis=1) + carried
        result(q).start()
        return carry

    def finish(q, carry):
        result(q).wait()
        return carry

    lax.fori_loop(0, heads // 2, pair, 0, unroll=2)
    lax.fori_loop(0, heads // 2, finish, 0)


def total_kernel(got_ref, total_ref):
    state = got_ref[0, :N, :]
    log = got_ref[0, N:, :]
    for i in range(1, got_ref.shape[0]):
        gone = got_ref[i, N:, :]
        state = jnp.exp(-gone[:1]) * state + got_ref[i, :N, :]
        log = log + gone
    for k in range(total_ref.shape[0]):
        total_ref[k, :N, :] = state
        total_ref[k, N:, :] = log


def spread_kernel(got_ref, totals_ref, place_ref, out_ref):
    place = place_ref[...]
    state = jnp.zeros(out_ref.shape[1:], f32)
    for k in range(totals_ref.shape[0] - 1):
        later = jnp.exp(-totals_ref[k, N : N + 1, :]) * state + totals_ref[k, :N, :]
        state = jnp.where(jnp.broadcast_to(place, state.shape) > k, later, state)
    for i in range(got_ref.shape[0]):
        out_ref[i] = state
        state = jnp.exp(-got_ref[i, N : N + 1, :]) * state + got_ref[i, :N, :]


def carry_kernel(state_ref, *refs):
    far, (gated_ref, energy_ref), near = refs[:5], refs[5:7], refs[7:12]
    acc, sems = refs[12:]
    read_ref, columns_ref, pooled_ref, w_ref, base_ref = near
    heads = state_ref.shape[0]

    def base(q):
        lanes = pl.ds(pl.multiple_of(q * 2 * P_SIZE, 2 * P_SIZE), 2 * P_SIZE)
        return pltpu.make_async_copy(far[4].at[:, lanes], base_ref.at[:, lanes], sems.at[q + 4])

    copies = fetch(far[:4], near[:4], sems)
    for q in range(heads // 2):
        base(q).start()
    acc[...] = jnp.zeros_like(acc)
    for copy in copies:
        copy.wait()
    read = read_ref[...]
    read_twice = jnp.concatenate([read, read], axis=1)

    def pair(q, carry):
        lanes = pl.ds(pl.multiple_of(q * 2 * P_SIZE, 2 * P_SIZE), 2 * P_SIZE)
        w = w_ref[:, lanes]
        gate = dot(pooled_ref[...], jnp.concatenate([w, w, w], axis=0))
        half = 0.5 * gate
        silu = half + half * jnp.tanh(half)
        carried = dot(read_twice, side_by_side([state_ref[2 * q], state_ref[2 * q + 1]]))
        carried = dot(columns_ref[:, : 3 * heads], pick(heads, q)) * carried
        base(q).wait()
        gated = (base_ref[:, lanes] + carried) * silu
        gated_ref[:, lanes] = gated
        squares = gated * gated
        acc[...] += squares[:, :P_SIZE] + squares[:, P_SIZE:]
        return carry

    lax.fori_loop(0, heads // 2, pair, 0, unroll=2)
    energy_ref[...] = jnp.sum(acc[...].T, axis=0, keepdims=True)


def norm_kernel(gated_ref, mine_ref, other_ref, gain_ref, out_ref, held, sems):
    inverse = lax.rsqrt((mine_ref[...] + other_ref[...]) / DI + EPSILON)
    copies = []
    for k in range(held.shape[0] // P_SIZE):
        rows = slice(k * P_SIZE, (k + 1) * P_SIZE)
        column = jnp.broadcast_to(inverse[:, rows], (P_SIZE, P_SIZE)).T

        def head(h, carry):
            lanes = pl.ds(pl.multiple_of(h * P_SIZE, P_SIZE), P_SIZE)
            held[rows, lanes] = (gated_ref[rows, lanes] * column * gain_ref[:, lanes]).astype(bf16)
            return carry

        lax.fori_loop(0, held.shape[1] // P_SIZE, head, 0, unroll=8)
        copies.append(pltpu.make_async_copy(held.at[rows], out_ref.at[rows], sems.at[k]))
        copies[-1].start()
    for copy in copies:
        copy.wait()


def outside(arrays):
    return tuple(pltpu.with_memory_space_constraint(array, pltpu.HBM) for array in arrays)


def call(kernel, ins, outs, scratch=(), specs=None):
    return pl.pallas_call(
        kernel,
        out_shape=[
            pltpu.HBM(*out[:2]) if out[2:] else jax.ShapeDtypeStruct(*out) for out in outs
        ],
        in_specs=specs or [VMEM] * len(ins),
        out_specs=[HBM if out[2:] else VMEM for out in outs],
        scratch_shapes=list(scratch),
        compiler_params=PARAMS,
    )(*ins)


def swap(value, axis):
    return lax.ppermute(value, axis, [(0, 1), (1, 0)])


def body(
    depth_logits,
    features,
    cell_index,
    embed,
    w_visual,
    w_gate,
    input_map,
    output_map,
    forget,
    skip,
    frame_ids,
    norm_gain,
):
    tokens, width = embed.shape
    heads = forget.shape[1]
    blocks = tokens // BLK
    pixels, bins = depth_logits.shape[1:]
    shards = lax.axis_size("ctx")
    groups = [list(range(g, g + heads)) for g in range(0, shards, heads)]
    peers = [list(range(g, shards, heads)) for g in range(heads)]
    place = jnp.full((1, P_SIZE), lax.axis_index("ctx") // heads, jnp.int32)

    near = (depth_logits.transpose(2, 0, 1), cell_index.transpose(2, 0, 1), features[0].T)
    far = (forget.T, input_map, w_visual, embed, norm_gain.reshape(1, width))
    partial_sum, forget_t, writes, w_visual, embed, norm_gain = call(
        pool_kernel,
        outside(near + far),
        [((tokens // 2, 2 * CF), f32)] + [(array.shape, array.dtype) for array in far],
        [
            pltpu.VMEM((bins, 1, pixels), f32),
            pltpu.VMEM((bins, 1, pixels), jnp.int32),
            pltpu.VMEM((CF, pixels), bf16),
            pltpu.VMEM((bins, 1, pixels), f32),
            pltpu.VMEM((tokens, 2 * pixels), bf16),
            pltpu.SemaphoreType.DMA((len(near + far),)),
        ],
        specs=[HBM] * len(near + far),
    )
    partial_sum, place = lax.optimization_barrier((partial_sum, place))
    chip_sum = partial_sum + swap(partial_sum, "mp")
    other_sum = swap(chip_sum, "section")

    keys, ends, columns, row_sums, early_keys = call(
        decay_kernel,
        (forget_t, writes),
        [
            ((blocks, heads, N, BLK), bf16),
            ((blocks, heads, 128), f32),
            ((tokens, 9 * heads), bf16, True),
            ((heads, tokens), f32, True),
            ((heads, N, BLK), bf16, True),
        ],
        [
            pltpu.VMEM((tokens, 9 * heads), bf16),
            pltpu.VMEM((heads, tokens), f32),
            pltpu.VMEM((tokens, 128), f32),
            pltpu.VMEM((128, tokens), f32),
            pltpu.SemaphoreType.DMA((3,)),
        ],
    )

    pay, stream, pooled = call(
        stream_kernel,
        (chip_sum, other_sum, w_visual, embed, keys, ends),
        [
            ((heads, N + EXTRA, P_SIZE), f32),
            ((tokens, width), bf16, True),
            ((tokens, 3 * CF), bf16, True),
        ],
        [
            pltpu.VMEM((tokens, width), bf16),
            pltpu.VMEM((tokens, 3 * CF), bf16),
            pltpu.SemaphoreType.DMA((heads // 2 + 1,)),
        ],
    )
    got = lax.all_to_all(pay, "ctx", 0, 0, axis_index_groups=groups, tiled=True)

    held = (input_map, output_map, frame_ids.reshape(1, tokens), row_sums, columns)
    held += (early_keys, stream)
    (base,) = call(
        within_kernel,
        (skip.reshape(1, heads),) + outside(held),
        [((tokens, width), f32, True)],
        [pltpu.VMEM(array.shape, array.dtype) for array in held]
        + [
            pltpu.VMEM((tokens, width), f32),
            pltpu.VMEM((blocks, BLK, BLK), f32),
            pltpu.SemaphoreType.DMA((len(held),)),
            pltpu.SemaphoreType.DMA((heads // 2,)),
        ],
        specs=[SMEM] + [HBM] * len(held),
    )

    (total,) = call(total_kernel, (got,), [((shards // heads, N + EXTRA, P_SIZE), f32)])
    totals = lax.all_to_all(total, "ctx", 0, 0, axis_index_groups=peers, tiled=True)
    (sent,) = call(spread_kernel, (got, totals, place), [((heads, N, P_SIZE), f32)])
    incoming = lax.all_to_all(sent, "ctx", 0, 0, axis_index_groups=groups, tiled=True)

    held = (output_map, columns, pooled, w_gate, base)
    gated, energy = call(
        carry_kernel,
        (incoming,) + outside(held),
        [((tokens, width), f32), ((1, tokens), f32)],
        [pltpu.VMEM(array.shape, array.dtype) for array in held]
        + [pltpu.VMEM((tokens, P_SIZE), f32), pltpu.SemaphoreType.DMA((heads // 2 + 4,))],
        specs=[VMEM] + [HBM] * len(held),
    )
    chip_energy = energy + swap(energy, "mp")
    other_energy = swap(chip_energy, "section")
    (out,) = call(
        norm_kernel,
        (gated, chip_energy, other_energy, norm_gain),
        [((tokens, width), bf16, True)],
        [pltpu.VMEM((tokens, width), bf16), pltpu.SemaphoreType.DMA((tokens // P_SIZE,))],
    )
    return out


def solution(mesh):
    return jax.shard_map(
        body,
        mesh=mesh,
        in_specs=(
            P("section", ("ctx", "mp"), None),
            P("section", ("ctx", "mp"), None),
            P("section", ("ctx", "mp"), None),
            P("ctx", ("section", "mp")),
            P(None, ("section", "mp")),
            P(None, ("section", "mp")),
            P("ctx", None),
            P("ctx", None),
            P("ctx", ("section", "mp")),
            P(("section", "mp")),
            P("ctx"),
            P(("section", "mp")),
        ),
        out_specs=P("ctx", ("section", "mp")),
        check_vma=False,
    )
```

```python
import math

import jax
import jax.numpy as jnp
from jax import lax
from jax.experimental import pallas as pl
from jax.experimental.pallas import tpu as pltpu
from jax.sharding import PartitionSpec as P

P_SIZE = 128
N = 128
BLK = 256
CF = 64
DI = 8192
EPSILON = 1e-05
LOG2E = math.log2(math.e)
CHUNK = 64
EXTRA = 8

f32 = jnp.float32
bf16 = jnp.bfloat16

VMEM = pl.BlockSpec(memory_space=pltpu.VMEM)
SMEM = pl.BlockSpec(memory_space=pltpu.SMEM)
HBM = pl.BlockSpec(memory_space=pltpu.HBM)
PARAMS = pltpu.CompilerParams(vmem_limit_bytes=24 * 1024 * 1024)


def terms(x, count):
    parts = []
    for _ in range(count - 1):
        part = x.astype(bf16)
        parts.append(part)
        x = x - part.astype(f32)
    parts.append(x.astype(bf16))
    return parts


def dot(a, b):
    return jnp.dot(a, b, preferred_element_type=f32)


def fetch(far, near, sems):
    copies = [pltpu.make_async_copy(f, n, sems.at[i]) for i, (f, n) in enumerate(zip(far, near))]
    for copy in copies:
        copy.start()
    return copies


def pool_kernel(*refs):
    count = (len(refs) - 4) // 2
    far, out_ref, near = refs[:count], refs[count], refs[count + 1 : 2 * count - 2]
    logits_ref, cells_ref, feats_ref, prob, hits, sems = refs[2 * count - 2 :]
    near = (logits_ref, cells_ref, feats_ref) + tuple(near)
    copies = [pltpu.make_async_copy(far[i], near[i], sems.at[i]) for i in range(count)]
    for copy in copies:
        copy.start()
    for copy in copies[:3]:
        copy.wait()
    bins, _, rows = logits_ref.shape
    logits = logits_ref[...]
    raised = jnp.exp(logits - jnp.max(logits, axis=0, keepdims=True))
    prob[...] = raised / jnp.sum(raised, axis=0, keepdims=True)

    def chunk(k, carry):
        first = pl.multiple_of(k * CHUNK, CHUNK)
        ids = lax.broadcasted_iota(jnp.int32, (CHUNK, rows), 0) + first
        acc = jnp.zeros((CHUNK, rows), f32)
        for d in range(bins):
            acc = acc + jnp.where(cells_ref[d] == ids, prob[d], 0.0)
        high, low = terms(acc, 2)
        hits[pl.ds(first, CHUNK), :rows] = high
        hits[pl.ds(first, CHUNK), rows:] = low
        return carry

    lax.fori_loop(0, hits.shape[0] // CHUNK, chunk, 0)
    feats = feats_ref[...]
    pooled = lax.dot_general(
        hits[...],
        jnp.concatenate([feats, feats], axis=1),
        (((1,), (1,)), ((), ())),
        preferred_element_type=f32,
    )
    half = pooled.shape[0] // 2
    out_ref[...] = jnp.concatenate([pooled[:half], pooled[half:]], axis=1)
    for copy in copies[3:]:
        copy.wait()


def decay_kernel(
    forget_ref, in_ref, keys_ref, ends_ref, columns_out, rows_out, early_out, columns_ref, rows_ref, wide, turned, sems
):
    heads = forget_ref.shape[0]
    blocks = keys_ref.shape[0]
    row_order = lax.broadcasted_iota(jnp.int32, (BLK, BLK), 0)
    col_order = lax.broadcasted_iota(jnp.int32, (BLK, BLK), 1)
    upper = jnp.where(row_order <= col_order, 1.0, 0.0).astype(bf16)
    for b in range(blocks):
        span = slice(b * BLK, (b + 1) * BLK)
        cum = sum(dot(part, upper) for part in terms(forget_ref[:, span], 3))
        turned[:heads, span] = cum
        end = cum[:, BLK - 1 :]
        rise = jnp.exp(cum - end)
        ends_ref[b] = jnp.broadcast_to(end, (heads, 128))
        write_t = in_ref[span, :].astype(f32).T
        for h in range(heads):
            keys_ref[b, h] = (write_t * rise[h : h + 1, :]).astype(bf16)
        if b == 0:
            early = pltpu.make_async_copy(keys_ref.at[0], early_out, sems.at[2])
            early.start()
    rows_ref[...] = turned[:heads, :] * LOG2E
    wide[...] = turned[...].T
    before = jnp.zeros((1, heads), f32)
    for b in range(blocks):
        span = slice(b * BLK, (b + 1) * BLK)
        cum = wide[span, :heads]
        parts = terms(jnp.exp(-(cum + before)), 3) + terms(jnp.exp(-cum), 3) + terms(cum * LOG2E, 3)
        columns_ref[span, :] = jnp.concatenate(parts, axis=1)
        before = before + cum[BLK - 1 :, :]
    for copy in fetch((columns_ref, rows_ref), (columns_out, rows_out), sems):
        copy.wait()
    early.wait()


def stream_kernel(
    mine_ref, other_ref, w_ref, embed_ref, keys_ref, ends_ref, pay_ref, stream_out, pooled_out, stream_ref, pooled_ref, sems
):
    packed = mine_ref[...] + other_ref[...]
    pooled = jnp.concatenate([packed[:, :CF], packed[:, CF:]], axis=0)
    pooled_ref[...] = jnp.concatenate(terms(pooled, 3), axis=1)
    heads = pay_ref.shape[0]
    saved = pltpu.make_async_copy(pooled_ref, pooled_out, sems.at[heads // 2])
    saved.start()

    def result(q):
        lanes = pl.ds(pl.multiple_of(q * 256, 256), 256)
        return pltpu.make_async_copy(stream_ref.at[:, lanes], stream_out.at[:, lanes], sems.at[q])

    def pair(q, carry):
        lanes = pl.ds(pl.multiple_of(q * 256, 256), 256)
        w = w_ref[:, lanes]
        visual = dot(pooled_ref[...], jnp.concatenate([w, w, w], axis=0))
        stream_ref[:, lanes] = (embed_ref[:, lanes].astype(f32) + visual).astype(bf16)
        result(q).start()
        return carry

    def states(q, carry):
        stream = stream_ref[:, pl.ds(pl.multiple_of(q * 256, 256), 256)]
        for j in range(2):
            h = 2 * q + j
            part = stream[:, j * P_SIZE : (j + 1) * P_SIZE]
            early = dot(keys_ref[0, h], part[:BLK])
            late = dot(keys_ref[1, h], part[BLK:])
            end_early = ends_ref[0, pl.ds(h, 1), :]
            end_late = ends_ref[1, pl.ds(h, 1), :]
            pay_ref[h, :N, :] = jnp.exp(-end_late) * early + late
            pay_ref[h, N:, :] = jnp.broadcast_to(end_early + end_late, (EXTRA, P_SIZE))
        return carry

    def finish(q, carry):
        result(q).wait()
        return carry

    lax.fori_loop(0, heads // 2, pair, 0, unroll=2)
    lax.fori_loop(0, heads // 2, states, 0, unroll=2)
    lax.fori_loop(0, heads // 2, finish, 0)
    saved.wait()


def pick(heads, q):
    row = lax.broadcasted_iota(jnp.int32, (3 * heads, 2 * P_SIZE), 0)
    lane = lax.broadcasted_iota(jnp.int32, (3 * heads, 2 * P_SIZE), 1)
    h = 2 * q + jnp.where(lane < P_SIZE, 0, 1)
    hit = (row == h) | (row == h + heads) | (row == h + 2 * heads)
    return jnp.where(hit, 1.0, 0.0).astype(bf16)


def side_by_side(states):
    return jnp.concatenate([jnp.concatenate(terms(state, 2), axis=0) for state in states], axis=1)


def within_kernel(skip_ref, *refs):
    far, (base_out, gain_ref), near = refs[:9], refs[9:11], refs[11:20]
    base_ref, scored, in_sems, out_sems = refs[20:]
    copies = fetch(far, near, in_sems)
    in_ref, read_ref, frames_ref, rows_ref, columns_ref, w_ref, pooled_ref, keys_ref, stream_ref = near
    heads = keys_ref.shape[0]
    row_order = lax.broadcasted_iota(jnp.int32, (BLK, BLK), 0)
    col_order = lax.broadcasted_iota(jnp.int32, (BLK, BLK), 1)
    causal = col_order <= row_order
    for copy in copies[:3]:
        copy.wait()
    for b in range(scored.shape[0]):
        span = slice(b * BLK, (b + 1) * BLK)
        scores = lax.dot_general(
            read_ref[span, :], in_ref[span, :], (((1,), (1,)), ((), ())), preferred_element_type=f32
        )
        frame_row = frames_ref[:, span].astype(f32)
        frame_col = jnp.broadcast_to(frame_row, (128, BLK)).T
        same = jnp.concatenate([frame_col, frame_col], axis=1) == frame_row
        scored[b] = jnp.where(causal | same, scores, 0.0)
    for copy in copies[3:]:
        copy.wait()
    read = read_ref[BLK:, :]
    read_twice = jnp.concatenate([read, read], axis=1)
    late_rows = slice(BLK, 2 * BLK)

    def result(q):
        lanes = pl.ds(pl.multiple_of(q * 2 * P_SIZE, 2 * P_SIZE), 2 * P_SIZE)
        return pltpu.make_async_copy(base_ref.at[:, lanes], base_out.at[:, lanes], out_sems.at[q])

    def pair(q, carry):
        lanes = pl.ds(pl.multiple_of(q * 2 * P_SIZE, 2 * P_SIZE), 2 * P_SIZE)
        w = w_ref[:, lanes]
        gate = dot(pooled_ref[...], jnp.concatenate([w, w, w], axis=0))
        half = 0.5 * gate
        silu = half + half * jnp.tanh(half)
        chosen = pick(heads, q)
        gain_ref[:, lanes] = (silu * dot(columns_ref[:, : 3 * heads], chosen)).astype(bf16)
        cum_col = dot(columns_ref[:, 6 * heads :], chosen)
        stream = stream_ref[:, lanes]
        mixed = [[], []]
        for j in range(2):
            h = 2 * q + j
            cum_row = rows_ref[pl.ds(h, 1), :]
            side = slice(j * P_SIZE, (j + 1) * P_SIZE)
            for b in range(2):
                span = slice(b * BLK, (b + 1) * BLK)
                column = cum_col[span, side]
                distance = jnp.abs(jnp.concatenate([column, column], axis=1) - cum_row[:, span])
                weights = (scored[b] * jnp.exp2(-distance)).astype(bf16)
                part = stream[span, side]
                mixed[b].append(dot(weights, part) + skip_ref[0, h] * part.astype(f32))
        own = dot(columns_ref[late_rows, 3 * heads : 6 * heads], chosen)
        first = [
            dot(keys_ref[2 * q + j], stream[:BLK, j * P_SIZE : (j + 1) * P_SIZE]) for j in range(2)
        ]
        carried = own * dot(read_twice, side_by_side(first))
        base_ref[:BLK, lanes] = jnp.concatenate(mixed[0], axis=1) * silu[:BLK]
        base_ref[BLK:, lanes] = (jnp.concatenate(mixed[1], axis=1) + carried) * silu[BLK:]
        result(q).start()
        return carry

    def finish(q, carry):
        result(q).wait()
        return carry

    lax.fori_loop(0, heads // 2, pair, 0)
    lax.fori_loop(0, heads // 2, finish, 0)


def total_kernel(got_ref, total_ref):
    state = got_ref[0, :N, :]
    log = got_ref[0, N:, :]
    for i in range(1, got_ref.shape[0]):
        gone = got_ref[i, N:, :]
        state = jnp.exp(-gone[:1]) * state + got_ref[i, :N, :]
        log = log + gone
    for k in range(total_ref.shape[0]):
        total_ref[k, :N, :] = state
        total_ref[k, N:, :] = log


def spread_kernel(got_ref, totals_ref, place_ref, out_ref):
    place = place_ref[...]
    state = jnp.zeros(out_ref.shape[1:], f32)
    for k in range(totals_ref.shape[0] - 1):
        later = jnp.exp(-totals_ref[k, N : N + 1, :]) * state + totals_ref[k, :N, :]
        state = jnp.where(jnp.broadcast_to(place, state.shape) > k, later, state)
    for i in range(got_ref.shape[0]):
        out_ref[i] = state
        state = jnp.exp(-got_ref[i, N : N + 1, :]) * state + got_ref[i, :N, :]


def carry_kernel(state_ref, gain_ref, read_far, base_far, gated_ref, energy_ref, read_ref, base_ref, acc, sems):
    heads = state_ref.shape[0]

    def base(q):
        lanes = pl.ds(pl.multiple_of(q * 2 * P_SIZE, 2 * P_SIZE), 2 * P_SIZE)
        return pltpu.make_async_copy(base_far.at[:, lanes], base_ref.at[:, lanes], sems.at[q])

    first = pltpu.make_async_copy(read_far, read_ref, sems.at[heads // 2])
    first.start()
    for q in range(heads // 2):
        base(q).start()
    acc[...] = jnp.zeros_like(acc)
    first.wait()
    read = read_ref[...]
    read_twice = jnp.concatenate([read, read], axis=1)

    def pair(q, carry):
        lanes = pl.ds(pl.multiple_of(q * 2 * P_SIZE, 2 * P_SIZE), 2 * P_SIZE)
        carried = dot(read_twice, side_by_side([state_ref[2 * q], state_ref[2 * q + 1]]))
        base(q).wait()
        gated = base_ref[:, lanes] + gain_ref[:, lanes].astype(f32) * carried
        gated_ref[:, lanes] = gated
        squares = gated * gated
        acc[...] += squares[:, :P_SIZE] + squares[:, P_SIZE:]
        return carry

    lax.fori_loop(0, heads // 2, pair, 0)
    energy_ref[...] = jnp.sum(acc[...].T, axis=0, keepdims=True)


def norm_kernel(gated_ref, mine_ref, other_ref, gain_ref, out_ref, held, sems):
    inverse = lax.rsqrt((mine_ref[...] + other_ref[...]) / DI + EPSILON)
    copies = []
    for k in range(held.shape[0] // P_SIZE):
        rows = slice(k * P_SIZE, (k + 1) * P_SIZE)
        column = jnp.broadcast_to(inverse[:, rows], (P_SIZE, P_SIZE)).T

        def head(h, carry):
            lanes = pl.ds(pl.multiple_of(h * P_SIZE, P_SIZE), P_SIZE)
            held[rows, lanes] = (gated_ref[rows, lanes] * column * gain_ref[:, lanes]).astype(bf16)
            return carry

        lax.fori_loop(0, held.shape[1] // P_SIZE, head, 0, unroll=8)
        copies.append(pltpu.make_async_copy(held.at[rows], out_ref.at[rows], sems.at[k]))
        copies[-1].start()
    for copy in copies:
        copy.wait()


def outside(arrays):
    return tuple(pltpu.with_memory_space_constraint(array, pltpu.HBM) for array in arrays)


def call(kernel, ins, outs, scratch=(), specs=None):
    return pl.pallas_call(
        kernel,
        out_shape=[
            pltpu.HBM(*out[:2]) if out[2:] else jax.ShapeDtypeStruct(*out) for out in outs
        ],
        in_specs=specs or [VMEM] * len(ins),
        out_specs=[HBM if out[2:] else VMEM for out in outs],
        scratch_shapes=list(scratch),
        compiler_params=PARAMS,
    )(*ins)


def swap(value, axis):
    return lax.ppermute(value, axis, [(0, 1), (1, 0)])


def body(
    depth_logits,
    features,
    cell_index,
    embed,
    w_visual,
    w_gate,
    input_map,
    output_map,
    forget,
    skip,
    frame_ids,
    norm_gain,
):
    tokens, width = embed.shape
    heads = forget.shape[1]
    blocks = tokens // BLK
    pixels, bins = depth_logits.shape[1:]
    shards = lax.axis_size("ctx")
    groups = [list(range(g, g + heads)) for g in range(0, shards, heads)]
    peers = [list(range(g, shards, heads)) for g in range(heads)]
    place = jnp.full((1, P_SIZE), lax.axis_index("ctx") // heads, jnp.int32)

    near = (depth_logits.transpose(2, 0, 1), cell_index.transpose(2, 0, 1), features[0].T)
    far = (forget.T, input_map, w_visual, embed, norm_gain.reshape(1, width))
    partial_sum, forget_t, writes, w_visual, embed, norm_gain = call(
        pool_kernel,
        outside(near + far),
        [((tokens // 2, 2 * CF), f32)] + [(array.shape, array.dtype) for array in far],
        [
            pltpu.VMEM((bins, 1, pixels), f32),
            pltpu.VMEM((bins, 1, pixels), jnp.int32),
            pltpu.VMEM((CF, pixels), bf16),
            pltpu.VMEM((bins, 1, pixels), f32),
            pltpu.VMEM((tokens, 2 * pixels), bf16),
            pltpu.SemaphoreType.DMA((len(near + far),)),
        ],
        specs=[HBM] * len(near + far),
    )
    partial_sum, place = lax.optimization_barrier((partial_sum, place))
    chip_sum = partial_sum + swap(partial_sum, "mp")
    other_sum = swap(chip_sum, "section")

    keys, ends, columns, row_sums, early_keys = call(
        decay_kernel,
        (forget_t, writes),
        [
            ((blocks, heads, N, BLK), bf16),
            ((blocks, heads, 128), f32),
            ((tokens, 9 * heads), bf16, True),
            ((heads, tokens), f32, True),
            ((heads, N, BLK), bf16, True),
        ],
        [
            pltpu.VMEM((tokens, 9 * heads), bf16),
            pltpu.VMEM((heads, tokens), f32),
            pltpu.VMEM((tokens, 128), f32),
            pltpu.VMEM((128, tokens), f32),
            pltpu.SemaphoreType.DMA((3,)),
        ],
    )

    pay, stream, pooled = call(
        stream_kernel,
        (chip_sum, other_sum, w_visual, embed, keys, ends),
        [
            ((heads, N + EXTRA, P_SIZE), f32),
            ((tokens, width), bf16, True),
            ((tokens, 3 * CF), bf16, True),
        ],
        [
            pltpu.VMEM((tokens, width), bf16),
            pltpu.VMEM((tokens, 3 * CF), bf16),
            pltpu.SemaphoreType.DMA((heads // 2 + 1,)),
        ],
    )
    got = lax.all_to_all(pay, "ctx", 0, 0, axis_index_groups=groups, tiled=True)

    held = (input_map, output_map, frame_ids.reshape(1, tokens), row_sums, columns)
    held += (w_gate, pooled, early_keys, stream)
    base, gain = call(
        within_kernel,
        (skip.reshape(1, heads),) + outside(held),
        [((tokens, width), f32, True), ((tokens, width), bf16)],
        [pltpu.VMEM(array.shape, array.dtype) for array in held]
        + [
            pltpu.VMEM((tokens, width), f32),
            pltpu.VMEM((blocks, BLK, BLK), f32),
            pltpu.SemaphoreType.DMA((len(held),)),
            pltpu.SemaphoreType.DMA((heads // 2,)),
        ],
        specs=[SMEM] + [HBM] * len(held),
    )

    (total,) = call(total_kernel, (got,), [((shards // heads, N + EXTRA, P_SIZE), f32)])
    totals = lax.all_to_all(total, "ctx", 0, 0, axis_index_groups=peers, tiled=True)
    (sent,) = call(spread_kernel, (got, totals, place), [((heads, N, P_SIZE), f32)])
    incoming = lax.all_to_all(sent, "ctx", 0, 0, axis_index_groups=groups, tiled=True)

    gated, energy = call(
        carry_kernel,
        (incoming, gain) + outside((output_map, base)),
        [((tokens, width), f32), ((1, tokens), f32)],
        [
            pltpu.VMEM((tokens, N), bf16),
            pltpu.VMEM((tokens, width), f32),
            pltpu.VMEM((tokens, P_SIZE), f32),
            pltpu.SemaphoreType.DMA((heads // 2 + 1,)),
        ],
        specs=[VMEM, VMEM, HBM, HBM],
    )
    chip_energy = energy + swap(energy, "mp")
    other_energy = swap(chip_energy, "section")
    (out,) = call(
        norm_kernel,
        (gated, chip_energy, other_energy, norm_gain),
        [((tokens, width), bf16, True)],
        [pltpu.VMEM((tokens, width), bf16), pltpu.SemaphoreType.DMA((tokens // P_SIZE,))],
    )
    return out


def solution(mesh):
    return jax.shard_map(
        body,
        mesh=mesh,
        in_specs=(
            P("section", ("ctx", "mp"), None),
            P("section", ("ctx", "mp"), None),
            P("section", ("ctx", "mp"), None),
            P("ctx", ("section", "mp")),
            P(None, ("section", "mp")),
            P(None, ("section", "mp")),
            P("ctx", None),
            P("ctx", None),
            P("ctx", ("section", "mp")),
            P(("section", "mp")),
            P("ctx"),
            P(("section", "mp")),
        ),
        out_specs=P("ctx", ("section", "mp")),
        check_vma=False,
    )
```

```python
import math

import jax
import jax.numpy as jnp
from jax import lax
from jax.experimental import pallas as pl
from jax.experimental.pallas import tpu as pltpu
from jax.sharding import PartitionSpec as P

P_SIZE = 128
N = 128
BLK = 256
CF = 64
DI = 8192
EPSILON = 1e-05
LOG2E = math.log2(math.e)
SPAN = 128
CHUNK = 32
EXTRA = 8

f32 = jnp.float32
bf16 = jnp.bfloat16

VMEM = pl.BlockSpec(memory_space=pltpu.VMEM)
SMEM = pl.BlockSpec(memory_space=pltpu.SMEM)
HBM = pl.BlockSpec(memory_space=pltpu.HBM)
PARAMS = pltpu.CompilerParams(vmem_limit_bytes=24 * 1024 * 1024)


def terms(x, count):
    parts = []
    for _ in range(count - 1):
        part = x.astype(bf16)
        parts.append(part)
        x = x - part.astype(f32)
    parts.append(x.astype(bf16))
    return parts


def dot(a, b):
    return jnp.dot(a, b, preferred_element_type=f32)


def fetch(far, near, sems):
    copies = [pltpu.make_async_copy(f, n, sems.at[i]) for i, (f, n) in enumerate(zip(far, near))]
    for copy in copies:
        copy.start()
    return copies


def pool_kernel(*refs):
    count = (len(refs) - 5) // 2
    far, out_ref, near = refs[:count], refs[count], refs[count + 1 : 2 * count - 2]
    logits_ref, cells_ref, feats_ref, place, prob, hits, sems = refs[2 * count - 2 :]
    near = (logits_ref, cells_ref, feats_ref) + tuple(near)
    copies = [pltpu.make_async_copy(far[i], near[i], sems.at[i]) for i in range(count)]
    for copy in copies:
        copy.start()
    for copy in copies[:3]:
        copy.wait()
    bins, _, rows = logits_ref.shape
    spans = hits.shape[0] // SPAN
    logits = logits_ref[...]
    raised = jnp.exp(logits - jnp.max(logits, axis=0, keepdims=True))
    probability = raised / jnp.sum(raised, axis=0, keepdims=True)
    cells = cells_ref[...]
    place[...] = cells & (SPAN - 1)
    for k in range(spans):
        prob[k] = jnp.where(cells // SPAN == k, probability, 0.0)

    def chunk(i, carry):
        first = pl.multiple_of(i * CHUNK, CHUNK)
        ids = lax.broadcasted_iota(jnp.int32, (CHUNK, rows), 0) + first
        sums = [jnp.zeros((CHUNK, rows), f32) for _ in range(spans)]
        for d in range(bins):
            hit = place[d] == ids
            sums = [sums[k] + jnp.where(hit, prob[k, d], 0.0) for k in range(spans)]
        for k in range(spans):
            high, low = terms(sums[k], 2)
            hits[pl.ds(k * SPAN + first, CHUNK), :rows] = high
            hits[pl.ds(k * SPAN + first, CHUNK), rows:] = low
        return carry

    lax.fori_loop(0, SPAN // CHUNK, chunk, 0)
    feats = feats_ref[...]
    pooled = lax.dot_general(
        hits[...],
        jnp.concatenate([feats, feats], axis=1),
        (((1,), (1,)), ((), ())),
        preferred_element_type=f32,
    )
    half = pooled.shape[0] // 2
    out_ref[...] = jnp.concatenate([pooled[:half], pooled[half:]], axis=1)
    for copy in copies[3:]:
        copy.wait()


def decay_kernel(
    forget_ref, in_ref, keys_ref, ends_ref, columns_out, rows_out, early_out, columns_ref, rows_ref, wide, turned, sems
):
    heads = forget_ref.shape[0]
    blocks = keys_ref.shape[0]
    row_order = lax.broadcasted_iota(jnp.int32, (BLK, BLK), 0)
    col_order = lax.broadcasted_iota(jnp.int32, (BLK, BLK), 1)
    upper = jnp.where(row_order <= col_order, 1.0, 0.0).astype(bf16)
    for b in range(blocks):
        span = slice(b * BLK, (b + 1) * BLK)
        cum = sum(dot(part, upper) for part in terms(forget_ref[:, span], 3))
        turned[:heads, span] = cum
        end = cum[:, BLK - 1 :]
        rise = jnp.exp(cum - end)
        ends_ref[b] = jnp.broadcast_to(end, (heads, 128))
        write_t = in_ref[span, :].astype(f32).T
        for h in range(heads):
            keys_ref[b, h] = (write_t * rise[h : h + 1, :]).astype(bf16)
        if b == 0:
            early = pltpu.make_async_copy(keys_ref.at[0], early_out, sems.at[2])
            early.start()
    rows_ref[...] = turned[:heads, :] * LOG2E
    wide[...] = turned[...].T
    before = jnp.zeros((1, heads), f32)
    for b in range(blocks):
        span = slice(b * BLK, (b + 1) * BLK)
        cum = wide[span, :heads]
        parts = terms(jnp.exp(-(cum + before)), 3) + terms(jnp.exp(-cum), 3) + terms(cum * LOG2E, 3)
        columns_ref[span, :] = jnp.concatenate(parts, axis=1)
        before = before + cum[BLK - 1 :, :]
    for copy in fetch((columns_ref, rows_ref), (columns_out, rows_out), sems):
        copy.wait()
    early.wait()


def stream_kernel(
    mine_ref, other_ref, w_ref, embed_ref, keys_ref, ends_ref, pay_ref, stream_out, pooled_out, stream_ref, pooled_ref, sems
):
    packed = mine_ref[...] + other_ref[...]
    pooled = jnp.concatenate([packed[:, :CF], packed[:, CF:]], axis=0)
    pooled_ref[...] = jnp.concatenate(terms(pooled, 3), axis=1)
    heads = pay_ref.shape[0]
    saved = pltpu.make_async_copy(pooled_ref, pooled_out, sems.at[heads // 2])
    saved.start()

    def result(q):
        lanes = pl.ds(pl.multiple_of(q * 256, 256), 256)
        return pltpu.make_async_copy(stream_ref.at[:, lanes], stream_out.at[:, lanes], sems.at[q])

    def pair(q, carry):
        lanes = pl.ds(pl.multiple_of(q * 256, 256), 256)
        w = w_ref[:, lanes]
        visual = dot(pooled_ref[...], jnp.concatenate([w, w, w], axis=0))
        stream_ref[:, lanes] = (embed_ref[:, lanes].astype(f32) + visual).astype(bf16)
        result(q).start()
        return carry

    def states(q, carry):
        stream = stream_ref[:, pl.ds(pl.multiple_of(q * 256, 256), 256)]
        for j in range(2):
            h = 2 * q + j
            part = stream[:, j * P_SIZE : (j + 1) * P_SIZE]
            early = dot(keys_ref[0, h], part[:BLK])
            late = dot(keys_ref[1, h], part[BLK:])
            end_early = ends_ref[0, pl.ds(h, 1), :]
            end_late = ends_ref[1, pl.ds(h, 1), :]
            pay_ref[h, :N, :] = jnp.exp(-end_late) * early + late
            pay_ref[h, N:, :] = jnp.broadcast_to(end_early + end_late, (EXTRA, P_SIZE))
        return carry

    def finish(q, carry):
        result(q).wait()
        return carry

    lax.fori_loop(0, heads // 2, pair, 0, unroll=2)
    lax.fori_loop(0, heads // 2, states, 0, unroll=2)
    lax.fori_loop(0, heads // 2, finish, 0)
    saved.wait()


def pick(heads, q):
    row = lax.broadcasted_iota(jnp.int32, (3 * heads, 2 * P_SIZE), 0)
    lane = lax.broadcasted_iota(jnp.int32, (3 * heads, 2 * P_SIZE), 1)
    h = 2 * q + jnp.where(lane < P_SIZE, 0, 1)
    hit = (row == h) | (row == h + heads) | (row == h + 2 * heads)
    return jnp.where(hit, 1.0, 0.0).astype(bf16)


def side_by_side(states):
    return jnp.concatenate([jnp.concatenate(terms(state, 2), axis=0) for state in states], axis=1)


def within_kernel(skip_ref, *refs):
    far, (base_out, gain_out), near = refs[:9], refs[9:11], refs[11:20]
    base_ref, gain_ref, scored, in_sems, out_sems = refs[20:]
    copies = fetch(far, near, in_sems)
    in_ref, read_ref, frames_ref, rows_ref, columns_ref, w_ref, pooled_ref, keys_ref, stream_ref = near
    heads = keys_ref.shape[0]
    row_order = lax.broadcasted_iota(jnp.int32, (BLK, BLK), 0)
    col_order = lax.broadcasted_iota(jnp.int32, (BLK, BLK), 1)
    causal = col_order <= row_order
    for copy in copies[:3]:
        copy.wait()
    for b in range(scored.shape[0]):
        span = slice(b * BLK, (b + 1) * BLK)
        scores = lax.dot_general(
            read_ref[span, :], in_ref[span, :], (((1,), (1,)), ((), ())), preferred_element_type=f32
        )
        frame_row = frames_ref[:, span].astype(f32)
        frame_col = jnp.broadcast_to(frame_row, (128, BLK)).T
        same = jnp.concatenate([frame_col, frame_col], axis=1) == frame_row
        scored[b] = jnp.where(causal | same, scores, 0.0)
    for copy in copies[3:]:
        copy.wait()
    read = read_ref[BLK:, :]
    read_twice = jnp.concatenate([read, read], axis=1)
    late_rows = slice(BLK, 2 * BLK)

    def results(q):
        lanes = pl.ds(pl.multiple_of(q * 2 * P_SIZE, 2 * P_SIZE), 2 * P_SIZE)
        return (
            pltpu.make_async_copy(base_ref.at[:, lanes], base_out.at[:, lanes], out_sems.at[0, q]),
            pltpu.make_async_copy(gain_ref.at[:, lanes], gain_out.at[:, lanes], out_sems.at[1, q]),
        )

    def pair(q, carry):
        lanes = pl.ds(pl.multiple_of(q * 2 * P_SIZE, 2 * P_SIZE), 2 * P_SIZE)
        w = w_ref[:, lanes]
        gate = dot(pooled_ref[...], jnp.concatenate([w, w, w], axis=0))
        half = 0.5 * gate
        silu = half + half * jnp.tanh(half)
        chosen = pick(heads, q)
        gain_ref[:, lanes] = silu * dot(columns_ref[:, : 3 * heads], chosen)
        cum_col = dot(columns_ref[:, 6 * heads :], chosen)
        stream = stream_ref[:, lanes]
        mixed = [[], []]
        for j in range(2):
            h = 2 * q + j
            cum_row = rows_ref[pl.ds(h, 1), :]
            side = slice(j * P_SIZE, (j + 1) * P_SIZE)
            for b in range(2):
                span = slice(b * BLK, (b + 1) * BLK)
                column = cum_col[span, side]
                distance = jnp.abs(jnp.concatenate([column, column], axis=1) - cum_row[:, span])
                weights = (scored[b] * jnp.exp2(-distance)).astype(bf16)
                part = stream[span, side]
                mixed[b].append(dot(weights, part) + skip_ref[0, h] * part.astype(f32))
        own = dot(columns_ref[late_rows, 3 * heads : 6 * heads], chosen)
        first = [
            dot(keys_ref[2 * q + j], stream[:BLK, j * P_SIZE : (j + 1) * P_SIZE]) for j in range(2)
        ]
        carried = own * dot(read_twice, side_by_side(first))
        base_ref[:BLK, lanes] = jnp.concatenate(mixed[0], axis=1) * silu[:BLK]
        base_ref[BLK:, lanes] = (jnp.concatenate(mixed[1], axis=1) + carried) * silu[BLK:]
        for copy in results(q):
            copy.start()
        return carry

    def finish(q, carry):
        for copy in results(q):
            copy.wait()
        return carry

    lax.fori_loop(0, heads // 2, pair, 0, unroll=2)
    lax.fori_loop(0, heads // 2, finish, 0)


def total_kernel(got_ref, total_ref):
    state = got_ref[0, :N, :]
    log = got_ref[0, N:, :]
    for i in range(1, got_ref.shape[0]):
        gone = got_ref[i, N:, :]
        state = jnp.exp(-gone[:1]) * state + got_ref[i, :N, :]
        log = log + gone
    for k in range(total_ref.shape[0]):
        total_ref[k, :N, :] = state
        total_ref[k, N:, :] = log


def spread_kernel(got_ref, totals_ref, place_ref, out_ref, held, sems):
    place = place_ref[...]
    state = jnp.zeros(held.shape[1:], f32)
    for k in range(totals_ref.shape[0] - 1):
        later = jnp.exp(-totals_ref[k, N : N + 1, :]) * state + totals_ref[k, :N, :]
        state = jnp.where(jnp.broadcast_to(place, state.shape) > k, later, state)
    copies = []
    for i in range(got_ref.shape[0]):
        held[i] = state
        copies.append(pltpu.make_async_copy(held.at[i], out_ref.at[i], sems.at[i]))
        copies[-1].start()
        state = jnp.exp(-got_ref[i, N : N + 1, :]) * state + got_ref[i, :N, :]
    for copy in copies:
        copy.wait()


def carry_kernel(state_ref, read_far, base_far, gain_far, gated_ref, energy_ref, read_ref, base_ref, gain_ref, acc, sems):
    heads = state_ref.shape[0]

    def operands(q):
        lanes = pl.ds(pl.multiple_of(q * 2 * P_SIZE, 2 * P_SIZE), 2 * P_SIZE)
        return (
            pltpu.make_async_copy(base_far.at[:, lanes], base_ref.at[:, lanes], sems.at[0, q]),
            pltpu.make_async_copy(gain_far.at[:, lanes], gain_ref.at[:, lanes], sems.at[1, q]),
        )

    first = pltpu.make_async_copy(read_far, read_ref, sems.at[0, heads // 2])
    first.start()
    for q in range(heads // 2):
        for copy in operands(q):
            copy.start()
    acc[...] = jnp.zeros_like(acc)
    first.wait()
    read = read_ref[...]
    read_twice = jnp.concatenate([read, read], axis=1)

    def pair(q, carry):
        lanes = pl.ds(pl.multiple_of(q * 2 * P_SIZE, 2 * P_SIZE), 2 * P_SIZE)
        gated_ref[:, lanes] = dot(read_twice, side_by_side([state_ref[2 * q], state_ref[2 * q + 1]]))
        return carry

    def gate(q, carry):
        lanes = pl.ds(pl.multiple_of(q * 2 * P_SIZE, 2 * P_SIZE), 2 * P_SIZE)
        for copy in operands(q):
            copy.wait()
        gated = base_ref[:, lanes] + gain_ref[:, lanes] * gated_ref[:, lanes]
        gated_ref[:, lanes] = gated
        squares = gated * gated
        acc[...] += squares[:, :P_SIZE] + squares[:, P_SIZE:]
        return carry

    lax.fori_loop(0, heads // 2, pair, 0, unroll=2)
    lax.fori_loop(0, heads // 2, gate, 0)
    energy_ref[...] = jnp.sum(acc[...].T, axis=0, keepdims=True)


def norm_kernel(gated_ref, mine_ref, other_ref, gain_ref, out_ref, held, sems):
    inverse = lax.rsqrt((mine_ref[...] + other_ref[...]) / DI + EPSILON)
    copies = []
    for k in range(held.shape[0] // P_SIZE):
        rows = slice(k * P_SIZE, (k + 1) * P_SIZE)
        column = jnp.broadcast_to(inverse[:, rows], (P_SIZE, P_SIZE)).T

        def head(h, carry):
            lanes = pl.ds(pl.multiple_of(h * P_SIZE, P_SIZE), P_SIZE)
            held[rows, lanes] = (gated_ref[rows, lanes] * column * gain_ref[:, lanes]).astype(bf16)
            return carry

        lax.fori_loop(0, held.shape[1] // P_SIZE, head, 0, unroll=8)
        copies.append(pltpu.make_async_copy(held.at[rows], out_ref.at[rows], sems.at[k]))
        copies[-1].start()
    for copy in copies:
        copy.wait()


def outside(arrays):
    return tuple(pltpu.with_memory_space_constraint(array, pltpu.HBM) for array in arrays)


def call(kernel, ins, outs, scratch=(), specs=None):
    return pl.pallas_call(
        kernel,
        out_shape=[
            pltpu.HBM(*out[:2]) if out[2:] else jax.ShapeDtypeStruct(*out) for out in outs
        ],
        in_specs=specs or [VMEM] * len(ins),
        out_specs=[HBM if out[2:] else VMEM for out in outs],
        scratch_shapes=list(scratch),
        compiler_params=PARAMS,
    )(*ins)


def swap(value, axis):
    return lax.ppermute(value, axis, [(0, 1), (1, 0)])


def body(
    depth_logits,
    features,
    cell_index,
    embed,
    w_visual,
    w_gate,
    input_map,
    output_map,
    forget,
    skip,
    frame_ids,
    norm_gain,
):
    tokens, width = embed.shape
    heads = forget.shape[1]
    blocks = tokens // BLK
    pixels, bins = depth_logits.shape[1:]
    shards = lax.axis_size("ctx")
    groups = [list(range(g, g + heads)) for g in range(0, shards, heads)]
    peers = [list(range(g, shards, heads)) for g in range(heads)]
    place = jnp.full((1, P_SIZE), lax.axis_index("ctx") // heads, jnp.int32)

    near = (depth_logits.transpose(2, 0, 1), cell_index.transpose(2, 0, 1), features[0].T)
    far = (forget.T, input_map, w_visual, embed, norm_gain.reshape(1, width))
    partial_sum, forget_t, writes, w_visual, embed, norm_gain = call(
        pool_kernel,
        outside(near + far),
        [((tokens // 2, 2 * CF), f32)] + [(array.shape, array.dtype) for array in far],
        [
            pltpu.VMEM((bins, 1, pixels), f32),
            pltpu.VMEM((bins, 1, pixels), jnp.int32),
            pltpu.VMEM((CF, pixels), bf16),
            pltpu.VMEM((bins, 1, pixels), jnp.int32),
            pltpu.VMEM((tokens // SPAN, bins, 1, pixels), f32),
            pltpu.VMEM((tokens, 2 * pixels), bf16),
            pltpu.SemaphoreType.DMA((len(near + far),)),
        ],
        specs=[HBM] * len(near + far),
    )
    partial_sum, place = lax.optimization_barrier((partial_sum, place))
    chip_sum = partial_sum + swap(partial_sum, "mp")
    other_sum = swap(chip_sum, "section")

    keys, ends, columns, row_sums, early_keys = call(
        decay_kernel,
        (forget_t, writes),
        [
            ((blocks, heads, N, BLK), bf16),
            ((blocks, heads, 128), f32),
            ((tokens, 9 * heads), bf16, True),
            ((heads, tokens), f32, True),
            ((heads, N, BLK), bf16, True),
        ],
        [
            pltpu.VMEM((tokens, 9 * heads), bf16),
            pltpu.VMEM((heads, tokens), f32),
            pltpu.VMEM((tokens, 128), f32),
            pltpu.VMEM((128, tokens), f32),
            pltpu.SemaphoreType.DMA((3,)),
        ],
    )

    pay, stream, pooled = call(
        stream_kernel,
        (chip_sum, other_sum, w_visual, embed, keys, ends),
        [
            ((heads, N + EXTRA, P_SIZE), f32),
            ((tokens, width), bf16, True),
            ((tokens, 3 * CF), bf16, True),
        ],
        [
            pltpu.VMEM((tokens, width), bf16),
            pltpu.VMEM((tokens, 3 * CF), bf16),
            pltpu.SemaphoreType.DMA((heads // 2 + 1,)),
        ],
    )
    got = lax.all_to_all(pay, "ctx", 0, 0, axis_index_groups=groups, tiled=True)

    held = (input_map, output_map, frame_ids.reshape(1, tokens), row_sums, columns)
    held += (w_gate, pooled, early_keys, stream)
    base, gain = call(
        within_kernel,
        (skip.reshape(1, heads),) + outside(held),
        [((tokens, width), f32, True), ((tokens, width), f32, True)],
        [pltpu.VMEM(array.shape, array.dtype) for array in held]
        + [
            pltpu.VMEM((tokens, width), f32),
            pltpu.VMEM((tokens, width), f32),
            pltpu.VMEM((blocks, BLK, BLK), f32),
            pltpu.SemaphoreType.DMA((len(held),)),
            pltpu.SemaphoreType.DMA((2, heads // 2)),
        ],
        specs=[SMEM] + [HBM] * len(held),
    )

    (total,) = call(total_kernel, (got,), [((shards // heads, N + EXTRA, P_SIZE), f32)])
    totals = lax.all_to_all(total, "ctx", 0, 0, axis_index_groups=peers, tiled=True)
    (sent,) = call(
        spread_kernel,
        (got, totals, place),
        [((heads, N, P_SIZE), f32, True)],
        [pltpu.VMEM((heads, N, P_SIZE), f32), pltpu.SemaphoreType.DMA((heads,))],
    )
    incoming = lax.all_to_all(sent, "ctx", 0, 0, axis_index_groups=groups, tiled=True)

    gated, energy = call(
        carry_kernel,
        (incoming,) + outside((output_map, base, gain)),
        [((tokens, width), f32), ((1, tokens), f32)],
        [
            pltpu.VMEM((tokens, N), bf16),
            pltpu.VMEM((tokens, width), f32),
            pltpu.VMEM((tokens, width), f32),
            pltpu.VMEM((tokens, P_SIZE), f32),
            pltpu.SemaphoreType.DMA((2, heads // 2 + 1)),
        ],
        specs=[VMEM, HBM, HBM, HBM],
    )
    chip_energy = energy + swap(energy, "mp")
    other_energy = swap(chip_energy, "section")
    (out,) = call(
        norm_kernel,
        (gated, chip_energy, other_energy, norm_gain),
        [((tokens, width), bf16, True)],
        [pltpu.VMEM((tokens, width), bf16), pltpu.SemaphoreType.DMA((tokens // P_SIZE,))],
    )
    return out


def solution(mesh):
    return jax.shard_map(
        body,
        mesh=mesh,
        in_specs=(
            P("section", ("ctx", "mp"), None),
            P("section", ("ctx", "mp"), None),
            P("section", ("ctx", "mp"), None),
            P("ctx", ("section", "mp")),
            P(None, ("section", "mp")),
            P(None, ("section", "mp")),
            P("ctx", None),
            P("ctx", None),
            P("ctx", ("section", "mp")),
            P(("section", "mp")),
            P("ctx"),
            P(("section", "mp")),
        ),
        out_specs=P("ctx", ("section", "mp")),
        check_vma=False,
    )
```

```python
import math

import jax
import jax.numpy as jnp
from jax import lax
from jax.experimental import pallas as pl
from jax.experimental.pallas import tpu as pltpu
from jax.sharding import PartitionSpec as P

P_SIZE = 128
N = 128
BLK = 256
CF = 64
DI = 8192
EPSILON = 1e-05
LOG2E = math.log2(math.e)
SPAN = 128
CHUNK = 32
EXTRA = 8

f32 = jnp.float32
bf16 = jnp.bfloat16

VMEM = pl.BlockSpec(memory_space=pltpu.VMEM)
SMEM = pl.BlockSpec(memory_space=pltpu.SMEM)
HBM = pl.BlockSpec(memory_space=pltpu.HBM)
PARAMS = pltpu.CompilerParams(vmem_limit_bytes=24 * 1024 * 1024)


def terms(x, count):
    parts = []
    for _ in range(count - 1):
        part = x.astype(bf16)
        parts.append(part)
        x = x - part.astype(f32)
    parts.append(x.astype(bf16))
    return parts


def dot(a, b):
    return jnp.dot(a, b, preferred_element_type=f32)


def fetch(far, near, sems):
    copies = [pltpu.make_async_copy(f, n, sems.at[i]) for i, (f, n) in enumerate(zip(far, near))]
    for copy in copies:
        copy.start()
    return copies


def pool_kernel(*refs):
    count = (len(refs) - 5) // 2
    far, out_ref, near = refs[:count], refs[count], refs[count + 1 : 2 * count - 2]
    logits_ref, cells_ref, feats_ref, place, prob, hits, sems = refs[2 * count - 2 :]
    near = (logits_ref, cells_ref, feats_ref) + tuple(near)
    copies = [pltpu.make_async_copy(far[i], near[i], sems.at[i]) for i in range(count)]
    for copy in copies:
        copy.start()
    for copy in copies[:3]:
        copy.wait()
    bins, _, rows = logits_ref.shape
    spans = hits.shape[0] // SPAN
    logits = logits_ref[...]
    raised = jnp.exp(logits - jnp.max(logits, axis=0, keepdims=True))
    probability = raised / jnp.sum(raised, axis=0, keepdims=True)
    cells = cells_ref[...]
    place[...] = cells & (SPAN - 1)
    for k in range(spans):
        prob[k] = jnp.where(cells // SPAN == k, probability, 0.0)

    def chunk(i, carry):
        first = pl.multiple_of(i * CHUNK, CHUNK)
        ids = lax.broadcasted_iota(jnp.int32, (CHUNK, rows), 0) + first
        sums = [jnp.zeros((CHUNK, rows), f32) for _ in range(spans)]
        for d in range(bins):
            hit = place[d] == ids
            sums = [sums[k] + jnp.where(hit, prob[k, d], 0.0) for k in range(spans)]
        for k in range(spans):
            high, low = terms(sums[k], 2)
            hits[pl.ds(k * SPAN + first, CHUNK), :rows] = high
            hits[pl.ds(k * SPAN + first, CHUNK), rows:] = low
        return carry

    lax.fori_loop(0, SPAN // CHUNK, chunk, 0)
    feats = feats_ref[...]
    pooled = lax.dot_general(
        hits[...],
        jnp.concatenate([feats, feats], axis=1),
        (((1,), (1,)), ((), ())),
        preferred_element_type=f32,
    )
    half = pooled.shape[0] // 2
    out_ref[...] = jnp.concatenate([pooled[:half], pooled[half:]], axis=1)
    for copy in copies[3:]:
        copy.wait()


def decay_kernel(
    forget_ref, in_ref, keys_ref, ends_ref, columns_out, rows_out, early_out, columns_ref, rows_ref, wide, turned, sems
):
    heads = forget_ref.shape[0]
    blocks = keys_ref.shape[0]
    row_order = lax.broadcasted_iota(jnp.int32, (BLK, BLK), 0)
    col_order = lax.broadcasted_iota(jnp.int32, (BLK, BLK), 1)
    upper = jnp.where(row_order <= col_order, 1.0, 0.0).astype(bf16)
    for b in range(blocks):
        span = slice(b * BLK, (b + 1) * BLK)
        cum = sum(dot(part, upper) for part in terms(forget_ref[:, span], 3))
        turned[:heads, span] = cum
        end = cum[:, BLK - 1 :]
        rise = jnp.exp(cum - end)
        ends_ref[b] = jnp.broadcast_to(end, (heads, 128))
        write_t = in_ref[span, :].astype(f32).T
        for h in range(heads):
            keys_ref[b, h] = (write_t * rise[h : h + 1, :]).astype(bf16)
        if b == 0:
            early = pltpu.make_async_copy(keys_ref.at[0], early_out, sems.at[2])
            early.start()
    rows_ref[...] = turned[:heads, :] * LOG2E
    wide[...] = turned[...].T
    before = jnp.zeros((1, heads), f32)
    for b in range(blocks):
        span = slice(b * BLK, (b + 1) * BLK)
        cum = wide[span, :heads]
        parts = terms(jnp.exp(-(cum + before)), 3) + terms(jnp.exp(-cum), 3) + terms(cum * LOG2E, 3)
        columns_ref[span, :] = jnp.concatenate(parts, axis=1)
        before = before + cum[BLK - 1 :, :]
    for copy in fetch((columns_ref, rows_ref), (columns_out, rows_out), sems):
        copy.wait()
    early.wait()


def stream_kernel(
    mine_ref, other_ref, w_ref, embed_ref, keys_ref, ends_ref, pay_ref, stream_out, pooled_out, stream_ref, pooled_ref, sems
):
    packed = mine_ref[...] + other_ref[...]
    pooled = jnp.concatenate([packed[:, :CF], packed[:, CF:]], axis=0)
    pooled_ref[...] = jnp.concatenate(terms(pooled, 3), axis=1)
    heads = pay_ref.shape[0]
    saved = pltpu.make_async_copy(pooled_ref, pooled_out, sems.at[heads // 2])
    saved.start()

    def result(q):
        lanes = pl.ds(pl.multiple_of(q * 256, 256), 256)
        return pltpu.make_async_copy(stream_ref.at[:, lanes], stream_out.at[:, lanes], sems.at[q])

    def pair(q, carry):
        lanes = pl.ds(pl.multiple_of(q * 256, 256), 256)
        w = w_ref[:, lanes]
        visual = dot(pooled_ref[...], jnp.concatenate([w, w, w], axis=0))
        stream_ref[:, lanes] = (embed_ref[:, lanes].astype(f32) + visual).astype(bf16)
        result(q).start()
        return carry

    def states(q, carry):
        stream = stream_ref[:, pl.ds(pl.multiple_of(q * 256, 256), 256)]
        for j in range(2):
            h = 2 * q + j
            part = stream[:, j * P_SIZE : (j + 1) * P_SIZE]
            early = dot(keys_ref[0, h], part[:BLK])
            late = dot(keys_ref[1, h], part[BLK:])
            end_early = ends_ref[0, pl.ds(h, 1), :]
            end_late = ends_ref[1, pl.ds(h, 1), :]
            pay_ref[h, :N, :] = jnp.exp(-end_late) * early + late
            pay_ref[h, N:, :] = jnp.broadcast_to(end_early + end_late, (EXTRA, P_SIZE))
        return carry

    def finish(q, carry):
        result(q).wait()
        return carry

    lax.fori_loop(0, heads // 2, pair, 0, unroll=2)
    lax.fori_loop(0, heads // 2, states, 0, unroll=2)
    lax.fori_loop(0, heads // 2, finish, 0)
    saved.wait()


def pick(heads, q):
    row = lax.broadcasted_iota(jnp.int32, (3 * heads, 2 * P_SIZE), 0)
    lane = lax.broadcasted_iota(jnp.int32, (3 * heads, 2 * P_SIZE), 1)
    h = 2 * q + jnp.where(lane < P_SIZE, 0, 1)
    hit = (row == h) | (row == h + heads) | (row == h + 2 * heads)
    return jnp.where(hit, 1.0, 0.0).astype(bf16)


def side_by_side(states):
    return jnp.concatenate([jnp.concatenate(terms(state, 2), axis=0) for state in states], axis=1)


def within_kernel(skip_ref, *refs):
    far, (base_out, gain_out, gain_near), near = refs[:9], refs[9:12], refs[12:21]
    base_ref, gain_ref, scored, in_sems, out_sems = refs[21:]
    copies = fetch(far, near, in_sems)
    in_ref, read_ref, frames_ref, rows_ref, columns_ref, w_ref, pooled_ref, keys_ref, stream_ref = near
    heads = keys_ref.shape[0]
    row_order = lax.broadcasted_iota(jnp.int32, (BLK, BLK), 0)
    col_order = lax.broadcasted_iota(jnp.int32, (BLK, BLK), 1)
    causal = col_order <= row_order
    for copy in copies[:3]:
        copy.wait()
    for b in range(scored.shape[0]):
        span = slice(b * BLK, (b + 1) * BLK)
        scores = lax.dot_general(
            read_ref[span, :], in_ref[span, :], (((1,), (1,)), ((), ())), preferred_element_type=f32
        )
        frame_row = frames_ref[:, span].astype(f32)
        frame_col = jnp.broadcast_to(frame_row, (128, BLK)).T
        same = jnp.concatenate([frame_col, frame_col], axis=1) == frame_row
        scored[b] = jnp.where(causal | same, scores, 0.0)
    for copy in copies[3:]:
        copy.wait()
    read = read_ref[BLK:, :]
    read_twice = jnp.concatenate([read, read], axis=1)
    late_rows = slice(BLK, 2 * BLK)

    kept = gain_near.shape[1] // (2 * P_SIZE)

    def base_result(q):
        lanes = pl.ds(pl.multiple_of(q * 2 * P_SIZE, 2 * P_SIZE), 2 * P_SIZE)
        return pltpu.make_async_copy(base_ref.at[:, lanes], base_out.at[:, lanes], out_sems.at[0, q])

    def gain_result(q):
        lanes = pl.ds(pl.multiple_of((q - kept) * 2 * P_SIZE, 2 * P_SIZE), 2 * P_SIZE)
        return pltpu.make_async_copy(gain_ref.at[:, lanes], gain_out.at[:, lanes], out_sems.at[1, q])

    def pair(q, gains, gain_lanes):
        lanes = pl.ds(pl.multiple_of(q * 2 * P_SIZE, 2 * P_SIZE), 2 * P_SIZE)
        w = w_ref[:, lanes]
        gate = dot(pooled_ref[...], jnp.concatenate([w, w, w], axis=0))
        half = 0.5 * gate
        silu = half + half * jnp.tanh(half)
        chosen = pick(heads, q)
        gains[:, gain_lanes] = silu * dot(columns_ref[:, : 3 * heads], chosen)
        cum_col = dot(columns_ref[:, 6 * heads :], chosen)
        stream = stream_ref[:, lanes]
        mixed = [[], []]
        for j in range(2):
            h = 2 * q + j
            cum_row = rows_ref[pl.ds(h, 1), :]
            side = slice(j * P_SIZE, (j + 1) * P_SIZE)
            for b in range(2):
                span = slice(b * BLK, (b + 1) * BLK)
                column = cum_col[span, side]
                distance = jnp.abs(jnp.concatenate([column, column], axis=1) - cum_row[:, span])
                weights = (scored[b] * jnp.exp2(-distance)).astype(bf16)
                part = stream[span, side]
                mixed[b].append(dot(weights, part) + skip_ref[0, h] * part.astype(f32))
        own = dot(columns_ref[late_rows, 3 * heads : 6 * heads], chosen)
        first = [
            dot(keys_ref[2 * q + j], stream[:BLK, j * P_SIZE : (j + 1) * P_SIZE]) for j in range(2)
        ]
        carried = own * dot(read_twice, side_by_side(first))
        base_ref[:BLK, lanes] = jnp.concatenate(mixed[0], axis=1) * silu[:BLK]
        base_ref[BLK:, lanes] = (jnp.concatenate(mixed[1], axis=1) + carried) * silu[BLK:]
        base_result(q).start()

    def near_pair(q, carry):
        pair(q, gain_near, pl.ds(pl.multiple_of(q * 2 * P_SIZE, 2 * P_SIZE), 2 * P_SIZE))
        return carry

    def far_pair(q, carry):
        pair(q, gain_ref, pl.ds(pl.multiple_of((q - kept) * 2 * P_SIZE, 2 * P_SIZE), 2 * P_SIZE))
        gain_result(q).start()
        return carry

    def base_finish(q, carry):
        base_result(q).wait()
        return carry

    def gain_finish(q, carry):
        gain_result(q).wait()
        return carry

    lax.fori_loop(0, kept, near_pair, 0)
    lax.fori_loop(kept, heads // 2, far_pair, 0)
    lax.fori_loop(0, heads // 2, base_finish, 0)
    lax.fori_loop(kept, heads // 2, gain_finish, 0)


def total_kernel(got_ref, total_ref):
    state = got_ref[0, :N, :]
    log = got_ref[0, N:, :]
    for i in range(1, got_ref.shape[0]):
        gone = got_ref[i, N:, :]
        state = jnp.exp(-gone[:1]) * state + got_ref[i, :N, :]
        log = log + gone
    for k in range(total_ref.shape[0]):
        total_ref[k, :N, :] = state
        total_ref[k, N:, :] = log


def spread_kernel(got_ref, totals_ref, place_ref, out_ref, held, sems):
    place = place_ref[...]
    state = jnp.zeros(held.shape[1:], f32)
    for k in range(totals_ref.shape[0] - 1):
        later = jnp.exp(-totals_ref[k, N : N + 1, :]) * state + totals_ref[k, :N, :]
        state = jnp.where(jnp.broadcast_to(place, state.shape) > k, later, state)
    copies = []
    for i in range(got_ref.shape[0]):
        held[i] = state
        copies.append(pltpu.make_async_copy(held.at[i], out_ref.at[i], sems.at[i]))
        copies[-1].start()
        state = jnp.exp(-got_ref[i, N : N + 1, :]) * state + got_ref[i, :N, :]
    for copy in copies:
        copy.wait()


def carry_kernel(
    state_ref, gain_near, read_far, base_far, gain_far, gated_ref, energy_ref, read_ref, base_ref, gain_ref, acc, sems
):
    heads = state_ref.shape[0]
    kept = gain_near.shape[1] // (2 * P_SIZE)

    def span(q):
        return pl.ds(pl.multiple_of(q * 2 * P_SIZE, 2 * P_SIZE), 2 * P_SIZE)

    def base(q):
        return pltpu.make_async_copy(base_far.at[:, span(q)], base_ref.at[:, span(q)], sems.at[0, q])

    def gain(q):
        lanes = span(q - kept)
        return pltpu.make_async_copy(gain_far.at[:, lanes], gain_ref.at[:, lanes], sems.at[1, q])

    first = pltpu.make_async_copy(read_far, read_ref, sems.at[0, heads // 2])
    first.start()
    for q in range(heads // 2):
        base(q).start()
        if q >= kept:
            gain(q).start()
    acc[...] = jnp.zeros_like(acc)
    first.wait()
    read = read_ref[...]
    read_twice = jnp.concatenate([read, read], axis=1)

    def pair(q, carry):
        states = side_by_side([state_ref[2 * q], state_ref[2 * q + 1]])
        gated_ref[:, span(q)] = dot(read_twice, states)
        return carry

    def gate(q, gains):
        base(q).wait()
        gated = base_ref[:, span(q)] + gains * gated_ref[:, span(q)]
        gated_ref[:, span(q)] = gated
        squares = gated * gated
        acc[...] += squares[:, :P_SIZE] + squares[:, P_SIZE:]

    def near_gate(q, carry):
        gate(q, gain_near[:, span(q)])
        return carry

    def far_gate(q, carry):
        gain(q).wait()
        gate(q, gain_ref[:, span(q - kept)])
        return carry

    lax.fori_loop(0, heads // 2, pair, 0, unroll=2)
    lax.fori_loop(0, kept, near_gate, 0)
    lax.fori_loop(kept, heads // 2, far_gate, 0)
    energy_ref[...] = jnp.sum(acc[...].T, axis=0, keepdims=True)


def norm_kernel(gated_ref, mine_ref, core_ref, side_ref, cross_ref, gain_ref, out_ref, held, sems):
    energy = (mine_ref[...] + core_ref[...]) + (side_ref[...] + cross_ref[...])
    inverse = lax.rsqrt(energy / DI + EPSILON)
    copies = []
    for k in range(held.shape[0] // P_SIZE):
        rows = slice(k * P_SIZE, (k + 1) * P_SIZE)
        column = jnp.broadcast_to(inverse[:, rows], (P_SIZE, P_SIZE)).T

        def head(h, carry):
            lanes = pl.ds(pl.multiple_of(h * P_SIZE, P_SIZE), P_SIZE)
            held[rows, lanes] = (gated_ref[rows, lanes] * column * gain_ref[:, lanes]).astype(bf16)
            return carry

        lax.fori_loop(0, held.shape[1] // P_SIZE, head, 0, unroll=8)
        copies.append(pltpu.make_async_copy(held.at[rows], out_ref.at[rows], sems.at[k]))
        copies[-1].start()
    for copy in copies:
        copy.wait()


def outside(arrays):
    return tuple(pltpu.with_memory_space_constraint(array, pltpu.HBM) for array in arrays)


def call(kernel, ins, outs, scratch=(), specs=None):
    return pl.pallas_call(
        kernel,
        out_shape=[
            pltpu.HBM(*out[:2]) if out[2:] else jax.ShapeDtypeStruct(*out) for out in outs
        ],
        in_specs=specs or [VMEM] * len(ins),
        out_specs=[HBM if out[2:] else VMEM for out in outs],
        scratch_shapes=list(scratch),
        compiler_params=PARAMS,
    )(*ins)


def swap(value, axis):
    return lax.ppermute(value, axis, [(0, 1), (1, 0)])


def body(
    depth_logits,
    features,
    cell_index,
    embed,
    w_visual,
    w_gate,
    input_map,
    output_map,
    forget,
    skip,
    frame_ids,
    norm_gain,
):
    tokens, width = embed.shape
    heads = forget.shape[1]
    blocks = tokens // BLK
    pixels, bins = depth_logits.shape[1:]
    shards = lax.axis_size("ctx")
    groups = [list(range(g, g + heads)) for g in range(0, shards, heads)]
    peers = [list(range(g, shards, heads)) for g in range(heads)]
    place = jnp.full((1, P_SIZE), lax.axis_index("ctx") // heads, jnp.int32)

    near = (depth_logits.transpose(2, 0, 1), cell_index.transpose(2, 0, 1), features[0].T)
    far = (forget.T, input_map, w_visual, embed, norm_gain.reshape(1, width))
    partial_sum, forget_t, writes, w_visual, embed, norm_gain = call(
        pool_kernel,
        outside(near + far),
        [((tokens // 2, 2 * CF), f32)] + [(array.shape, array.dtype) for array in far],
        [
            pltpu.VMEM((bins, 1, pixels), f32),
            pltpu.VMEM((bins, 1, pixels), jnp.int32),
            pltpu.VMEM((CF, pixels), bf16),
            pltpu.VMEM((bins, 1, pixels), jnp.int32),
            pltpu.VMEM((tokens // SPAN, bins, 1, pixels), f32),
            pltpu.VMEM((tokens, 2 * pixels), bf16),
            pltpu.SemaphoreType.DMA((len(near + far),)),
        ],
        specs=[HBM] * len(near + far),
    )
    partial_sum, place = lax.optimization_barrier((partial_sum, place))
    chip_sum = partial_sum + swap(partial_sum, "mp")
    other_sum = swap(chip_sum, "section")

    keys, ends, columns, row_sums, early_keys = call(
        decay_kernel,
        (forget_t, writes),
        [
            ((blocks, heads, N, BLK), bf16),
            ((blocks, heads, 128), f32),
            ((tokens, 9 * heads), bf16, True),
            ((heads, tokens), f32, True),
            ((heads, N, BLK), bf16, True),
        ],
        [
            pltpu.VMEM((tokens, 9 * heads), bf16),
            pltpu.VMEM((heads, tokens), f32),
            pltpu.VMEM((tokens, 128), f32),
            pltpu.VMEM((128, tokens), f32),
            pltpu.SemaphoreType.DMA((3,)),
        ],
    )

    pay, stream, pooled = call(
        stream_kernel,
        (chip_sum, other_sum, w_visual, embed, keys, ends),
        [
            ((heads, N + EXTRA, P_SIZE), f32),
            ((tokens, width), bf16, True),
            ((tokens, 3 * CF), bf16, True),
        ],
        [
            pltpu.VMEM((tokens, width), bf16),
            pltpu.VMEM((tokens, 3 * CF), bf16),
            pltpu.SemaphoreType.DMA((heads // 2 + 1,)),
        ],
    )
    got = lax.all_to_all(pay, "ctx", 0, 0, axis_index_groups=groups, tiled=True)

    held = (input_map, output_map, frame_ids.reshape(1, tokens), row_sums, columns)
    held += (w_gate, pooled, early_keys, stream)
    base, gain, gain_near = call(
        within_kernel,
        (skip.reshape(1, heads),) + outside(held),
        [
            ((tokens, width), f32, True),
            ((tokens, width // 2), f32, True),
            ((tokens, width // 2), f32),
        ],
        [pltpu.VMEM(array.shape, array.dtype) for array in held]
        + [
            pltpu.VMEM((tokens, width), f32),
            pltpu.VMEM((tokens, width // 2), f32),
            pltpu.VMEM((blocks, BLK, BLK), f32),
            pltpu.SemaphoreType.DMA((len(held),)),
            pltpu.SemaphoreType.DMA((2, heads // 2)),
        ],
        specs=[SMEM] + [HBM] * len(held),
    )

    (total,) = call(total_kernel, (got,), [((shards // heads, N + EXTRA, P_SIZE), f32)])
    totals = lax.all_to_all(total, "ctx", 0, 0, axis_index_groups=peers, tiled=True)
    (sent,) = call(
        spread_kernel,
        (got, totals, place),
        [((heads, N, P_SIZE), f32, True)],
        [pltpu.VMEM((heads, N, P_SIZE), f32), pltpu.SemaphoreType.DMA((heads,))],
    )
    incoming = lax.all_to_all(sent, "ctx", 0, 0, axis_index_groups=groups, tiled=True)

    gated, energy = call(
        carry_kernel,
        (incoming, gain_near) + outside((output_map, base, gain)),
        [((tokens, width), f32), ((1, tokens), f32)],
        [
            pltpu.VMEM((tokens, N), bf16),
            pltpu.VMEM((tokens, width), f32),
            pltpu.VMEM((tokens, width // 2), f32),
            pltpu.VMEM((tokens, P_SIZE), f32),
            pltpu.SemaphoreType.DMA((2, heads // 2 + 1)),
        ],
        specs=[VMEM] * 2 + [HBM] * 3,
    )
    others = [
        lax.ppermute(energy, ("section", "mp"), [(i, i ^ k) for i in range(4)]) for k in (1, 2, 3)
    ]
    (out,) = call(
        norm_kernel,
        (gated, energy, *others, norm_gain),
        [((tokens, width), bf16, True)],
        [pltpu.VMEM((tokens, width), bf16), pltpu.SemaphoreType.DMA((tokens // P_SIZE,))],
    )
    return out


def solution(mesh):
    return jax.shard_map(
        body,
        mesh=mesh,
        in_specs=(
            P("section", ("ctx", "mp"), None),
            P("section", ("ctx", "mp"), None),
            P("section", ("ctx", "mp"), None),
            P("ctx", ("section", "mp")),
            P(None, ("section", "mp")),
            P(None, ("section", "mp")),
            P("ctx", None),
            P("ctx", None),
            P("ctx", ("section", "mp")),
            P(("section", "mp")),
            P("ctx"),
            P(("section", "mp")),
        ),
        out_specs=P("ctx", ("section", "mp")),
        check_vma=False,
    )
```

```python
import math

import jax
import jax.numpy as jnp
from jax import lax
from jax.experimental import pallas as pl
from jax.experimental.pallas import tpu as pltpu
from jax.sharding import PartitionSpec as P

P_SIZE = 128
N = 128
BLK = 256
CF = 64
DI = 8192
EPSILON = 1e-05
LOG2E = math.log2(math.e)
SPAN = 128
CHUNK = 32
EXTRA = 8

f32 = jnp.float32
bf16 = jnp.bfloat16

VMEM = pl.BlockSpec(memory_space=pltpu.VMEM)
SMEM = pl.BlockSpec(memory_space=pltpu.SMEM)
HBM = pl.BlockSpec(memory_space=pltpu.HBM)
PARAMS = pltpu.CompilerParams(vmem_limit_bytes=24 * 1024 * 1024)


def terms(x, count):
    parts = []
    for _ in range(count - 1):
        part = x.astype(bf16)
        parts.append(part)
        x = x - part.astype(f32)
    parts.append(x.astype(bf16))
    return parts


def dot(a, b):
    return jnp.dot(a, b, preferred_element_type=f32)


def fetch(far, near, sems):
    copies = [pltpu.make_async_copy(f, n, sems.at[i]) for i, (f, n) in enumerate(zip(far, near))]
    for copy in copies:
        copy.start()
    return copies


def pool_kernel(*refs):
    count = (len(refs) - 5) // 2
    far, out_ref, near = refs[:count], refs[count], refs[count + 1 : 2 * count - 2]
    logits_ref, cells_ref, feats_ref, place, prob, hits, sems = refs[2 * count - 2 :]
    near = (logits_ref, cells_ref, feats_ref) + tuple(near)
    copies = [pltpu.make_async_copy(far[i], near[i], sems.at[i]) for i in range(count)]
    for copy in copies:
        copy.start()
    for copy in copies[:3]:
        copy.wait()
    bins, _, rows = logits_ref.shape
    spans = hits.shape[0] // SPAN
    logits = logits_ref[...]
    raised = jnp.exp(logits - jnp.max(logits, axis=0, keepdims=True))
    probability = raised / jnp.sum(raised, axis=0, keepdims=True)
    cells = cells_ref[...]
    place[...] = cells & (SPAN - 1)
    for k in range(spans):
        prob[k] = jnp.where(cells // SPAN == k, probability, 0.0)

    def chunk(i, carry):
        first = pl.multiple_of(i * CHUNK, CHUNK)
        ids = lax.broadcasted_iota(jnp.int32, (CHUNK, rows), 0) + first
        sums = [jnp.zeros((CHUNK, rows), f32) for _ in range(spans)]
        for d in range(bins):
            hit = place[d] == ids
            sums = [sums[k] + jnp.where(hit, prob[k, d], 0.0) for k in range(spans)]
        for k in range(spans):
            high, low = terms(sums[k], 2)
            hits[pl.ds(k * SPAN + first, CHUNK), :rows] = high
            hits[pl.ds(k * SPAN + first, CHUNK), rows:] = low
        return carry

    lax.fori_loop(0, SPAN // CHUNK, chunk, 0)
    feats = feats_ref[...]
    pooled = lax.dot_general(
        hits[...],
        jnp.concatenate([feats, feats], axis=1),
        (((1,), (1,)), ((), ())),
        preferred_element_type=f32,
    )
    half = pooled.shape[0] // 2
    out_ref[...] = jnp.concatenate([pooled[:half], pooled[half:]], axis=1)
    for copy in copies[3:]:
        copy.wait()


def decay_kernel(
    forget_ref, in_ref, keys_ref, ends_ref, columns_out, rows_out, early_out, columns_ref, rows_ref, wide, turned, sems
):
    heads = forget_ref.shape[0]
    blocks = keys_ref.shape[0]
    row_order = lax.broadcasted_iota(jnp.int32, (BLK, BLK), 0)
    col_order = lax.broadcasted_iota(jnp.int32, (BLK, BLK), 1)
    upper = jnp.where(row_order <= col_order, 1.0, 0.0).astype(bf16)
    for b in range(blocks):
        span = slice(b * BLK, (b + 1) * BLK)
        cum = sum(dot(part, upper) for part in terms(forget_ref[:, span], 3))
        turned[:heads, span] = cum
        end = cum[:, BLK - 1 :]
        rise = jnp.exp(cum - end)
        ends_ref[b] = jnp.broadcast_to(end, (heads, 128))
        write_t = in_ref[span, :].astype(f32).T
        for h in range(heads):
            keys_ref[b, h] = (write_t * rise[h : h + 1, :]).astype(bf16)
        if b == 0:
            early = pltpu.make_async_copy(keys_ref.at[0], early_out, sems.at[2])
            early.start()
    rows_ref[...] = turned[:heads, :] * LOG2E
    wide[...] = turned[...].T
    before = jnp.zeros((1, heads), f32)
    for b in range(blocks):
        span = slice(b * BLK, (b + 1) * BLK)
        cum = wide[span, :heads]
        parts = terms(jnp.exp(-(cum + before)), 3) + terms(jnp.exp(-cum), 3) + terms(cum * LOG2E, 3)
        columns_ref[span, :] = jnp.concatenate(parts, axis=1)
        before = before + cum[BLK - 1 :, :]
    for copy in fetch((columns_ref, rows_ref), (columns_out, rows_out), sems):
        copy.wait()
    early.wait()


def stream_kernel(
    mine_ref, other_ref, w_ref, embed_ref, keys_ref, ends_ref, pay_ref, stream_out, pooled_out, stream_ref, pooled_ref, sems
):
    packed = mine_ref[...] + other_ref[...]
    pooled = jnp.concatenate([packed[:, :CF], packed[:, CF:]], axis=0)
    pooled_ref[...] = jnp.concatenate(terms(pooled, 3), axis=1)
    heads = pay_ref.shape[0]
    saved = pltpu.make_async_copy(pooled_ref, pooled_out, sems.at[heads // 2])
    saved.start()

    def result(q):
        lanes = pl.ds(pl.multiple_of(q * 256, 256), 256)
        return pltpu.make_async_copy(stream_ref.at[:, lanes], stream_out.at[:, lanes], sems.at[q])

    def pair(q, carry):
        lanes = pl.ds(pl.multiple_of(q * 256, 256), 256)
        w = w_ref[:, lanes]
        visual = dot(pooled_ref[...], jnp.concatenate([w, w, w], axis=0))
        stream_ref[:, lanes] = (embed_ref[:, lanes].astype(f32) + visual).astype(bf16)
        result(q).start()
        return carry

    def states(q, carry):
        stream = stream_ref[:, pl.ds(pl.multiple_of(q * 256, 256), 256)]
        for j in range(2):
            h = 2 * q + j
            part = stream[:, j * P_SIZE : (j + 1) * P_SIZE]
            early = dot(keys_ref[0, h], part[:BLK])
            late = dot(keys_ref[1, h], part[BLK:])
            end_early = ends_ref[0, pl.ds(h, 1), :]
            end_late = ends_ref[1, pl.ds(h, 1), :]
            pay_ref[h, :N, :] = jnp.exp(-end_late) * early + late
            pay_ref[h, N:, :] = jnp.broadcast_to(end_early + end_late, (EXTRA, P_SIZE))
        return carry

    def finish(q, carry):
        result(q).wait()
        return carry

    lax.fori_loop(0, heads // 2, pair, 0, unroll=2)
    lax.fori_loop(0, heads // 2, states, 0, unroll=2)
    lax.fori_loop(0, heads // 2, finish, 0)
    saved.wait()


def pick(heads, q):
    row = lax.broadcasted_iota(jnp.int32, (3 * heads, 2 * P_SIZE), 0)
    lane = lax.broadcasted_iota(jnp.int32, (3 * heads, 2 * P_SIZE), 1)
    h = 2 * q + jnp.where(lane < P_SIZE, 0, 1)
    hit = (row == h) | (row == h + heads) | (row == h + 2 * heads)
    return jnp.where(hit, 1.0, 0.0).astype(bf16)


def side_by_side(states):
    return jnp.concatenate([jnp.concatenate(terms(state, 2), axis=0) for state in states], axis=1)


def within_kernel(skip_ref, *refs):
    far, (base_out, gain_out, gain_near), near = refs[:9], refs[9:12], refs[12:21]
    base_ref, gain_ref, scored, in_sems, out_sems = refs[21:]
    copies = fetch(far, near, in_sems)
    in_ref, read_ref, frames_ref, rows_ref, columns_ref, w_ref, pooled_ref, keys_ref, stream_ref = near
    heads = keys_ref.shape[0]
    row_order = lax.broadcasted_iota(jnp.int32, (BLK, BLK), 0)
    col_order = lax.broadcasted_iota(jnp.int32, (BLK, BLK), 1)
    causal = col_order <= row_order
    for copy in copies[:3]:
        copy.wait()
    for b in range(scored.shape[0]):
        span = slice(b * BLK, (b + 1) * BLK)
        scores = lax.dot_general(
            read_ref[span, :], in_ref[span, :], (((1,), (1,)), ((), ())), preferred_element_type=f32
        )
        frame_row = frames_ref[:, span].astype(f32)
        frame_col = jnp.broadcast_to(frame_row, (128, BLK)).T
        same = jnp.concatenate([frame_col, frame_col], axis=1) == frame_row
        scored[b] = jnp.where(causal | same, scores, 0.0)
    for copy in copies[3:]:
        copy.wait()
    read = read_ref[BLK:, :]
    read_twice = jnp.concatenate([read, read], axis=1)
    late_rows = slice(BLK, 2 * BLK)

    kept = gain_near.shape[1] // (2 * P_SIZE)

    def base_result(q):
        lanes = pl.ds(pl.multiple_of(q * 2 * P_SIZE, 2 * P_SIZE), 2 * P_SIZE)
        return pltpu.make_async_copy(base_ref.at[:, lanes], base_out.at[:, lanes], out_sems.at[0, q])

    def gain_result(q):
        lanes = pl.ds(pl.multiple_of((q - kept) * 2 * P_SIZE, 2 * P_SIZE), 2 * P_SIZE)
        return pltpu.make_async_copy(gain_ref.at[:, lanes], gain_out.at[:, lanes], out_sems.at[1, q])

    def pair(q, gains, gain_lanes):
        lanes = pl.ds(pl.multiple_of(q * 2 * P_SIZE, 2 * P_SIZE), 2 * P_SIZE)
        w = w_ref[:, lanes]
        gate = dot(pooled_ref[...], jnp.concatenate([w, w, w], axis=0))
        half = 0.5 * gate
        silu = half + half * jnp.tanh(half)
        chosen = pick(heads, q)
        gains[:, gain_lanes] = silu * dot(columns_ref[:, : 3 * heads], chosen)
        cum_col = dot(columns_ref[:, 6 * heads :], chosen)
        stream = stream_ref[:, lanes]
        mixed = [[], []]
        for j in range(2):
            h = 2 * q + j
            cum_row = rows_ref[pl.ds(h, 1), :]
            side = slice(j * P_SIZE, (j + 1) * P_SIZE)
            for b in range(2):
                span = slice(b * BLK, (b + 1) * BLK)
                column = cum_col[span, side]
                distance = jnp.abs(jnp.concatenate([column, column], axis=1) - cum_row[:, span])
                weights = (scored[b] * jnp.exp2(-distance)).astype(bf16)
                part = stream[span, side]
                mixed[b].append(dot(weights, part) + skip_ref[0, h] * part.astype(f32))
        own = dot(columns_ref[late_rows, 3 * heads : 6 * heads], chosen)
        first = [
            dot(keys_ref[2 * q + j], stream[:BLK, j * P_SIZE : (j + 1) * P_SIZE]) for j in range(2)
        ]
        carried = own * dot(read_twice, side_by_side(first))
        base_ref[:BLK, lanes] = jnp.concatenate(mixed[0], axis=1) * silu[:BLK]
        base_ref[BLK:, lanes] = (jnp.concatenate(mixed[1], axis=1) + carried) * silu[BLK:]
        base_result(q).start()

    def near_pair(q, carry):
        pair(q, gain_near, pl.ds(pl.multiple_of(q * 2 * P_SIZE, 2 * P_SIZE), 2 * P_SIZE))
        return carry

    def far_pair(q, carry):
        pair(q, gain_ref, pl.ds(pl.multiple_of((q - kept) * 2 * P_SIZE, 2 * P_SIZE), 2 * P_SIZE))
        gain_result(q).start()
        return carry

    def base_finish(q, carry):
        base_result(q).wait()
        return carry

    def gain_finish(q, carry):
        gain_result(q).wait()
        return carry

    lax.fori_loop(0, kept, near_pair, 0, unroll=2)
    lax.fori_loop(kept, heads // 2, far_pair, 0, unroll=2)
    lax.fori_loop(0, heads // 2, base_finish, 0)
    lax.fori_loop(kept, heads // 2, gain_finish, 0)


def total_kernel(got_ref, total_ref):
    state = got_ref[0, :N, :]
    log = got_ref[0, N:, :]
    for i in range(1, got_ref.shape[0]):
        gone = got_ref[i, N:, :]
        state = jnp.exp(-gone[:1]) * state + got_ref[i, :N, :]
        log = log + gone
    for k in range(total_ref.shape[0]):
        total_ref[k, :N, :] = state
        total_ref[k, N:, :] = log


def spread_kernel(got_ref, totals_ref, place_ref, out_ref, held, sems):
    place = place_ref[...]
    state = jnp.zeros(held.shape[1:], f32)
    for k in range(totals_ref.shape[0] - 1):
        later = jnp.exp(-totals_ref[k, N : N + 1, :]) * state + totals_ref[k, :N, :]
        state = jnp.where(jnp.broadcast_to(place, state.shape) > k, later, state)
    copies = []
    for i in range(got_ref.shape[0]):
        held[i] = state
        copies.append(pltpu.make_async_copy(held.at[i], out_ref.at[i], sems.at[i]))
        copies[-1].start()
        state = jnp.exp(-got_ref[i, N : N + 1, :]) * state + got_ref[i, :N, :]
    for copy in copies:
        copy.wait()


def carry_kernel(
    state_ref, gain_near, read_ref, base_far, gain_far, gated_ref, energy_ref, base_ref, gain_ref, acc, sems
):
    heads = state_ref.shape[0]
    kept = gain_near.shape[1] // (2 * P_SIZE)

    def span(q):
        return pl.ds(pl.multiple_of(q * 2 * P_SIZE, 2 * P_SIZE), 2 * P_SIZE)

    def base(q):
        return pltpu.make_async_copy(base_far.at[:, span(q)], base_ref.at[:, span(q)], sems.at[0, q])

    def gain(q):
        lanes = span(q - kept)
        return pltpu.make_async_copy(gain_far.at[:, lanes], gain_ref.at[:, lanes], sems.at[1, q])

    for q in range(heads // 2):
        base(q).start()
        if q >= kept:
            gain(q).start()
    acc[...] = jnp.zeros_like(acc)
    read = read_ref[...]
    read_twice = jnp.concatenate([read, read], axis=1)

    def pair(q, carry):
        states = side_by_side([state_ref[2 * q], state_ref[2 * q + 1]])
        gated_ref[:, span(q)] = dot(read_twice, states)
        return carry

    def gate(q, gains):
        gated = base_ref[:, span(q)] + gains * gated_ref[:, span(q)]
        gated_ref[:, span(q)] = gated
        squares = gated * gated
        acc[...] += squares[:, :P_SIZE] + squares[:, P_SIZE:]

    def near_gate(q, carry):
        gate(q, gain_near[:, span(q)])
        return carry

    def far_gate(q, carry):
        gate(q, gain_ref[:, span(q - kept)])
        return carry

    lax.fori_loop(0, heads // 2, pair, 0, unroll=2)
    for q in range(kept):
        base(q).wait()
    lax.fori_loop(0, kept, near_gate, 0, unroll=2)
    for q in range(kept, heads // 2):
        base(q).wait()
        gain(q).wait()
    lax.fori_loop(kept, heads // 2, far_gate, 0, unroll=2)
    energy_ref[...] = jnp.sum(acc[...].T, axis=0, keepdims=True)


def norm_kernel(gated_ref, mine_ref, core_ref, side_ref, cross_ref, gain_ref, out_ref, held, sems):
    energy = (mine_ref[...] + core_ref[...]) + (side_ref[...] + cross_ref[...])
    inverse = lax.rsqrt(energy / DI + EPSILON)
    copies = []
    for k in range(held.shape[0] // P_SIZE):
        rows = slice(k * P_SIZE, (k + 1) * P_SIZE)
        column = jnp.broadcast_to(inverse[:, rows], (P_SIZE, P_SIZE)).T

        def head(h, carry):
            lanes = pl.ds(pl.multiple_of(h * P_SIZE, P_SIZE), P_SIZE)
            held[rows, lanes] = (gated_ref[rows, lanes] * column * gain_ref[:, lanes]).astype(bf16)
            return carry

        lax.fori_loop(0, held.shape[1] // P_SIZE, head, 0, unroll=8)
        copies.append(pltpu.make_async_copy(held.at[rows], out_ref.at[rows], sems.at[k]))
        copies[-1].start()
    for copy in copies:
        copy.wait()


def outside(arrays):
    return tuple(pltpu.with_memory_space_constraint(array, pltpu.HBM) for array in arrays)


def call(kernel, ins, outs, scratch=(), specs=None):
    return pl.pallas_call(
        kernel,
        out_shape=[
            pltpu.HBM(*out[:2]) if out[2:] else jax.ShapeDtypeStruct(*out) for out in outs
        ],
        in_specs=specs or [VMEM] * len(ins),
        out_specs=[HBM if out[2:] else VMEM for out in outs],
        scratch_shapes=list(scratch),
        compiler_params=PARAMS,
    )(*ins)


def swap(value, axis):
    return lax.ppermute(value, axis, [(0, 1), (1, 0)])


def body(
    depth_logits,
    features,
    cell_index,
    embed,
    w_visual,
    w_gate,
    input_map,
    output_map,
    forget,
    skip,
    frame_ids,
    norm_gain,
):
    tokens, width = embed.shape
    heads = forget.shape[1]
    blocks = tokens // BLK
    pixels, bins = depth_logits.shape[1:]
    shards = lax.axis_size("ctx")
    groups = [list(range(g, g + heads)) for g in range(0, shards, heads)]
    peers = [list(range(g, shards, heads)) for g in range(heads)]
    place = jnp.full((1, P_SIZE), lax.axis_index("ctx") // heads, jnp.int32)

    near = (depth_logits.transpose(2, 0, 1), cell_index.transpose(2, 0, 1), features[0].T)
    far = (forget.T, input_map, w_visual, embed, norm_gain.reshape(1, width), output_map)
    partial_sum, forget_t, writes, w_visual, embed, norm_gain, reads = call(
        pool_kernel,
        outside(near + far),
        [((tokens // 2, 2 * CF), f32)] + [(array.shape, array.dtype) for array in far],
        [
            pltpu.VMEM((bins, 1, pixels), f32),
            pltpu.VMEM((bins, 1, pixels), jnp.int32),
            pltpu.VMEM((CF, pixels), bf16),
            pltpu.VMEM((bins, 1, pixels), jnp.int32),
            pltpu.VMEM((tokens // SPAN, bins, 1, pixels), f32),
            pltpu.VMEM((tokens, 2 * pixels), bf16),
            pltpu.SemaphoreType.DMA((len(near + far),)),
        ],
        specs=[HBM] * len(near + far),
    )
    partial_sum, place = lax.optimization_barrier((partial_sum, place))
    chip_sum = partial_sum + swap(partial_sum, "mp")
    other_sum = swap(chip_sum, "section")

    keys, ends, columns, row_sums, early_keys = call(
        decay_kernel,
        (forget_t, writes),
        [
            ((blocks, heads, N, BLK), bf16),
            ((blocks, heads, 128), f32),
            ((tokens, 9 * heads), bf16, True),
            ((heads, tokens), f32, True),
            ((heads, N, BLK), bf16, True),
        ],
        [
            pltpu.VMEM((tokens, 9 * heads), bf16),
            pltpu.VMEM((heads, tokens), f32),
            pltpu.VMEM((tokens, 128), f32),
            pltpu.VMEM((128, tokens), f32),
            pltpu.SemaphoreType.DMA((3,)),
        ],
    )

    pay, stream, pooled = call(
        stream_kernel,
        (chip_sum, other_sum, w_visual, embed, keys, ends),
        [
            ((heads, N + EXTRA, P_SIZE), f32),
            ((tokens, width), bf16, True),
            ((tokens, 3 * CF), bf16, True),
        ],
        [
            pltpu.VMEM((tokens, width), bf16),
            pltpu.VMEM((tokens, 3 * CF), bf16),
            pltpu.SemaphoreType.DMA((heads // 2 + 1,)),
        ],
    )
    got = lax.all_to_all(pay, "ctx", 0, 0, axis_index_groups=groups, tiled=True)

    held = (input_map, output_map, frame_ids.reshape(1, tokens), row_sums, columns)
    held += (w_gate, pooled, early_keys, stream)
    base, gain, gain_near = call(
        within_kernel,
        (skip.reshape(1, heads),) + outside(held),
        [
            ((tokens, width), f32, True),
            ((tokens, width // 2), f32, True),
            ((tokens, width // 2), f32),
        ],
        [pltpu.VMEM(array.shape, array.dtype) for array in held]
        + [
            pltpu.VMEM((tokens, width), f32),
            pltpu.VMEM((tokens, width // 2), f32),
            pltpu.VMEM((blocks, BLK, BLK), f32),
            pltpu.SemaphoreType.DMA((len(held),)),
            pltpu.SemaphoreType.DMA((2, heads // 2)),
        ],
        specs=[SMEM] + [HBM] * len(held),
    )

    (total,) = call(total_kernel, (got,), [((shards // heads, N + EXTRA, P_SIZE), f32)])
    totals = lax.all_to_all(total, "ctx", 0, 0, axis_index_groups=peers, tiled=True)
    (sent,) = call(
        spread_kernel,
        (got, totals, place),
        [((heads, N, P_SIZE), f32, True)],
        [pltpu.VMEM((heads, N, P_SIZE), f32), pltpu.SemaphoreType.DMA((heads,))],
    )
    incoming = lax.all_to_all(sent, "ctx", 0, 0, axis_index_groups=groups, tiled=True)

    gated, energy = call(
        carry_kernel,
        (incoming, gain_near, reads) + outside((base, gain)),
        [((tokens, width), f32), ((1, tokens), f32)],
        [
            pltpu.VMEM((tokens, width), f32),
            pltpu.VMEM((tokens, width // 2), f32),
            pltpu.VMEM((tokens, P_SIZE), f32),
            pltpu.SemaphoreType.DMA((2, heads // 2)),
        ],
        specs=[VMEM] * 3 + [HBM] * 2,
    )
    others = [
        lax.ppermute(energy, ("section", "mp"), [(i, i ^ k) for i in range(4)]) for k in (1, 2, 3)
    ]
    (out,) = call(
        norm_kernel,
        (gated, energy, *others, norm_gain),
        [((tokens, width), bf16, True)],
        [pltpu.VMEM((tokens, width), bf16), pltpu.SemaphoreType.DMA((tokens // P_SIZE,))],
    )
    return out


def solution(mesh):
    return jax.shard_map(
        body,
        mesh=mesh,
        in_specs=(
            P("section", ("ctx", "mp"), None),
            P("section", ("ctx", "mp"), None),
            P("section", ("ctx", "mp"), None),
            P("ctx", ("section", "mp")),
            P(None, ("section", "mp")),
            P(None, ("section", "mp")),
            P("ctx", None),
            P("ctx", None),
            P("ctx", ("section", "mp")),
            P(("section", "mp")),
            P("ctx"),
            P(("section", "mp")),
        ),
        out_specs=P("ctx", ("section", "mp")),
        check_vma=False,
    )
```
